32 devices in a mesh: seq: 8 (over z, x), head: 4 (over y, core).
Axes of the slice: x: 2, y: 2, z: 4, core: 2. Of those that a mesh axis runs over, the one named last changes fastest.
Arguments:
- tokens: bfloat16 [4096, 2240], P('seq', 'head'), may hold values from -6 to 6
- norm_gain: bfloat16 [2240], replicated, may hold values from 0.099609375 to 1.8984375
- w_query: bfloat16 [2240, 2048], P(None, 'head'), may hold values from -0.125 to 0.125
- w_key: bfloat16 [2240, 2048], P(None, 'head'), may hold values from -0.125 to 0.125
- w_value: bfloat16 [2240, 2048], P(None, 'head'), may hold values from -0.125 to 0.125
- w_decay: bfloat16 [2240, 16], P(None, 'head'), may hold values from -1 to 1
- w_beta: bfloat16 [2240, 16], P(None, 'head'), may hold values from -0.125 to 0.125
- head_rates: float32 [2, 16], P(None, 'head'), may hold values from -6.5 to 1.5, as said below
- head_gain: bfloat16 [128], replicated, may hold values from 0.099609375 to 1.8984375
- w_out: bfloat16 [2048, 2240], P('head'), may hold values from -0.1875 to 0.1875
- ffn_gain: bfloat16 [2240], replicated, may hold values from 0.099609375 to 1.8984375
- w_up: bfloat16 [2240, 5600], P(None, 'head'), may hold values from -0.125 to 0.125
- conv_taps: bfloat16 [3, 5600], P(None, 'head'), may hold values from -3 to 3
- w_down: bfloat16 [5600, 2240], P('head'), may hold values from -0.109375 to 0.109375
Outputs:
- layer_out: bfloat16 [4096, 2240], P('seq', 'head')
The draws below stay inside these ranges and needn't reach their ends.
Inputs may be any that keep to these rules, and one draw needn't show every extreme that they name: `head_rates`: row 0 is positive and at most 0.03; row 1 lies in -6.5 to 1.5.
All inputs are finite; a program needn't handle non-finite values.
Results may differ from the reference program's by a relative error of at most 0.02.
Values may be sent and summed in bfloat16 or wider, within the bound.
No kernel may reach another device: no remote copies, remote signals or barrier semaphores. Data moves between devices by JAX's collectives and lax.ppermute only.
A program may use at most 64 MiB of HBM per device.

```python
import math
import jax
import jax.numpy as jnp
from jax import lax

D = 2240
HEADS = 16
DK = 128
FF = 5600
BLOCK = 128
TOKENS = 4096
N_HEAD = 4


def draw_head_rates(key, part):
    unit_draw = jax.random.uniform(jax.random.fold_in(key, 11), (HEADS,), jnp.float32)
    jitter = jax.random.uniform(jax.random.fold_in(key, 12), (HEADS,), jnp.float32, -0.5, 0.5)
    lowest = math.log(0.05 / TOKENS)
    highest = math.log(0.03)
    rates = jnp.exp(lowest + unit_draw * (highest - lowest))
    biases = -6.0 + 7.0 * unit_draw + jitter
    return jnp.stack([rates, biases]).astype(jnp.float32)


def with_spikes(values, key, source, target, blocks, factor):
    def block_of(axis_at):
        return (jnp.arange(values.shape[axis_at]) // (values.shape[axis_at] // blocks)).reshape((-1,) + (1,) * (values.ndim - 1 - axis_at))

    near = jax.random.permutation(key, blocks)[block_of(target)]
    other_side = (block_of(target) + blocks // 2) % blocks
    return jnp.where((block_of(source) == near) | (block_of(source) == other_side), factor * values, values)


def levels(own_key, shape, shards, least, largest):
    level, own = 1.0, jax.random.fold_in(own_key, 6)
    for axis_at, shards_of in shards:
        steps = jnp.exp(jax.random.uniform(jax.random.fold_in(own, axis_at), (shards_of,), jnp.float32, least / len(shards), largest / len(shards)))
        level = level * jnp.repeat(steps, shape[axis_at] // shards_of).reshape([-1 if axis == axis_at else 1 for axis in range(len(shape))])
    return level


def normal_values(stream_key, dims, scale, bound, split=(), held_as=jnp.bfloat16):
    gain = levels(stream_key, dims, split, -0.22, 0.18) if split else 1.0
    entries = jax.random.normal(stream_key, dims, jnp.float32) * scale * gain
    return jnp.minimum(jnp.maximum(entries, -bound), bound).astype(held_as)


def gaussian_with(key, dims, deviation, most, split, heavy, held_as=jnp.bfloat16):
    drawn = deviation * jax.random.normal(key, dims, jnp.float32)
    if split:
        drawn = drawn * levels(key, dims, split, -0.22, 0.18)
    return jnp.clip(with_spikes(drawn, jax.random.fold_in(key, 3), *heavy), -most, most).astype(held_as)


def setup_inputs(seed: int = 0) -> dict:
    arg_keys = jax.random.split(jax.random.key(seed), 15)
    return {
        "tokens": normal_values(arg_keys[0], (TOKENS, D), 1.0, 6.0, ((0, 8), (1, 4))),
        "norm_gain": jnp.clip(1.0 + 0.18 * jax.random.normal(arg_keys[1], (D,), jnp.float32), 0.099609375, 1.8984375).astype(jnp.bfloat16),
        "w_query": normal_values(arg_keys[2], (D, HEADS * DK), D ** -0.5, 0.125, ((1, 4),)),
        "w_key": normal_values(arg_keys[3], (D, HEADS * DK), D ** -0.5, 0.125, ((1, 4),)),
        "w_value": normal_values(arg_keys[4], (D, HEADS * DK), D ** -0.5, 0.125, ((1, 4),)),
        "w_decay": normal_values(arg_keys[5], (D, HEADS), (D // 64) ** -0.5, 1.0, ((1, 4),)),
        "w_beta": normal_values(arg_keys[6], (D, HEADS), D ** -0.5, 0.125, ((1, 4),)),
        "head_rates": draw_head_rates(jax.random.fold_in(arg_keys[14], 71), 0),
        "head_gain": jnp.clip(1.0 + 0.18 * jax.random.normal(arg_keys[8], (DK,), jnp.float32), 0.099609375, 1.8984375).astype(jnp.bfloat16),
        "w_out": gaussian_with(arg_keys[9], (HEADS * DK, D), (HEADS * DK) ** -0.5, 0.1875, ((0, 4),), (0, 1, 4, 2.0)),
        "ffn_gain": jnp.clip(1.0 + 0.18 * jax.random.normal(arg_keys[10], (D,), jnp.float32), 0.099609375, 1.8984375).astype(jnp.bfloat16),
        "w_up": normal_values(arg_keys[11], (D, FF), D ** -0.5, 0.125, ((1, 4),)),
        "conv_taps": normal_values(arg_keys[12], (3, FF), 0.6, 3.0, ((1, 4),)),
        "w_down": gaussian_with(arg_keys[13], (FF, D), FF ** -0.5, 0.109375, ((0, 4),), (0, 1, 4, 2.0)),
    }


exact_mode = lax.Precision.HIGHEST
epsilon = 1e-06

def root_scale(matrix, gain_row):
    floating = matrix.astype(jnp.float32)
    inverse = lax.rsqrt(lax.optimization_barrier(jnp.mean(floating * floating, axis=-1, keepdims=True)) + epsilon)
    return floating * inverse * gain_row.astype(jnp.float32)

def unit_rows(matrix):
    return matrix * lax.rsqrt(lax.optimization_barrier(jnp.sum(matrix * matrix, axis=-1, keepdims=True)) + epsilon)

def inverse_apply(lower_part, right_side):
    length = lower_part.shape[-1]
    powered = lower_part
    result = right_side - jnp.einsum('...ij,...jk->...ik', powered, right_side, precision=exact_mode)
    for level_index in range((length - 1).bit_length() - 1):
        powered = jnp.einsum('...ij,...jk->...ik', powered, powered, precision=exact_mode)
        result = result + jnp.einsum('...ij,...jk->...ik', powered, result, precision=exact_mode)
    return result

def block_terms(query_rows, key_rows, value_rows, log_decay, strength):
    length = query_rows.shape[-2]
    rows_at = lax.broadcasted_iota(jnp.int32, (length, length), 0)
    cols_at = lax.broadcasted_iota(jnp.int32, (length, length), 1)
    strict = rows_at > cols_at
    inclusive = rows_at >= cols_at
    totals = jnp.cumsum(log_decay, axis=-1)
    spread = totals[..., :, None] - totals[..., None, :]
    decay_strict = jnp.where(strict, jnp.exp(jnp.where(strict, spread, 0.0)), 0.0)
    decay_incl = jnp.where(inclusive, jnp.exp(jnp.where(inclusive, spread, 0.0)), 0.0)
    key_inner = jnp.einsum('...id,...jd->...ij', key_rows, key_rows, precision=exact_mode)
    lower_part = strength[..., :, None] * decay_strict * key_inner
    growth = jnp.exp(totals)
    stacked = jnp.concatenate([strength[..., None] * value_rows, (strength * growth)[..., None] * key_rows], axis=-1)
    solved = inverse_apply(lower_part, stacked)
    value_width = value_rows.shape[-1]
    written = solved[..., :value_width]
    erased = solved[..., value_width:]
    scores = decay_incl * jnp.einsum('...id,...jd->...ij', query_rows, key_rows, precision=exact_mode)
    query_state = growth[..., None] * query_rows - jnp.einsum('...ij,...jd->...id', scores, erased, precision=exact_mode)
    local_out = jnp.einsum('...ij,...jd->...id', scores, written, precision=exact_mode)
    to_end = jnp.exp(totals[..., -1:] - totals)
    faded_keys = to_end[..., None] * key_rows
    identity = jnp.eye(key_rows.shape[-1], dtype=jnp.float32)
    transition = jnp.exp(totals[..., -1])[..., None, None] * identity - jnp.einsum('...ci,...cj->...ij', faded_keys, erased, precision=exact_mode)
    offset = jnp.einsum('...ci,...cj->...ij', faded_keys, written, precision=exact_mode)
    return (query_state, local_out, transition, offset)

def head_mixer(pieces):
    query_part, key_part, value_part, decay_part, strength_part = pieces
    query_state, local_out, transition, offset = block_terms(query_part, key_part, value_part, decay_part, strength_part)

    def advance(carried, block_pieces):
        state_query, state_free, trans_block, offset_block = block_pieces
        produced = jnp.dot(state_query, carried, precision=exact_mode) + state_free
        return (jnp.dot(trans_block, carried, precision=exact_mode) + offset_block, produced)
    initial = jnp.zeros((key_part.shape[-1], value_part.shape[-1]), jnp.float32)
    final_state, outputs = lax.scan(advance, initial, (query_state, local_out, transition, offset))
    return outputs

def into_blocks(matrix, head_count, block_count):
    return matrix.reshape(block_count, BLOCK, head_count, DK).transpose(2, 0, 1, 3)

def gate_blocks(matrix, head_count, block_count):
    return matrix.reshape(block_count, BLOCK, head_count).transpose(2, 0, 1)

def grouped_sum(left_rows, right_rows, groups):
    inner = left_rows.shape[1] // groups
    total = jnp.zeros((left_rows.shape[0], right_rows.shape[1]), jnp.float32)
    for group_index in range(groups):
        piece = jnp.dot(left_rows[:, group_index * inner:(group_index + 1) * inner], right_rows[group_index * inner:(group_index + 1) * inner], preferred_element_type=jnp.float32)
        rounded = lax.optimization_barrier(piece.astype(jnp.bfloat16))
        total = total + rounded.astype(jnp.float32)
    return total

def reference(tokens, norm_gain, w_query, w_key, w_value, w_decay, w_beta, head_rates, head_gain, w_out, ffn_gain, w_up, conv_taps, w_down):
    normed = root_scale(tokens, norm_gain).astype(jnp.bfloat16)
    query_all = jnp.dot(normed, w_query, preferred_element_type=jnp.float32).astype(jnp.bfloat16)
    key_all = jnp.dot(normed, w_key, preferred_element_type=jnp.float32).astype(jnp.bfloat16)
    value_all = jnp.dot(normed, w_value, preferred_element_type=jnp.float32).astype(jnp.bfloat16)
    decay_pre = jnp.dot(normed, w_decay, preferred_element_type=jnp.float32)
    log_decay = -head_rates[0] * jax.nn.softplus(decay_pre)
    strength = jax.nn.sigmoid(jnp.dot(normed, w_beta, preferred_element_type=jnp.float32) + head_rates[1])
    block_count = TOKENS // BLOCK
    query_rows = into_blocks(query_all.astype(jnp.float32), HEADS, block_count)
    key_rows = unit_rows(into_blocks(key_all.astype(jnp.float32), HEADS, block_count))
    value_rows = into_blocks(value_all.astype(jnp.float32), HEADS, block_count)
    outputs = lax.map(head_mixer, (query_rows, key_rows, value_rows, gate_blocks(log_decay, HEADS, block_count), gate_blocks(strength, HEADS, block_count)))
    head_out = outputs.reshape(HEADS, TOKENS, DK).transpose(1, 0, 2)
    mixed_heads = root_scale(head_out, head_gain).astype(jnp.bfloat16).reshape(TOKENS, HEADS * DK)
    middle = (tokens.astype(jnp.float32) + grouped_sum(mixed_heads, w_out, N_HEAD)).astype(jnp.bfloat16)
    hidden_in = root_scale(middle, ffn_gain).astype(jnp.bfloat16)
    lifted = jnp.dot(hidden_in, w_up, preferred_element_type=jnp.float32).astype(jnp.bfloat16)
    padded = jnp.pad(lifted, ((1, 1), (0, 0)))
    tap_values = conv_taps.astype(jnp.float32)
    convolved = tap_values[0] * padded[:-2] + tap_values[1] * padded[1:-1] + tap_values[2] * padded[2:]
    activated = jax.nn.gelu(convolved, approximate=True).astype(jnp.bfloat16)
    return (middle.astype(jnp.float32) + grouped_sum(activated, w_down, N_HEAD)).astype(jnp.bfloat16)
```

```python
import functools

import jax
import jax.numpy as jnp
from jax import lax
from jax.experimental import pallas as pl
from jax.experimental.pallas import tpu as pltpu
from jax.sharding import PartitionSpec as P

DK = 128
BLOCK = 128
epsilon = 1e-06
f32 = jnp.float32
bf16 = jnp.bfloat16
LIMIT = 56 * 1024 * 1024

VM = pl.BlockSpec(memory_space=pltpu.VMEM)
SM = pl.BlockSpec(memory_space=pltpu.SMEM)
ANY = pl.BlockSpec(memory_space=pl.ANY)


def params():
    return pltpu.CompilerParams(vmem_limit_bytes=LIMIT)


def dot(a, b):
    return jnp.dot(a, b, preferred_element_type=f32)


def dot_nt(a, b):
    return lax.dot_general(a, b, (((1,), (1,)), ((), ())), preferred_element_type=f32)


def dot_tn(a, b):
    return lax.dot_general(a, b, (((0,), (0,)), ((), ())), preferred_element_type=f32)


def iotas(shape):
    return lax.broadcasted_iota(jnp.int32, shape, 0), lax.broadcasted_iota(jnp.int32, shape, 1)


def maps_kernel(n, width, heads, order, *refs):
    pieces = refs[:n]
    gain, rates, weights, normed, keys, erased, entry, maps, totals = refs[n : n + 9]
    held, raw_k, raw_v, total_b, beta_b, total_t, sem = refs[n + 9 :]
    count, part = pieces[0].shape
    blocks = count // BLOCK
    inner = heads * DK
    copies = [
        pltpu.make_async_copy(
            weights.at[pl.ds(pl.multiple_of(order[p] * width, 128), width)],
            held.at[pl.ds(p * width, width)],
            sem.at[p],
        )
        for p in range(n)
    ]
    for copy in copies:
        copy.start()
    tail = (part // 128) * 128
    for p in range(n):
        if tail < width:
            normed[:, p * width + tail : (p + 1) * width] = jnp.zeros((count, width - tail), bf16)

    @pl.loop(0, count // 32)
    def _(r):
        rows = pl.ds(pl.multiple_of(r * 32, 32), 32)
        values = [ref[rows, :].astype(f32) for ref in pieces]
        square = sum(jnp.sum(v * v, axis=1, keepdims=True) for v in values)
        inverse = lax.rsqrt(square / (n * part) + epsilon)
        for p, v in enumerate(values):
            scale = gain[pl.ds(order[p], 1), :][:, :part]
            normed[rows, p * width : p * width + part] = (v * inverse * scale).astype(bf16)

    for copy in copies:
        copy.wait()

    pre = dot(normed[...], held[:, 2 * inner : 2 * inner + 128])
    soft = jnp.maximum(pre, 0.0) + jnp.log1p(jnp.exp(-jnp.abs(pre)))
    decay = -rates[0:1, :] * soft
    beta = jax.nn.sigmoid(pre + rates[1:2, :])
    row_at, col_at = iotas((BLOCK, BLOCK))
    lower = (row_at >= col_at).astype(f32)
    for c in range(blocks):
        part_total = jnp.dot(
            lower,
            decay[c * BLOCK : (c + 1) * BLOCK],
            precision=lax.Precision.HIGHEST,
            preferred_element_type=f32,
        )
        totals[c * BLOCK : (c + 1) * BLOCK, :] = part_total
        total_t[c] = part_total.T
    for h in range(heads):
        total_b[h] = jnp.broadcast_to(totals[:, h : h + 1], (count, DK))
        beta_b[h] = jnp.broadcast_to(beta[:, heads + h : heads + h + 1], (count, DK))

    @pl.loop(0, inner // 256)
    def _(t):
        cols = pl.ds(pl.multiple_of(t * 256, 256), 256)
        raw_k[:, cols] = dot(normed[...], held[:, cols]).astype(bf16)
        more = pl.ds(pl.multiple_of(inner + t * 256, 256), 256)
        raw_v[:, cols] = dot(normed[...], held[:, more]).astype(bf16)

    xor = jnp.where(row_at > col_at, row_at ^ col_at, 0)
    eye = jnp.where(row_at == col_at, 1.0, 0.0)

    @pl.loop(0, heads)
    def _(h):
        cols = pl.ds(pl.multiple_of(h * DK, DK), DK)
        wide = pl.ds(pl.multiple_of(h * 2 * DK, 2 * DK), 2 * DK)
        raw = raw_k[:, cols].astype(f32)
        unit = raw * lax.rsqrt(jnp.sum(raw * raw, axis=1, keepdims=True) + epsilon)
        keys[:, cols] = unit.astype(bf16)
        rows = [slice(c * BLOCK, (c + 1) * BLOCK) for c in range(blocks)]
        lows, solved = [], []
        for c in range(blocks):
            k = keys[rows[c], cols]
            t_col = total_b[h, rows[c], :]
            t_row = total_t[c, pl.ds(h, 1), :]
            fade = jnp.exp(jnp.minimum(t_col - t_row, 0.0))
            low = jnp.where(xor > 0, beta_b[h, rows[c], :] * fade * dot_nt(k, k), 0.0)
            lows.append(low)
            solved.append(eye - jnp.where(xor == 1, low, 0.0))
        size = 2
        while size < BLOCK:
            mask = (xor >= size) & (xor < 2 * size)
            first = []
            for c in range(blocks):
                link = jnp.where(mask, lows[c], 0.0).astype(bf16)
                first.append(dot(link, solved[c].astype(bf16)).astype(bf16))
            solved = [
                solved[c] - dot(solved[c].astype(bf16), first[c]) for c in range(blocks)
            ]
            size *= 2
        state = None
        grown = []
        for c in range(blocks):
            k = keys[rows[c], cols].astype(f32)
            t_col = total_b[h, rows[c], :]
            b_col = beta_b[h, rows[c], :]
            right = jnp.concatenate(
                [
                    (b_col * jnp.exp(t_col) * k).astype(bf16),
                    (b_col * raw_v[rows[c], cols].astype(f32)).astype(bf16),
                ],
                axis=1,
            )
            both = dot(solved[c].astype(bf16), right).astype(bf16)
            erased[rows[c], wide] = both
            t_end = t_col[BLOCK - 1 : BLOCK, :]
            faded = (jnp.exp(t_end - t_col) * k).astype(bf16)
            grown.append((jnp.exp(t_end), dot_tn(faded, both)))
        for c in range(blocks):
            end, product = grown[c]
            erase, write = product[:, :DK], product[:, DK:]
            if c == 0:
                state = jnp.concatenate([end * eye - erase, write], axis=1)
            else:
                step = dot(erase.astype(bf16), state.astype(bf16))
                state = (
                    jnp.concatenate([end, end], axis=1) * state
                    - step
                    + jnp.concatenate([jnp.zeros_like(write), write], axis=1)
                )
            if c < blocks - 1:
                entry[c, :, wide] = state.astype(bf16)
        maps[h] = state.astype(bf16)


def block_maps(order, pieces, gain, rates, weights, heads, width):
    n = len(pieces)
    count = pieces[0].shape[0]
    blocks = count // BLOCK
    inner = heads * DK
    return pl.pallas_call(
        functools.partial(maps_kernel, n, width, heads),
        out_shape=(
            jax.ShapeDtypeStruct((count, n * width), bf16),
            jax.ShapeDtypeStruct((count, inner), bf16),
            jax.ShapeDtypeStruct((count, 2 * inner), bf16),
            jax.ShapeDtypeStruct((blocks - 1, DK, 2 * inner), bf16),
            jax.ShapeDtypeStruct((heads, DK, 2 * DK), bf16),
            jax.ShapeDtypeStruct((count, 128), f32),
        ),
        in_specs=[SM] + [VM] * (n + 2) + [ANY],
        out_specs=[VM] * 6,
        scratch_shapes=[
            pltpu.VMEM((n * width, 2 * inner + 128), bf16),
            pltpu.VMEM((count, inner), bf16),
            pltpu.VMEM((count, inner), bf16),
            pltpu.VMEM((heads, count, DK), f32),
            pltpu.VMEM((heads, count, DK), f32),
            pltpu.VMEM((blocks, BLOCK, 128), f32),
            pltpu.SemaphoreType.DMA((n,)),
        ],
        compiler_params=params(),
        cost_estimate=pl.CostEstimate(
            flops=8 * 10**9, bytes_accessed=12 * 10**6, transcendentals=10**6
        ),
        name="block_maps",
    )(order, *pieces, gain, rates, weights)


def query_kernel(n, width, order, normed, weights, query, held, sem):
    copies = [
        pltpu.make_async_copy(
            weights.at[pl.ds(pl.multiple_of(order[p] * width, 128), width)],
            held.at[pl.ds(p * width, width)],
            sem.at[p],
        )
        for p in range(n)
    ]
    for copy in copies:
        copy.start()
    for copy in copies:
        copy.wait()

    @pl.loop(0, query.shape[1] // 256)
    def _(t):
        cols = pl.ds(pl.multiple_of(t * 256, 256), 256)
        query[:, cols] = dot(normed[...], held[:, cols]).astype(bf16)


def queries(order, normed, weights, width):
    n = normed.shape[1] // width
    return pl.pallas_call(
        functools.partial(query_kernel, n, width),
        out_shape=jax.ShapeDtypeStruct((normed.shape[0], weights.shape[1]), bf16),
        in_specs=[SM, VM, ANY],
        out_specs=VM,
        scratch_shapes=[pltpu.VMEM(weights.shape, bf16), pltpu.SemaphoreType.DMA((n,))],
        compiler_params=params(),
        cost_estimate=pl.CostEstimate(
            flops=2 * 10**9, bytes_accessed=6 * 10**6, transcendentals=0
        ),
        name="queries",
    )(order, normed, weights)


def outputs_kernel(heads, query, keys, erased, entry, totals, after, shard_query, free, total_t):
    count = query.shape[0]
    blocks = count // BLOCK
    row_at, col_at = iotas((BLOCK, BLOCK))
    for c in range(blocks):
        total_t[c] = totals[c * BLOCK : (c + 1) * BLOCK, :].T
    for h in range(heads):
        cols = slice(h * DK, (h + 1) * DK)
        wide = slice(h * 2 * DK, (h + 1) * 2 * DK)
        for c in range(blocks):
            rows = slice(c * BLOCK, (c + 1) * BLOCK)
            t_col = jnp.broadcast_to(totals[rows, h : h + 1], (BLOCK, BLOCK))
            t_row = total_t[c, h : h + 1, :]
            fade = jnp.where(row_at >= col_at, jnp.exp(jnp.minimum(t_col - t_row, 0.0)), 0.0)
            q = query[rows, cols]
            scores = (fade * dot_nt(q, keys[rows, cols])).astype(bf16)
            both = dot(scores, erased[rows, wide])
            reach = jnp.exp(t_col) * q.astype(f32) - both[:, :DK]
            local = both[:, DK:]
            if c > 0:
                product = dot(reach.astype(bf16), entry[c - 1, :, wide])
                reach = product[:, :DK]
                local = local + product[:, DK:]
            shard_query[rows, cols] = reach.astype(bf16)
            free[rows, cols] = local


def block_outputs(query, keys, erased, entry, totals, after, heads):
    count = query.shape[0]
    return pl.pallas_call(
        functools.partial(outputs_kernel, heads),
        out_shape=(
            jax.ShapeDtypeStruct(query.shape, bf16),
            jax.ShapeDtypeStruct(query.shape, f32),
        ),
        in_specs=[VM] * 5 + [ANY],
        out_specs=[VM] * 2,
        scratch_shapes=[pltpu.VMEM((count // BLOCK, BLOCK, 128), f32)],
        compiler_params=params(),
        cost_estimate=pl.CostEstimate(
            flops=3 * 10**9, bytes_accessed=4 * 10**6, transcendentals=10**6
        ),
        name="block_outputs",
    )(query, keys, erased, entry, totals, after)


def pair_kernel(place, own, other, pair, first, done):
    even = place[0] == 0
    for h in range(own.shape[0]):
        mine, theirs = own[h], other[h]
        early = jnp.where(even, mine, theirs)
        late = jnp.where(even, theirs, mine)
        product = dot(late[:, :DK], early)
        shift = late[:, DK:].astype(f32)
        pair[h] = (product + jnp.concatenate([jnp.zeros_like(shift), shift], axis=1)).astype(bf16)
        first[h] = early
    done[...] = jnp.zeros_like(done)


def pair_maps(place, own, other):
    return pl.pallas_call(
        pair_kernel,
        out_shape=(
            jax.ShapeDtypeStruct(own.shape, bf16),
            jax.ShapeDtypeStruct(own.shape, bf16),
            jax.ShapeDtypeStruct((8, 128), f32),
        ),
        in_specs=[SM, VM, VM],
        out_specs=[VM] * 3,
        compiler_params=params(),
        name="pair_maps",
    )(place, own, other)


def apply_map(whole, state):
    high = state.astype(bf16)
    low = (state - high.astype(f32)).astype(bf16)
    product = dot(whole[:, :DK], jnp.concatenate([high, low], axis=1))
    return product[:, :DK] + product[:, DK:] + whole[:, DK:].astype(f32)


def start_kernel(steps, place, first, *refs):
    pairs, (keep, give) = refs[:steps], refs[steps:]
    even = place[0] == 0
    for h in range(first.shape[0]):
        state = pairs[0][h][:, DK:].astype(f32)
        for pair in pairs[1:]:
            state = apply_map(pair[h], state)
        later = apply_map(first[h], state)
        keep[h] = jnp.where(even, state, later).astype(bf16)
        give[h] = jnp.where(even, later, state).astype(bf16)


def start_states(place, first, pairs):
    heads = first.shape[0]
    shape = jax.ShapeDtypeStruct((heads, DK, DK), bf16)
    return pl.pallas_call(
        functools.partial(start_kernel, len(pairs)),
        out_shape=(shape, shape),
        in_specs=[SM] + [VM] * (1 + len(pairs)),
        out_specs=[VM] * 2,
        compiler_params=params(),
        name="start_states",
    )(place, first, *pairs)


def mixer_kernel(heads, units, place, own, other, shard_query, free, gain, weights, give, keep, mixed, held, sem):
    copy = pltpu.make_async_copy(weights, held, sem)
    copy.start()
    even = place[0] == 0
    core = place[1]
    half = heads // 2
    for u, unit in enumerate(units):
        rows = slice(unit * BLOCK, (unit + 1) * BLOCK)
        for h in range(heads):
            cols = slice(h * DK, (h + 1) * DK)
            if h < half:
                state = jnp.where(even, own[h], other[h])
            else:
                state = jnp.where(even, other[h - half], own[h - half])
            out = dot(shard_query[rows, cols], state) + free[rows, cols]
            scale = lax.rsqrt(jnp.mean(out * out, axis=1, keepdims=True) + epsilon)
            mixed[u * BLOCK : (u + 1) * BLOCK, cols] = (
                out * scale * gain[...].astype(f32)
            ).astype(bf16)
    copy.wait()
    give_rows = pl.ds(pl.multiple_of((1 - core) * BLOCK, BLOCK), BLOCK)
    keep_rows = pl.ds(pl.multiple_of(core * BLOCK, BLOCK), BLOCK)
    give[...] = dot(mixed[give_rows, :], held[...]).astype(bf16)
    keep[...] = dot(mixed[keep_rows, :], held[...]).astype(bf16)


def mixer_out(place, own, other, shard_query, free, gain, weights, heads, units):
    shape = jax.ShapeDtypeStruct((BLOCK, weights.shape[1]), bf16)
    return pl.pallas_call(
        functools.partial(mixer_kernel, heads, units),
        out_shape=(shape, shape),
        in_specs=[SM] + [VM] * 5 + [ANY],
        out_specs=[VM] * 2,
        scratch_shapes=[
            pltpu.VMEM((2 * BLOCK, heads * DK), bf16),
            pltpu.VMEM(weights.shape, bf16),
            pltpu.SemaphoreType.DMA,
        ],
        compiler_params=params(),
        cost_estimate=pl.CostEstimate(
            flops=10**9, bytes_accessed=5 * 10**6, transcendentals=0
        ),
        name="mixer_out",
    )(place, own, other, shard_query, free, gain, weights)


def up_kernel(place, own, other, gain, weights, lifted, normed, held, sem):
    copy = pltpu.make_async_copy(weights, held, sem)
    copy.start()
    core = place[1]
    for u, ref in enumerate((own, other)):
        slot = core if u == 0 else 1 - core

        @pl.loop(0, BLOCK // 32)
        def _(r):
            rows = pl.ds(pl.multiple_of(r * 32, 32), 32)
            value = ref[rows, :].astype(f32)
            inverse = lax.rsqrt(jnp.mean(value * value, axis=1, keepdims=True) + epsilon)
            target = pl.ds(pl.multiple_of(slot * BLOCK + r * 32, 32), 32)
            normed[target, :] = (value * inverse * gain[...].astype(f32)).astype(bf16)

    copy.wait()
    lifted[...] = dot(normed[...], held[...]).astype(bf16)


def up_project(place, own, other, gain, weights):
    return pl.pallas_call(
        up_kernel,
        out_shape=jax.ShapeDtypeStruct((2 * BLOCK, weights.shape[1]), bf16),
        in_specs=[SM, VM, VM, VM, ANY],
        out_specs=VM,
        scratch_shapes=[
            pltpu.VMEM((2 * BLOCK, weights.shape[0]), bf16),
            pltpu.VMEM(weights.shape, bf16),
            pltpu.SemaphoreType.DMA,
        ],
        compiler_params=params(),
        cost_estimate=pl.CostEstimate(
            flops=2 * 10**9, bytes_accessed=8 * 10**6, transcendentals=0
        ),
        name="up_project",
    )(place, own, other, gain, weights)


def gelu_of(x):
    inner = 0.7978845608028654 * (x + 0.044715 * (x * x * x))
    return 0.5 * x * (1.0 + jnp.tanh(inner))


def down_kernel(n_out, order, outer, inside, before, after, taps, weights, *refs):
    outs = refs[:n_out]
    act, padded, held, sem = refs[n_out:]
    copies = [
        pltpu.make_async_copy(weights.at[order[p]], held.at[p], sem.at[p]) for p in range(n_out)
    ]
    for copy in copies:
        copy.start()
    count = act.shape[0]
    padded[7:8, :] = before[...].astype(f32)
    padded[8 : 8 + BLOCK, :] = outer[0:BLOCK, :].astype(f32)
    padded[8 + BLOCK : 8 + count - BLOCK, :] = inside[...].astype(f32)
    padded[8 + count - BLOCK : 8 + count, :] = outer[BLOCK:, :].astype(f32)
    padded[8 + count : 9 + count, :] = after[...].astype(f32)

    @pl.loop(0, count // 32)
    def _(r):
        base = pl.multiple_of(r * 32, 32)
        window = padded[pl.ds(base, 48), :]
        value = (
            taps[0:1, :] * window[7:39, :]
            + taps[1:2, :] * window[8:40, :]
            + taps[2:3, :] * window[9:41, :]
        )
        act[pl.ds(base, 32), :] = gelu_of(value).astype(bf16)

    for p in range(n_out):
        copies[p].wait()
        outs[p][...] = dot(act[...], held[p]).astype(bf16)


def down_project(order, outer, inside, before, after, taps, weights, n_out):
    hidden, part = weights.shape[1:]
    count = outer.shape[0] + inside.shape[0]
    shape = jax.ShapeDtypeStruct((count, part), bf16)
    results = pl.pallas_call(
        functools.partial(down_kernel, n_out),
        out_shape=[shape] * n_out + [jax.ShapeDtypeStruct((count, hidden), bf16)],
        in_specs=[SM] + [VM] * 5 + [ANY],
        out_specs=[VM] * (n_out + 1),
        scratch_shapes=[
            pltpu.VMEM((count + 16, hidden), f32),
            pltpu.VMEM((n_out, hidden, part), bf16),
            pltpu.SemaphoreType.DMA((n_out,)),
        ],
        compiler_params=params(),
        cost_estimate=pl.CostEstimate(
            flops=3 * 10**9, bytes_accessed=8 * 10**6, transcendentals=10**6
        ),
        name="down_project",
    )(order, outer, inside, before, after, taps, weights)
    return results[:n_out], results[n_out]


def rest_kernel(n_out, order, act, weights, *refs):
    outs = refs[:n_out]
    held, sem = refs[n_out:]
    copies = [
        pltpu.make_async_copy(weights.at[order[p]], held.at[p], sem.at[p]) for p in range(n_out)
    ]
    for copy in copies:
        copy.start()
    for p in range(n_out):
        copies[p].wait()
        outs[p][...] = dot(act[...], held[p]).astype(bf16)


def rest_project(order, act, weights, n_out):
    hidden, part = weights.shape[1:]
    shape = jax.ShapeDtypeStruct((act.shape[0], part), bf16)
    return pl.pallas_call(
        functools.partial(rest_kernel, n_out),
        out_shape=[shape] * n_out,
        in_specs=[SM, VM, ANY],
        out_specs=[VM] * n_out,
        scratch_shapes=[
            pltpu.VMEM((n_out, hidden, part), bf16),
            pltpu.SemaphoreType.DMA((n_out,)),
        ],
        compiler_params=params(),
        cost_estimate=pl.CostEstimate(
            flops=2 * 10**9, bytes_accessed=6 * 10**6, transcendentals=0
        ),
        name="rest_project",
    )(order, act, weights)


def core_swap(value, n):
    return lax.ppermute(value, "head", [(i, i ^ 1) for i in range(n)])


def y_shift(value, n, step):
    return lax.ppermute(value, "head", [(i, (i + 2 * step) % n) for i in range(n)])


def pair_swap(value, n):
    return lax.ppermute(value, "seq", [(i, i ^ 1) for i in range(n)])


def later(value, n, step):
    return lax.ppermute(value, "seq", [(i, i + 2 * step) for i in range(n - 2 * step)])


def widened(matrix, n, part, width):
    cols = matrix.shape[1]
    return jnp.pad(matrix.reshape(n, part, cols), ((0, 0), (0, width - part), (0, 0))).reshape(
        n * width, cols
    )


def shards(
    tokens,
    norm_gain,
    w_query,
    w_key,
    w_value,
    w_decay,
    w_beta,
    head_rates,
    head_gain,
    w_out,
    ffn_gain,
    w_up,
    conv_taps,
    w_down,
):
    n = lax.axis_size("head")
    seqs = lax.axis_size("seq")
    me = lax.axis_index("head")
    at = lax.axis_index("seq")
    core = me % 2
    parity = at % 2
    ys = n // 2
    count, part = tokens.shape
    heads = w_query.shape[1] // DK
    half = heads // 2
    hidden = w_up.shape[1]
    width = -(-part // 128) * 128
    features = n * part

    along = [tokens] + [y_shift(tokens, n, d) for d in range(1, ys)]
    pieces, order = [], []
    for d, piece in enumerate(along):
        from_here = (me + n - 2 * d) % n
        pieces += [piece, core_swap(piece, n)]
        order += [from_here, from_here ^ 1]
    order = jnp.stack(order).astype(jnp.int32)

    gates = jnp.concatenate([w_decay, w_beta], axis=1)
    gates = jnp.pad(gates, ((0, 0), (0, 128 - 2 * heads)))
    w_kvg = widened(jnp.concatenate([w_key, w_value, gates], axis=1), n, part, width)
    w_q = widened(w_query, n, part, width)
    gain_rows = jnp.pad(
        norm_gain.astype(f32).reshape(n, part), ((0, 0), (0, width - part))
    )
    empty = jnp.zeros((heads,), f32)
    fill = jnp.zeros((128 - 2 * heads,), f32)
    rates = jnp.stack(
        [
            jnp.concatenate([head_rates[0], empty, fill]),
            jnp.concatenate([empty, head_rates[1], fill]),
        ]
    )
    rates = jnp.pad(rates, ((0, 6), (0, 0)))
    w_parts = w_down.reshape(hidden, n, part).transpose(1, 0, 2)

    normed, keys, erased, entry, maps, totals = block_maps(
        order, pieces, gain_rows, rates, w_kvg, heads, width
    )

    place = jnp.stack([parity, core]).astype(jnp.int32)
    own_maps = lax.dynamic_slice_in_dim(maps, parity * half, half, 0)
    sent_maps = lax.dynamic_slice_in_dim(maps, (1 - parity) * half, half, 0)
    other_maps = pair_swap(sent_maps, seqs)
    query = queries(order, normed, w_q, width)
    pair, first, done = pair_maps(place, own_maps, other_maps)
    pairs = [later(pair, seqs, d) for d in range(seqs // 2 - 1, 0, -1)]
    shard_query, free = block_outputs(query, keys, erased, entry, totals, done, heads)
    kept_state, given_state = start_states(place, first, pairs)
    other_state = pair_swap(given_state, seqs)

    by_place = [None] * n
    whole = jnp.zeros((count, n, part), bf16)
    for j in range(n):
        block = pieces[0]
        for p in range(1, n):
            block = jnp.where(order[p] == j, pieces[p], block)
        by_place[j] = block
    whole = jnp.concatenate(by_place, axis=1)

    blocks = count // BLOCK
    head_scale = head_gain.reshape(1, DK)
    ffn_scale = ffn_gain.reshape(1, features)
    lifted = []
    middles = [None] * blocks
    for units in ((0, 3), (1, 2)):
        give, keep = mixer_out(
            place, kept_state, other_state, shard_query, free, head_scale, w_out, heads, units
        )
        arrived = core_swap(give, n)
        chip = (keep.astype(f32) + arrived.astype(f32)).astype(bf16)
        row = jnp.where(core == 0, units[0], units[1]) * BLOCK
        total = lax.dynamic_slice_in_dim(whole, row, BLOCK, 0).astype(f32) + chip.astype(f32)
        for d in range(1, ys):
            total = total + y_shift(chip, n, d).astype(f32)
        mid_own = total.astype(bf16)
        mid_other = core_swap(mid_own, n)
        lifted.append(up_project(place, mid_own, mid_other, ffn_scale, w_up))
        middles[units[0]] = jnp.where(core == 0, mid_own, mid_other)
        middles[units[1]] = jnp.where(core == 0, mid_other, mid_own)
    outer, inside = lifted

    up = [(i, i + 1) for i in range(seqs - 1)]
    down = [(i + 1, i) for i in range(seqs - 1)]
    before = lax.ppermute(outer[2 * BLOCK - 1 : 2 * BLOCK], "seq", up)
    after = lax.ppermute(outer[0:1], "seq", down)

    target, order_far = [], []
    for d in range(1, ys):
        there = (me + 2 * d) % n
        order_far += [there ^ 1, there]
    order_far = jnp.stack(order_far).astype(jnp.int32)
    order_near = jnp.stack([me ^ 1, me]).astype(jnp.int32)
    taps = conv_taps.astype(f32)
    far, act = down_project(
        order_far, outer, inside, before, after, taps, w_parts, 2 * (ys - 1)
    )
    near_give, near_keep = rest_project(order_near, act, w_parts, 2)
    total = near_keep.astype(f32)
    for d in range(1, ys):
        chip = (
            far[2 * d - 1].astype(f32) + core_swap(far[2 * d - 2], n).astype(f32)
        ).astype(bf16)
        total = total + y_shift(chip, n, d).astype(f32)
    total = total + core_swap(near_give, n).astype(f32)
    middle = jnp.concatenate(middles, axis=0)
    middle_part = lax.dynamic_slice_in_dim(middle, me * part, part, 1)
    return (middle_part.astype(f32) + total).astype(bf16)


def solution(mesh):
    placed = (
        P("seq", "head"),
        P(),
        P(None, "head"),
        P(None, "head"),
        P(None, "head"),
        P(None, "head"),
        P(None, "head"),
        P(None, "head"),
        P(),
        P("head", None),
        P(),
        P(None, "head"),
        P(None, "head"),
        P("head", None),
    )
    return jax.shard_map(
        shards, mesh=mesh, in_specs=placed, out_specs=P("seq", "head"), check_vma=False
    )
```

```python
import functools

import jax
import jax.numpy as jnp
from jax import lax
from jax.experimental import pallas as pl
from jax.experimental.pallas import tpu as pltpu
from jax.sharding import PartitionSpec as P

DK = 128
BLOCK = 128
epsilon = 1e-06
f32 = jnp.float32
bf16 = jnp.bfloat16

VM = pl.BlockSpec(memory_space=pltpu.VMEM)
SM = pl.BlockSpec(memory_space=pltpu.SMEM)
ANY = pl.BlockSpec(memory_space=pl.ANY)


def params(mebibytes):
    return pltpu.CompilerParams(vmem_limit_bytes=mebibytes * 1024 * 1024)


def cost(flops, moved):
    return pl.CostEstimate(flops=flops, bytes_accessed=moved, transcendentals=0)


def shape_of(shape, dtype=bf16):
    return jax.ShapeDtypeStruct(shape, dtype)


def dot(a, b):
    return jnp.dot(a, b, preferred_element_type=f32)


def dot_nt(a, b):
    return lax.dot_general(a, b, (((1,), (1,)), ((), ())), preferred_element_type=f32)


def dot_tn(a, b):
    return lax.dot_general(a, b, (((0,), (0,)), ((), ())), preferred_element_type=f32)


def iotas(shape):
    return lax.broadcasted_iota(jnp.int32, shape, 0), lax.broadcasted_iota(jnp.int32, shape, 1)


def column_of(row, lanes=128):
    return jnp.broadcast_to(row, (lanes, row.shape[1])).T


def square_sums(ref, features):
    tokens = ref.shape[1]

    def step(r, total):
        value = ref[pl.ds(pl.multiple_of(r * 32, 32), 32), :].astype(f32)
        value = value * value
        return total + (value[0:8] + value[8:16]) + (value[16:24] + value[24:32])

    total = lax.fori_loop(0, features // 32, step, jnp.zeros((8, tokens), f32))
    return jnp.sum(total, axis=0, keepdims=True)


def scaled_rows(ref, features, inverse, gain, target):
    full = features // 128

    def one(start, size):
        value = ref[pl.ds(start, size), :].astype(f32)
        scale = column_of(gain[:, pl.ds(start, size)].astype(f32))
        scale = jnp.concatenate([scale] * (value.shape[1] // 128), axis=1)
        target[:, pl.ds(start, size)] = (value * inverse * scale).astype(bf16).T

    @pl.loop(0, full)
    def _(f):
        one(pl.multiple_of(f * 128, 128), 128)

    if features % 128:
        one(full * 128, features % 128)


def maps_kernel(n, heads, slots, meta, *refs):
    pieces = refs[:n]
    gain, rates, gates, w_key, w_value = refs[n : n + 5]
    outs = refs[n + 5 : n + 13]
    normed, keys, erased, entry, own, sent, totals, part_a = outs[:8]
    part_b = refs[n + 13]
    whole, held_k, held_v, raw_k, raw_v, rows_at_head, total_b, beta_b, sem = refs[n + 14 :]
    features, count = whole.shape
    part = pieces[0].shape[0]
    blocks = count // BLOCK
    inner = heads * DK
    parity = meta[slots]
    copies = [
        pltpu.make_async_copy(
            pieces[p],
            whole.at[pl.ds(pl.multiple_of(meta[p] * part, 16), part)],
            sem.at[p],
        )
        for p in range(n)
    ]
    for copy in copies:
        copy.start()
    copy_k = pltpu.make_async_copy(w_key, held_k, sem.at[n])
    copy_v = pltpu.make_async_copy(w_value, held_v, sem.at[n + 1])
    copy_k.start()
    copy_v.start()
    for copy in copies:
        copy.wait()

    inverse = lax.rsqrt(square_sums(whole, features) / features + epsilon)
    scaled_rows(whole, features, inverse, gain, normed)

    part_a[:, :BLOCK] = whole[:, :BLOCK]
    part_a[:, BLOCK:] = whole[:, count - BLOCK :]
    part_b[...] = whole[:, BLOCK : count - BLOCK]

    pre = dot_nt(gates[...], normed[...])
    soft = jnp.maximum(pre, 0.0) + jnp.log1p(jnp.exp(-jnp.abs(pre)))
    rate = jnp.concatenate([rates[...]] * (count // 128), axis=1)
    decay = -rate * soft
    beta = jax.nn.sigmoid(pre + rate)
    row_at, col_at = iotas((BLOCK, BLOCK))
    upper = (row_at <= col_at).astype(f32)
    rows_at_head[...] = jnp.zeros_like(rows_at_head)
    for c in range(blocks):
        tokens = slice(c * BLOCK, (c + 1) * BLOCK)
        total = jnp.dot(
            decay[:, tokens], upper, precision=lax.Precision.HIGHEST, preferred_element_type=f32
        )
        totals[c] = total
        rows_at_head[0:16, :] = total
        rows_at_head[16:32, :] = beta[:, tokens]
        columns = rows_at_head[...].T
        for h in range(heads):
            total_b[h, tokens, :] = jnp.broadcast_to(columns[:, h : h + 1], (BLOCK, DK))
            at = 16 + heads + h
            beta_b[h, tokens, :] = jnp.broadcast_to(columns[:, at : at + 1], (BLOCK, DK))

    copy_k.wait()
    copy_v.wait()

    @pl.loop(0, inner // 256)
    def _(t):
        cols = pl.ds(pl.multiple_of(t * 256, 256), 256)
        raw_k[:, cols] = dot(normed[...], held_k[:, cols]).astype(bf16)
        raw_v[:, cols] = dot(normed[...], held_v[:, cols]).astype(bf16)

    xor = jnp.where(row_at > col_at, row_at ^ col_at, 0)
    eye = jnp.where(row_at == col_at, 1.0, 0.0)
    group = 2 if heads % 2 == 0 else 1

    @pl.loop(0, heads // group)
    def _(at):
        lows, solved = [], []
        chains = []
        for g in range(group):
            h = at * group + g
            cols = pl.ds(pl.multiple_of(h * DK, DK), DK)
            wide = pl.ds(pl.multiple_of(h * 2 * DK, 2 * DK), 2 * DK)
            raw = raw_k[:, cols].astype(f32)
            unit = raw * lax.rsqrt(jnp.sum(raw * raw, axis=1, keepdims=True) + epsilon)
            keys[:, cols] = unit.astype(bf16)
            for c in range(blocks):
                chains.append((h, cols, wide, c, slice(c * BLOCK, (c + 1) * BLOCK)))
        for h, cols, wide, c, rows in chains:
            k = keys[rows, cols]
            fade = jnp.exp(jnp.minimum(total_b[h, rows, :] - totals[c, pl.ds(h, 1), :], 0.0))
            low = jnp.where(xor > 0, beta_b[h, rows, :] * fade * dot_nt(k, k), 0.0)
            lows.append(low)
            solved.append(eye - jnp.where(xor == 1, low, 0.0))
        size = 2
        while size < BLOCK:
            mask = (xor >= size) & (xor < 2 * size)
            first = []
            for i in range(len(chains)):
                link = jnp.where(mask, lows[i], 0.0).astype(bf16)
                first.append(dot(link, solved[i].astype(bf16)).astype(bf16))
            solved = [
                solved[i] - dot(solved[i].astype(bf16), first[i]) for i in range(len(chains))
            ]
            size *= 2
        grown = []
        for i, (h, cols, wide, c, rows) in enumerate(chains):
            k = keys[rows, cols].astype(f32)
            t_col = total_b[h, rows, :]
            b_col = beta_b[h, rows, :]
            right = jnp.concatenate(
                [
                    (b_col * jnp.exp(t_col) * k).astype(bf16),
                    (b_col * raw_v[rows, cols].astype(f32)).astype(bf16),
                ],
                axis=1,
            )
            both = dot(solved[i].astype(bf16), right).astype(bf16)
            erased[rows, wide] = both
            t_end = t_col[BLOCK - 1 : BLOCK, :]
            faded = (jnp.exp(t_end - t_col) * k).astype(bf16)
            grown.append((jnp.exp(t_end), dot_tn(faded, both)))
        states = [None] * group
        for c in range(blocks):
            for g in range(group):
                h, cols, wide = chains[g * blocks][:3]
                end, product = grown[g * blocks + c]
                erase, write = product[:, :DK], product[:, DK:]
                if c == 0:
                    state = jnp.concatenate([end * eye - erase, write], axis=1)
                else:
                    step = dot(erase.astype(bf16), states[g].astype(bf16))
                    state = (
                        jnp.concatenate([end, end], axis=1) * states[g]
                        - step
                        + jnp.concatenate([jnp.zeros_like(write), write], axis=1)
                    )
                if c < blocks - 1:
                    entry[c, :, wide] = state.astype(bf16)
                states[g] = state
        for g in range(group):
            h = at * group + g
            half = heads // 2
            mine = (h >= half) == (parity == 1)
            slot = lax.rem(h, half)

            @pl.when(mine)
            def _():
                own[slot] = states[g].astype(bf16)

            @pl.when(jnp.logical_not(mine))
            def _():
                sent[slot] = states[g].astype(bf16)


def block_maps(meta, slots, pieces, gain, rates, gates, w_key, w_value):
    n = len(pieces)
    count = pieces[0].shape[1]
    features, inner = w_key.shape
    heads = inner // DK
    blocks = count // BLOCK
    middle = count - 2 * BLOCK
    return pl.pallas_call(
        functools.partial(maps_kernel, n, heads, slots),
        out_shape=(
            shape_of((count, features)),
            shape_of((count, inner)),
            shape_of((count, 2 * inner)),
            shape_of((blocks - 1, DK, 2 * inner)),
            shape_of((heads // 2, DK, 2 * DK)),
            shape_of((heads // 2, DK, 2 * DK)),
            shape_of((blocks, 16, 128), f32),
            shape_of((features, 2 * BLOCK)),
            shape_of((features, middle)),
        ),
        in_specs=[SM] + [ANY] * n + [VM] * 3 + [ANY] * 2,
        out_specs=[VM] * 9,
        scratch_shapes=[
            pltpu.VMEM((features, count), bf16),
            pltpu.VMEM(w_key.shape, bf16),
            pltpu.VMEM(w_value.shape, bf16),
            pltpu.VMEM((count, inner), bf16),
            pltpu.VMEM((count, inner), bf16),
            pltpu.VMEM((128, BLOCK), f32),
            pltpu.VMEM((heads, count, DK), f32),
            pltpu.VMEM((heads, count, DK), f32),
            pltpu.SemaphoreType.DMA((n + 2,)),
        ],
        compiler_params=params(28),
        cost_estimate=cost(10 * 10**9, 14 * 10**6),
        name="block_maps",
    )(meta, *pieces, gain, rates, gates, w_key, w_value)


def query_kernel(normed, weights, query, done, held, sem):
    copy = pltpu.make_async_copy(weights, held, sem)
    copy.start()
    done[...] = jnp.zeros_like(done)
    copy.wait()

    @pl.loop(0, query.shape[1] // 256)
    def _(t):
        cols = pl.ds(pl.multiple_of(t * 256, 256), 256)
        query[:, cols] = dot(normed[...], held[:, cols]).astype(bf16)


def queries(normed, weights):
    return pl.pallas_call(
        query_kernel,
        out_shape=(shape_of((normed.shape[0], weights.shape[1])), shape_of((8, 128), f32)),
        in_specs=[VM, ANY],
        out_specs=[VM] * 2,
        scratch_shapes=[pltpu.VMEM(weights.shape, bf16), pltpu.SemaphoreType.DMA],
        compiler_params=params(16),
        cost_estimate=cost(2 * 10**9, 6 * 10**6),
        name="queries",
    )(normed, weights)


def outputs_kernel(heads, query, keys, erased, entry, totals, after, shard_query, free, done, rows_at_head):
    count = query.shape[0]
    blocks = count // BLOCK
    row_at, col_at = iotas((BLOCK, BLOCK))
    done[...] = jnp.zeros_like(done)
    rows_at_head[...] = jnp.zeros_like(rows_at_head)
    for c in range(blocks):
        rows = slice(c * BLOCK, (c + 1) * BLOCK)
        rows_at_head[0:16, :] = totals[c]
        columns = rows_at_head[...].T
        for h in range(heads):
            cols = slice(h * DK, (h + 1) * DK)
            wide = slice(h * 2 * DK, (h + 1) * 2 * DK)
            t_col = jnp.broadcast_to(columns[:, h : h + 1], (BLOCK, BLOCK))
            t_row = totals[c, h : h + 1, :]
            fade = jnp.where(row_at >= col_at, jnp.exp(jnp.minimum(t_col - t_row, 0.0)), 0.0)
            q = query[rows, cols]
            scores = (fade * dot_nt(q, keys[rows, cols])).astype(bf16)
            both = dot(scores, erased[rows, wide])
            reach = jnp.exp(t_col) * q.astype(f32) - both[:, :DK]
            local = both[:, DK:]
            if c > 0:
                product = dot(reach.astype(bf16), entry[c - 1, :, wide])
                reach = product[:, :DK]
                local = local + product[:, DK:]
            shard_query[rows, cols] = reach.astype(bf16)
            free[rows, cols] = local


def block_outputs(query, keys, erased, entry, totals, after):
    heads = query.shape[1] // DK
    return pl.pallas_call(
        functools.partial(outputs_kernel, heads),
        out_shape=(shape_of(query.shape), shape_of(query.shape, f32), shape_of((8, 128), f32)),
        in_specs=[VM] * 5 + [ANY],
        out_specs=[VM] * 3,
        scratch_shapes=[pltpu.VMEM((128, BLOCK), f32)],
        compiler_params=params(16),
        cost_estimate=cost(3 * 10**9, 4 * 10**6),
        name="block_outputs",
    )(query, keys, erased, entry, totals, after)


def pair_kernel(slots, meta, own, other, after, pair, first, done):
    even = meta[slots] == 0
    for h in range(own.shape[0]):
        mine, theirs = own[h], other[h]
        early = jnp.where(even, mine, theirs)
        late = jnp.where(even, theirs, mine)
        product = dot(late[:, :DK], early)
        shift = late[:, DK:].astype(f32)
        pair[h] = (product + jnp.concatenate([jnp.zeros_like(shift), shift], axis=1)).astype(bf16)
        first[h] = early
    done[...] = jnp.zeros_like(done)


def pair_maps(meta, slots, own, other, after):
    return pl.pallas_call(
        functools.partial(pair_kernel, slots),
        out_shape=(shape_of(own.shape), shape_of(own.shape), shape_of((8, 128), f32)),
        in_specs=[SM, VM, VM, ANY],
        out_specs=[VM] * 3,
        compiler_params=params(8),
        name="pair_maps",
    )(meta, own, other, after)


def apply_map(whole, state):
    high = state.astype(bf16)
    low = (state - high.astype(f32)).astype(bf16)
    product = dot(whole[:, :DK], jnp.concatenate([high, low], axis=1))
    return product[:, :DK] + product[:, DK:] + whole[:, DK:].astype(f32)


def start_kernel(slots, steps, meta, first, *refs):
    pairs, (after, keep, give) = refs[:steps], refs[steps:]
    even = meta[slots] == 0
    for h in range(first.shape[0]):
        state = pairs[0][h][:, DK:].astype(f32)
        for pair in pairs[1:]:
            state = apply_map(pair[h], state)
        later = apply_map(first[h], state)
        keep[h] = jnp.where(even, state, later).astype(bf16)
        give[h] = jnp.where(even, later, state).astype(bf16)


def start_states(meta, slots, first, pairs, after):
    heads = first.shape[0]
    shape = shape_of((heads, DK, DK))
    return pl.pallas_call(
        functools.partial(start_kernel, slots, len(pairs)),
        out_shape=(shape, shape),
        in_specs=[SM] + [VM] * (1 + len(pairs)) + [ANY],
        out_specs=[VM] * 2,
        compiler_params=params(8),
        name="start_states",
    )(meta, first, *pairs, after)


def mixed_kernel(heads, slots, meta, own, other, shard_query, free, gain, mixed_a, mixed_b):
    even = meta[slots] == 0
    half = heads // 2
    blocks = shard_query.shape[0] // BLOCK
    for h in range(heads):
        cols = slice(h * DK, (h + 1) * DK)
        if h < half:
            state = jnp.where(even, own[h], other[h])
        else:
            state = jnp.where(even, other[h - half], own[h - half])
        for unit in range(blocks):
            rows = slice(unit * BLOCK, (unit + 1) * BLOCK)
            out = dot(shard_query[rows, cols], state) + free[rows, cols]
            scale = lax.rsqrt(jnp.mean(out * out, axis=1, keepdims=True) + epsilon)
            value = (out * scale * gain[...].astype(f32)).astype(bf16)
            if unit == 0:
                mixed_a[:BLOCK, cols] = value
            elif unit == blocks - 1:
                mixed_a[BLOCK:, cols] = value
            else:
                mixed_b[(unit - 1) * BLOCK : unit * BLOCK, cols] = value


def mixed_heads(meta, slots, own, other, shard_query, free, gain):
    count, inner = shard_query.shape
    return pl.pallas_call(
        functools.partial(mixed_kernel, inner // DK, slots),
        out_shape=(shape_of((2 * BLOCK, inner)), shape_of((count - 2 * BLOCK, inner))),
        in_specs=[SM] + [VM] * 5,
        out_specs=[VM] * 2,
        compiler_params=params(12),
        cost_estimate=cost(10**9, 3 * 10**6),
        name="mixed_heads",
    )(meta, own, other, shard_query, free, gain)


def attend_kernel(slots, meta, own, other, weights, other_weights, chip):
    rows = pl.ds(pl.multiple_of(meta[slots + 1] * chip.shape[0], 16), chip.shape[0])
    total = dot_nt(weights[rows, :], own[...]) + dot_nt(other_weights[...], other[...])
    chip[...] = total.astype(bf16)


def attend(meta, slots, own, other, weights, other_weights):
    return pl.pallas_call(
        functools.partial(attend_kernel, slots),
        out_shape=shape_of((other_weights.shape[0], own.shape[0])),
        in_specs=[SM] + [VM] * 4,
        out_specs=VM,
        compiler_params=params(16),
        cost_estimate=cost(10**9, 5 * 10**6),
        name="attend",
    )(meta, own, other, weights, other_weights)


def up_kernel(slots, adds, meta, *refs):
    tokens = refs[0]
    own, other = refs[1 : 1 + adds], refs[1 + adds : 1 + 2 * adds]
    gain, weights, lifted, middle_part, first, last, middle, hidden, held, sem = refs[1 + 2 * adds :]
    copy = pltpu.make_async_copy(weights, held, sem)
    copy.start()
    core, me = meta[slots + 1], meta[slots + 2]
    features = middle.shape[0]
    half = features // 2
    step = 32
    for side, parts in ((core, own), (1 - core, other)):

        @pl.loop(0, half // step)
        def _(r):
            rows = pl.ds(pl.multiple_of(r * step, step), step)
            target = pl.ds(pl.multiple_of(side * half + r * step, 32), step)
            total = tokens[target, :].astype(f32)
            for ref in parts:
                total = total + ref[rows, :].astype(f32)
            middle[target, :] = total.astype(bf16).astype(f32)

    inverse = lax.rsqrt(square_sums(middle, features) / features + epsilon)
    scaled_rows(middle, features, inverse, gain, hidden)
    part = middle_part.shape[0]
    middle_part[...] = middle[pl.ds(pl.multiple_of(me * part, 8), part), :]
    copy.wait()
    lifted[...] = dot(hidden[...], held[...]).astype(bf16)
    count = lifted.shape[0]
    first[...] = lifted[0:1, :]
    last[...] = lifted[count - 1 : count, :]


def up_project(meta, slots, tokens, own, other, gain, weights, part):
    features, hidden = weights.shape
    count = tokens.shape[1]
    return pl.pallas_call(
        functools.partial(up_kernel, slots, len(own)),
        out_shape=(
            shape_of((count, hidden)),
            shape_of((part, count), f32),
            shape_of((1, hidden)),
            shape_of((1, hidden)),
        ),
        in_specs=[SM] + [VM] * (2 + 2 * len(own)) + [ANY],
        out_specs=[VM] * 4,
        scratch_shapes=[
            pltpu.VMEM((features, count), f32),
            pltpu.VMEM((count, features), bf16),
            pltpu.VMEM(weights.shape, bf16),
            pltpu.SemaphoreType.DMA,
        ],
        compiler_params=params(24),
        cost_estimate=cost(2 * 10**9, 8 * 10**6),
        name="up_project",
    )(meta, tokens, *own, *other, gain, weights)


def gelu_of(x):
    inner = 0.7978845608028654 * (x + 0.044715 * (x * x * x))
    return 0.5 * x * (1.0 + jnp.tanh(inner))


def down_kernel(n_out, at, meta, outer, inside, before, after, taps, weights, *refs):
    outs = refs[:n_out]
    act, padded, held, sem = refs[n_out:]
    copies = [
        pltpu.make_async_copy(weights.at[meta[at + p]], held.at[p], sem.at[p])
        for p in range(n_out)
    ]
    for copy in copies:
        copy.start()
    count = act.shape[0]
    padded[7:8, :] = before[...].astype(f32)
    padded[8 : 8 + BLOCK, :] = outer[0:BLOCK, :].astype(f32)
    padded[8 + BLOCK : 8 + count - BLOCK, :] = inside[...].astype(f32)
    padded[8 + count - BLOCK : 8 + count, :] = outer[BLOCK:, :].astype(f32)
    padded[8 + count : 9 + count, :] = after[...].astype(f32)

    @pl.loop(0, count // 32)
    def _(r):
        base = pl.multiple_of(r * 32, 32)
        window = padded[pl.ds(base, 48), :]
        value = (
            taps[0:1, :] * window[7:39, :]
            + taps[1:2, :] * window[8:40, :]
            + taps[2:3, :] * window[9:41, :]
        )
        act[pl.ds(base, 32), :] = gelu_of(value).astype(bf16)

    for p in range(n_out):
        copies[p].wait()
        outs[p][...] = dot_nt(held[p], act[...]).astype(bf16)


def down_project(meta, at, outer, inside, before, after, taps, weights, n_out):
    part, hidden = weights.shape[1:]
    count = outer.shape[0] + inside.shape[0]
    results = pl.pallas_call(
        functools.partial(down_kernel, n_out, at),
        out_shape=[shape_of((part, count))] * n_out + [shape_of((count, hidden))],
        in_specs=[SM] + [VM] * 5 + [ANY],
        out_specs=[VM] * (n_out + 1),
        scratch_shapes=[
            pltpu.VMEM((count + 16, hidden), f32),
            pltpu.VMEM((n_out, part, hidden), bf16),
            pltpu.SemaphoreType.DMA((n_out,)),
        ],
        compiler_params=params(24),
        cost_estimate=cost(4 * 10**9, 8 * 10**6),
        name="down_project",
    )(meta, outer, inside, before, after, taps, weights)
    return results[:n_out], results[n_out]


def rest_kernel(at, meta, act, middle_a, middle_b, weights, give, base, held, sem):
    copies = [
        pltpu.make_async_copy(weights.at[meta[at + p]], held.at[p], sem.at[p]) for p in range(2)
    ]
    for copy in copies:
        copy.start()
    count = act.shape[0]
    copies[0].wait()
    give[...] = dot_nt(held[0], act[...]).astype(bf16)
    copies[1].wait()
    kept = dot_nt(held[1], act[...]).astype(bf16).astype(f32)
    base[:, :BLOCK] = kept[:, :BLOCK] + middle_a[:, :BLOCK]
    base[:, BLOCK : count - BLOCK] = kept[:, BLOCK : count - BLOCK] + middle_b[...]
    base[:, count - BLOCK :] = kept[:, count - BLOCK :] + middle_a[:, BLOCK:]


def rest_project(meta, at, act, middle_a, middle_b, weights):
    part, hidden = weights.shape[1:]
    count = act.shape[0]
    return pl.pallas_call(
        functools.partial(rest_kernel, at),
        out_shape=(shape_of((part, count)), shape_of((part, count), f32)),
        in_specs=[SM] + [VM] * 3 + [ANY],
        out_specs=[VM] * 2,
        scratch_shapes=[
            pltpu.VMEM((2, part, hidden), bf16),
            pltpu.SemaphoreType.DMA((2,)),
        ],
        compiler_params=params(20),
        cost_estimate=cost(2 * 10**9, 6 * 10**6),
        name="rest_project",
    )(meta, act, middle_a, middle_b, weights)


def core_swap(value, n):
    return lax.ppermute(value, "head", [(i, i ^ 1) for i in range(n)])


def y_shift(value, n, step):
    return lax.ppermute(value, "head", [(i, (i + 2 * step) % n) for i in range(n)])


def pair_swap(value, n):
    return lax.ppermute(value, "seq", [(i, i ^ 1) for i in range(n)])


def later(value, n, step):
    return lax.ppermute(value, "seq", [(i, i + 2 * step) for i in range(n - 2 * step)])


def shards(
    tokens,
    norm_gain,
    w_query,
    w_key,
    w_value,
    w_decay,
    w_beta,
    head_rates,
    head_gain,
    w_out,
    ffn_gain,
    w_up,
    conv_taps,
    w_down,
):
    n = lax.axis_size("head")
    seqs = lax.axis_size("seq")
    me = lax.axis_index("head")
    at = lax.axis_index("seq")
    core = me % 2
    parity = at % 2
    ys = n // 2
    count, part = tokens.shape
    heads = w_query.shape[1] // DK
    hidden = w_up.shape[1]
    features = n * part

    mine = tokens.T
    along = [mine] + [y_shift(mine, n, d) for d in range(1, ys)]
    pieces, order = [], []
    for d, piece in enumerate(along):
        from_here = (me + n - 2 * d) % n
        pieces += [piece, core_swap(piece, n)]
        order += [from_here, from_here ^ 1]
    if part % 16:
        by_place = []
        for j in range(n):
            block = pieces[0]
            for p in range(1, n):
                block = jnp.where(order[p] == j, pieces[p], block)
            by_place.append(block)
        pieces, order = [jnp.concatenate(by_place, axis=0)], [jnp.zeros_like(me)]
    slots = len(order)
    far_order = []
    for d in range(1, ys):
        there = (me + 2 * d) % n
        far_order += [there ^ 1, there]
    near_order = [me ^ 1, me]
    meta = jnp.stack(order + [parity, core, me] + far_order + near_order).astype(jnp.int32)
    far_at = slots + 3
    near_at = far_at + len(far_order)

    w_out_t = w_out.T
    other_w_out = core_swap(
        lax.dynamic_slice_in_dim(w_out_t, (1 - core) * (features // 2), features // 2, 0), n
    )

    gates = jnp.concatenate([w_decay.T, w_beta.T], axis=0)
    gates = jnp.pad(gates, ((0, 16 - 2 * heads), (0, 0)))
    rates = jnp.pad(head_rates.reshape(2 * heads, 1), ((0, 16 - 2 * heads), (0, 0)))
    rates = jnp.broadcast_to(rates, (16, 128))
    taps = conv_taps.astype(f32)

    normed, keys, erased, entry, own_maps, sent_maps, totals, tokens_a, tokens_b = block_maps(
        meta, slots, pieces, norm_gain.reshape(1, features), rates, gates, w_key, w_value
    )

    other_maps = pair_swap(sent_maps, seqs)
    query, query_done = queries(normed, w_query)
    pair, first, done = pair_maps(meta, slots, own_maps, other_maps, query_done)
    pairs = [later(pair, seqs, d) for d in range(seqs // 2 - 1, 0, -1)]
    shard_query, free, out_done = block_outputs(query, keys, erased, entry, totals, done)
    kept_state, given_state = start_states(meta, slots, first, pairs, out_done)
    other_state = pair_swap(given_state, seqs)

    mixed = mixed_heads(
        meta, slots, kept_state, other_state, shard_query, free, head_gain.reshape(1, DK)
    )
    ups = []
    for own_mixed, own_tokens in zip(mixed, (tokens_a, tokens_b)):
        chip = attend(meta, slots, own_mixed, core_swap(own_mixed, n), w_out_t, other_w_out)
        own = [chip] + [y_shift(chip, n, d) for d in range(1, ys)]
        other = [core_swap(value, n) for value in own]
        ups.append(
            up_project(
                meta,
                slots,
                own_tokens,
                own,
                other,
                ffn_gain.reshape(1, features),
                w_up,
                part,
            )
        )
    (outer, middle_a, first_row, last_row), (inside, middle_b, _, _) = ups
    before = lax.ppermute(last_row, "seq", [(i, i + 1) for i in range(seqs - 1)])
    after = lax.ppermute(first_row, "seq", [(i + 1, i) for i in range(seqs - 1)])

    w_parts = w_down.T.reshape(n, part, hidden)
    far, act = down_project(
        meta, far_at, outer, inside, before, after, taps, w_parts, len(far_order)
    )
    near_give, total = rest_project(meta, near_at, act, middle_a, middle_b, w_parts)
    for d in range(1, ys):
        chip = (
            far[2 * d - 1].astype(f32) + core_swap(far[2 * d - 2], n).astype(f32)
        ).astype(bf16)
        total = total + y_shift(chip, n, d).astype(f32)
    total = total + core_swap(near_give, n).astype(f32)
    return total.astype(bf16).T


def solution(mesh):
    placed = (
        P("seq", "head"),
        P(),
        P(None, "head"),
        P(None, "head"),
        P(None, "head"),
        P(None, "head"),
        P(None, "head"),
        P(None, "head"),
        P(),
        P("head", None),
        P(),
        P(None, "head"),
        P(None, "head"),
        P("head", None),
    )
    return jax.shard_map(
        shards, mesh=mesh, in_specs=placed, out_specs=P("seq", "head"), check_vma=False
    )
```

```python
import functools

import jax
import jax.numpy as jnp
from jax import lax
from jax.experimental import pallas as pl
from jax.experimental.pallas import tpu as pltpu
from jax.sharding import PartitionSpec as P

DK = 128
BLOCK = 128
epsilon = 1e-06
f32 = jnp.float32
bf16 = jnp.bfloat16

PARITY, CORE, ME, CHIP = 0, 1, 2, 3

VM = pl.BlockSpec(memory_space=pltpu.VMEM)
SM = pl.BlockSpec(memory_space=pltpu.SMEM)
ANY = pl.BlockSpec(memory_space=pl.ANY)


def params(mebibytes):
    return pltpu.CompilerParams(vmem_limit_bytes=mebibytes * 1024 * 1024)


def cost(flops, moved):
    return pl.CostEstimate(flops=flops, bytes_accessed=moved, transcendentals=0)


def shape_of(shape, dtype=bf16):
    return jax.ShapeDtypeStruct(shape, dtype)


def dot(a, b):
    return jnp.dot(a, b, preferred_element_type=f32)


def dot_nt(a, b):
    return lax.dot_general(a, b, (((1,), (1,)), ((), ())), preferred_element_type=f32)


def dot_tn(a, b):
    return lax.dot_general(a, b, (((0,), (0,)), ((), ())), preferred_element_type=f32)


def iotas(shape):
    return lax.broadcasted_iota(jnp.int32, shape, 0), lax.broadcasted_iota(jnp.int32, shape, 1)


def column_of(row, lanes=128):
    return jnp.broadcast_to(row, (lanes, row.shape[1])).T


def scale_pass(source, gain_at, target):
    features, tokens = source.shape
    squares = jnp.zeros((8, tokens), f32)
    for start in range(0, features, 128):
        size = min(128, features - start)
        value = source[start : start + size, :].astype(f32)
        scale = column_of(gain_at(start, size))
        scale = jnp.concatenate([scale] * (tokens // 128), axis=1)
        target[:, start : start + size] = (value * scale).astype(bf16).T
        value = value * value
        for r in range(0, size, 8):
            squares = squares + value[r : r + 8]
    return squares


def inverse_of(squares, features):
    return lax.rsqrt(jnp.sum(squares, axis=0, keepdims=True) / features + epsilon)


def fill_columns(row, target):
    for start in range(0, row.shape[1], 128):
        target[start : start + 128, :] = column_of(row[:, start : start + 128])


def doubled(tile):
    return jnp.concatenate([tile, tile], axis=1)


def slots_of(meta, n):
    return [meta[CORE], 1 - meta[CORE]] if n == 2 else [0]


def load_pair(meta, pieces, whole, sem):
    part = pieces[0].shape[0]
    copies = [
        pltpu.make_async_copy(
            piece, whole.at[pl.ds(pl.multiple_of(slot * part, 16), part)], sem.at[p]
        )
        for p, (piece, slot) in enumerate(zip(pieces, slots_of(meta, len(pieces))))
    ]
    for copy in copies:
        copy.start()
    for copy in copies:
        copy.wait()


def held_rows(meta, at, weights, held, sem):
    span = held.shape[1]
    rows = pl.ds(pl.multiple_of(meta[at] * span, 16), span)
    copies = [
        pltpu.make_async_copy(ref.at[rows], held.at[i], sem.at[i]) for i, ref in enumerate(weights)
    ]
    for copy in copies:
        copy.start()
    return copies


def early_kernel(count_in, at, meta, *refs):
    first = at == CHIP
    pieces = refs[:count_in]
    gain, gates, w_key, w_value, w_query, w_down = refs[count_in : count_in + 6]
    refs = refs[count_in + 6 :]
    before, refs = (None, refs) if first else (refs[:5], refs[5:])
    acc_k, acc_v, acc_q, acc_g, squares = refs[:5]
    partner_w, whole, scaled, held, held_sem, sem = refs[5:] if first else (None, *refs[5:])
    rows_copies = held_rows(meta, at, (w_key, w_value, w_query), held, held_sem)
    copies = [
        pltpu.make_async_copy(
            w_down.at[2 * y + 1 - meta[CORE]], partner_w.at[y], sem.at[count_in + y]
        )
        for y in range(partner_w.shape[0] if first else 0)
    ]
    for copy in copies:
        copy.start()
    load_pair(meta, pieces, whole, sem)
    sums = scale_pass(whole, lambda at, size: gain[:, at : at + size], scaled)
    gate = dot_nt(gates[...], scaled[...])
    squares[...] = sums if first else before[4][...] + sums
    acc_g[...] = gate if first else before[3][...] + gate
    for i, out in enumerate((acc_k, acc_v, acc_q)):
        rows_copies[i].wait()
        product = dot(scaled[...], held[i])
        out[...] = product if first else before[i][...] + product
    for copy in copies:
        copy.wait()


def early_project(meta, at, pieces, gain, gates, w_key, w_value, w_query, w_down, before):
    first = before is None
    blocks, part, hidden = w_down.shape
    ys = blocks // 2
    span = gain.shape[1]
    count = pieces[0].shape[1]
    inner = w_key.shape[1]
    return pl.pallas_call(
        functools.partial(early_kernel, len(pieces), at),
        out_shape=[shape_of((count, inner), f32)] * 3
        + [shape_of((16, count), f32), shape_of((8, count), f32)]
        + [shape_of((ys, part, hidden))] * first,
        in_specs=[SM] + [ANY] * len(pieces) + [VM] * 2 + [ANY] * 4 + [VM] * (0 if first else 5),
        out_specs=[VM] * (5 + first),
        scratch_shapes=[
            pltpu.VMEM((span, count), bf16),
            pltpu.VMEM((count, span), bf16),
            pltpu.VMEM((3, span, inner), bf16),
            pltpu.SemaphoreType.DMA((3,)),
            pltpu.SemaphoreType.DMA((len(pieces) + ys,)),
        ],
        compiler_params=params(24),
        cost_estimate=cost(3 * 10**9, 8 * 10**6),
        name="early_project",
    )(meta, *pieces, gain, gates, w_key, w_value, w_query, w_down, *(before or ()))


def maps_kernel(n, heads, at, meta, *refs):
    pieces = refs[:n]
    gain, rates, gates, w_key, w_value, acc_k, acc_v, acc_g, squares = refs[n : n + 9]
    scaled, scale_b, keys, erased, entry, own, sent, totals = refs[n + 9 : n + 17]
    whole, raw_k, raw_v, rows_at_head, total_b, beta_b, held, held_sem, sem = refs[n + 17 :]
    span, count = whole.shape
    blocks = count // BLOCK
    inner = heads * DK
    features = w_key.shape[0]
    parity = meta[PARITY]
    rows_copies = held_rows(meta, at, (w_key, w_value), held, held_sem)
    load_pair(meta, pieces, whole, sem)
    sums = scale_pass(whole, lambda at, size: gain[:, at : at + size], scaled)
    inverse = inverse_of(sums + squares[...], features)
    fill_columns(inverse, scale_b)

    pre = (acc_g[...] + dot_nt(gates[...], scaled[...])) * inverse
    soft = jnp.maximum(pre, 0.0) + jnp.log1p(jnp.exp(-jnp.abs(pre)))
    rate = jnp.concatenate([rates[...]] * (count // 128), axis=1)
    decay = -rate * soft
    beta = jax.nn.sigmoid(pre + rate)
    row_at, col_at = iotas((BLOCK, BLOCK))
    upper = (row_at <= col_at).astype(f32)
    rows_at_head[...] = jnp.zeros_like(rows_at_head)
    for c in range(blocks):
        tokens = slice(c * BLOCK, (c + 1) * BLOCK)
        total = jnp.dot(
            decay[:, tokens], upper, precision=lax.Precision.HIGHEST, preferred_element_type=f32
        )
        totals[c] = total
        rows_at_head[0:16, :] = total
        rows_at_head[16:32, :] = beta[:, tokens]
        columns = rows_at_head[...].T
        for h in range(heads):
            total_b[h, tokens, :] = jnp.broadcast_to(columns[:, h : h + 1], (BLOCK, DK))
            lane = 16 + heads + h
            beta_b[h, tokens, :] = jnp.broadcast_to(columns[:, lane : lane + 1], (BLOCK, DK))

    for copy in rows_copies:
        copy.wait()
    for start in range(0, inner, 256):
        cols = slice(start, start + 256)
        scale = doubled(scale_b[...])
        raw_k[:, cols] = ((acc_k[:, cols] + dot(scaled[...], held[0, :, cols])) * scale).astype(bf16)
        raw_v[:, cols] = ((acc_v[:, cols] + dot(scaled[...], held[1, :, cols])) * scale).astype(bf16)

    xor = jnp.where(row_at > col_at, row_at ^ col_at, 0)
    eye = jnp.where(row_at == col_at, 1.0, 0.0)
    group = 2 if heads % 2 == 0 else 1

    @pl.loop(0, heads // group)
    def _(batch):
        lows, solved = [], []
        chains = []
        for g in range(group):
            h = batch * group + g
            cols = pl.ds(pl.multiple_of(h * DK, DK), DK)
            wide = pl.ds(pl.multiple_of(h * 2 * DK, 2 * DK), 2 * DK)
            raw = raw_k[:, cols].astype(f32)
            unit = raw * lax.rsqrt(jnp.sum(raw * raw, axis=1, keepdims=True) + epsilon)
            keys[:, cols] = unit.astype(bf16)
            for c in range(blocks):
                chains.append((h, cols, wide, c, slice(c * BLOCK, (c + 1) * BLOCK)))
        for h, cols, wide, c, rows in chains:
            k = keys[rows, cols]
            fade = jnp.exp(jnp.minimum(total_b[h, rows, :] - totals[c, pl.ds(h, 1), :], 0.0))
            low = jnp.where(xor > 0, beta_b[h, rows, :] * fade * dot_nt(k, k), 0.0)
            lows.append(low)
            solved.append(eye - jnp.where(xor == 1, low, 0.0))
        size = 2
        while size < BLOCK:
            mask = (xor >= size) & (xor < 2 * size)
            first = []
            for i in range(len(chains)):
                link = jnp.where(mask, lows[i], 0.0).astype(bf16)
                first.append(dot(link, solved[i].astype(bf16)).astype(bf16))
            solved = [
                solved[i] - dot(solved[i].astype(bf16), first[i]) for i in range(len(chains))
            ]
            size *= 2
        grown = []
        for i, (h, cols, wide, c, rows) in enumerate(chains):
            k = keys[rows, cols].astype(f32)
            t_col = total_b[h, rows, :]
            b_col = beta_b[h, rows, :]
            right = jnp.concatenate(
                [
                    (b_col * jnp.exp(t_col) * k).astype(bf16),
                    (b_col * raw_v[rows, cols].astype(f32)).astype(bf16),
                ],
                axis=1,
            )
            both = dot(solved[i].astype(bf16), right).astype(bf16)
            erased[rows, wide] = both
            t_end = t_col[BLOCK - 1 : BLOCK, :]
            faded = (jnp.exp(t_end - t_col) * k).astype(bf16)
            grown.append((jnp.exp(t_end), dot_tn(faded, both)))
        states = [None] * group
        for c in range(blocks):
            for g in range(group):
                h, cols, wide = chains[g * blocks][:3]
                end, product = grown[g * blocks + c]
                erase, write = product[:, :DK], product[:, DK:]
                if c == 0:
                    state = jnp.concatenate([end * eye - erase, write], axis=1)
                else:
                    step = dot(erase.astype(bf16), states[g].astype(bf16))
                    state = (
                        jnp.concatenate([end, end], axis=1) * states[g]
                        - step
                        + jnp.concatenate([jnp.zeros_like(write), write], axis=1)
                    )
                if c < blocks - 1:
                    entry[c, :, wide] = state.astype(bf16)
                states[g] = state
        for g in range(group):
            h = batch * group + g
            half = heads // 2
            mine = (h >= half) == (parity == 1)
            slot = lax.rem(h, half)

            @pl.when(mine)
            def _():
                own[slot] = states[g].astype(bf16)

            @pl.when(jnp.logical_not(mine))
            def _():
                sent[slot] = states[g].astype(bf16)


def block_maps(meta, at, pieces, gain, rates, gates, w_key, w_value, early):
    n = len(pieces)
    acc_k, acc_v, acc_q, acc_g, squares = early
    count = pieces[0].shape[1]
    span = gain.shape[1]
    inner = w_key.shape[1]
    heads = inner // DK
    blocks = count // BLOCK
    return pl.pallas_call(
        functools.partial(maps_kernel, n, heads, at),
        out_shape=(
            shape_of((count, span)),
            shape_of((count, DK), f32),
            shape_of((count, inner)),
            shape_of((count, 2 * inner)),
            shape_of((blocks - 1, DK, 2 * inner)),
            shape_of((heads // 2, DK, 2 * DK)),
            shape_of((heads // 2, DK, 2 * DK)),
            shape_of((blocks, 16, 128), f32),
        ),
        in_specs=[SM] + [ANY] * n + [VM] * 3 + [ANY] * 2 + [VM] * 4,
        out_specs=[VM] * 8,
        scratch_shapes=[
            pltpu.VMEM((span, count), bf16),
            pltpu.VMEM((count, inner), bf16),
            pltpu.VMEM((count, inner), bf16),
            pltpu.VMEM((128, BLOCK), f32),
            pltpu.VMEM((heads, count, DK), f32),
            pltpu.VMEM((heads, count, DK), f32),
            pltpu.VMEM((2, span, inner), bf16),
            pltpu.SemaphoreType.DMA((2,)),
            pltpu.SemaphoreType.DMA((n,)),
        ],
        compiler_params=params(24),
        cost_estimate=cost(10 * 10**9, 14 * 10**6),
        name="block_maps",
    )(meta, *pieces, gain, rates, gates, w_key, w_value, acc_k, acc_v, acc_g, squares)


def query_kernel(n, ys, meta, scaled, scale_b, weights, acc, *refs):
    pieces, (query, tokens_a, tokens_b, done, held, sem) = refs[: n * ys], refs[n * ys :]
    (copy,) = held_rows(meta, CHIP + ys - 1, (weights,), held, sem)
    span = scaled.shape[1]
    part, count = pieces[0].shape
    for d in range(ys):
        for p, slot in enumerate(slots_of(meta, n)):
            piece = pieces[d * n + p]
            base = meta[CHIP + d] * span + slot * part
            step = part // 7

            @pl.loop(0, 7)
            def _(r):
                rows = pl.ds(pl.multiple_of(r * step, 8), step)
                target = pl.ds(pl.multiple_of(base + r * step, 8), step)
                tokens_a[target, :BLOCK] = piece[rows, :BLOCK]
                tokens_a[target, BLOCK:] = piece[rows, count - BLOCK :]
                tokens_b[target, :] = piece[rows, BLOCK : count - BLOCK]

    done[...] = jnp.zeros_like(done)
    copy.wait()
    for start in range(0, query.shape[1], 256):
        cols = slice(start, start + 256)
        product = acc[:, cols] + dot(scaled[...], held[0, :, cols])
        query[:, cols] = (product * doubled(scale_b[...])).astype(bf16)


def queries(meta, ys, scaled, scale_b, weights, acc, pieces):
    n = len(pieces) // ys
    features = weights.shape[0]
    count = acc.shape[0]
    return pl.pallas_call(
        functools.partial(query_kernel, n, ys),
        out_shape=(
            shape_of(acc.shape),
            shape_of((features, 2 * BLOCK)),
            shape_of((features, count - 2 * BLOCK)),
            shape_of((8, 128), f32),
        ),
        in_specs=[SM] + [VM] * 2 + [ANY] + [VM] * (1 + len(pieces)),
        out_specs=[VM] * 4,
        scratch_shapes=[
            pltpu.VMEM((1, scaled.shape[1], acc.shape[1]), bf16),
            pltpu.SemaphoreType.DMA((1,)),
        ],
        compiler_params=params(16),
        cost_estimate=cost(10**9, 8 * 10**6),
        name="queries",
    )(meta, scaled, scale_b, weights, acc, *pieces)


def outputs_kernel(heads, query, keys, erased, entry, totals, after, shard_query, free, done, rows_at_head):
    count = query.shape[0]
    blocks = count // BLOCK
    row_at, col_at = iotas((BLOCK, BLOCK))
    done[...] = jnp.zeros_like(done)
    rows_at_head[...] = jnp.zeros_like(rows_at_head)
    for c in range(blocks):
        rows = slice(c * BLOCK, (c + 1) * BLOCK)
        rows_at_head[0:16, :] = totals[c]
        columns = rows_at_head[...].T
        for h in range(heads):
            cols = slice(h * DK, (h + 1) * DK)
            wide = slice(h * 2 * DK, (h + 1) * 2 * DK)
            t_col = jnp.broadcast_to(columns[:, h : h + 1], (BLOCK, BLOCK))
            t_row = totals[c, h : h + 1, :]
            fade = jnp.where(row_at >= col_at, jnp.exp(jnp.minimum(t_col - t_row, 0.0)), 0.0)
            q = query[rows, cols]
            scores = (fade * dot_nt(q, keys[rows, cols])).astype(bf16)
            both = dot(scores, erased[rows, wide])
            reach = jnp.exp(t_col) * q.astype(f32) - both[:, :DK]
            local = both[:, DK:]
            if c > 0:
                product = dot(reach.astype(bf16), entry[c - 1, :, wide])
                reach = product[:, :DK]
                local = local + product[:, DK:]
            shard_query[rows, cols] = reach.astype(bf16)
            free[rows, cols] = local


def block_outputs(query, keys, erased, entry, totals, after):
    heads = query.shape[1] // DK
    return pl.pallas_call(
        functools.partial(outputs_kernel, heads),
        out_shape=(shape_of(query.shape), shape_of(query.shape, f32), shape_of((8, 128), f32)),
        in_specs=[VM] * 5 + [ANY],
        out_specs=[VM] * 3,
        scratch_shapes=[pltpu.VMEM((128, BLOCK), f32)],
        compiler_params=params(16),
        cost_estimate=cost(3 * 10**9, 4 * 10**6),
        name="block_outputs",
    )(query, keys, erased, entry, totals, after)


def pair_kernel(meta, own, other, after, pair, first, done):
    even = meta[PARITY] == 0
    for h in range(own.shape[0]):
        mine, theirs = own[h], other[h]
        early = jnp.where(even, mine, theirs)
        late = jnp.where(even, theirs, mine)
        product = dot(late[:, :DK], early)
        shift = late[:, DK:].astype(f32)
        pair[h] = (product + jnp.concatenate([jnp.zeros_like(shift), shift], axis=1)).astype(bf16)
        first[h] = early
    done[...] = jnp.zeros_like(done)


def pair_maps(meta, own, other, after):
    return pl.pallas_call(
        pair_kernel,
        out_shape=(shape_of(own.shape), shape_of(own.shape), shape_of((8, 128), f32)),
        in_specs=[SM, VM, VM, ANY],
        out_specs=[VM] * 3,
        compiler_params=params(8),
        name="pair_maps",
    )(meta, own, other, after)


def apply_map(whole, state):
    high = state.astype(bf16)
    low = (state - high.astype(f32)).astype(bf16)
    product = dot(whole[:, :DK], jnp.concatenate([high, low], axis=1))
    return product[:, :DK] + product[:, DK:] + whole[:, DK:].astype(f32)


def start_kernel(steps, meta, first, *refs):
    pairs, (after, keep, give) = refs[:steps], refs[steps:]
    even = meta[PARITY] == 0
    for h in range(first.shape[0]):
        state = pairs[0][h][:, DK:].astype(f32)
        for pair in pairs[1:]:
            state = apply_map(pair[h], state)
        later = apply_map(first[h], state)
        keep[h] = jnp.where(even, state, later).astype(bf16)
        give[h] = jnp.where(even, later, state).astype(bf16)


def start_states(meta, first, pairs, after):
    heads = first.shape[0]
    shape = shape_of((heads, DK, DK))
    return pl.pallas_call(
        functools.partial(start_kernel, len(pairs)),
        out_shape=(shape, shape),
        in_specs=[SM] + [VM] * (1 + len(pairs)) + [ANY],
        out_specs=[VM] * 2,
        compiler_params=params(8),
        name="start_states",
    )(meta, first, *pairs, after)


def mixed_kernel(heads, meta, own, other, shard_query, free, gain, mixed_a, mixed_b):
    even = meta[PARITY] == 0
    half = heads // 2
    blocks = shard_query.shape[0] // BLOCK
    for h in range(heads):
        cols = slice(h * DK, (h + 1) * DK)
        if h < half:
            state = jnp.where(even, own[h], other[h])
        else:
            state = jnp.where(even, other[h - half], own[h - half])
        for unit in range(blocks):
            rows = slice(unit * BLOCK, (unit + 1) * BLOCK)
            out = dot(shard_query[rows, cols], state) + free[rows, cols]
            scale = lax.rsqrt(jnp.mean(out * out, axis=1, keepdims=True) + epsilon)
            value = (out * scale * gain[...].astype(f32)).astype(bf16)
            if unit == 0:
                mixed_a[:BLOCK, cols] = value
            elif unit == blocks - 1:
                mixed_a[BLOCK:, cols] = value
            else:
                mixed_b[(unit - 1) * BLOCK : unit * BLOCK, cols] = value


def mixed_heads(meta, own, other, shard_query, free, gain):
    count, inner = shard_query.shape
    return pl.pallas_call(
        functools.partial(mixed_kernel, inner // DK),
        out_shape=(shape_of((2 * BLOCK, inner)), shape_of((count - 2 * BLOCK, inner))),
        in_specs=[SM] + [VM] * 5,
        out_specs=[VM] * 2,
        compiler_params=params(12),
        cost_estimate=cost(10**9, 3 * 10**6),
        name="mixed_heads",
    )(meta, own, other, shard_query, free, gain)


def attend_kernel(meta, own, other, weights, other_weights, chip):
    rows = pl.ds(pl.multiple_of(meta[CORE] * chip.shape[0], 16), chip.shape[0])
    total = dot_nt(weights[rows, :], own[...]) + dot_nt(other_weights[rows, :], other[...])
    chip[...] = total.astype(bf16)


def attend(meta, own, other, weights, other_weights):
    return pl.pallas_call(
        attend_kernel,
        out_shape=shape_of((weights.shape[0] // 2, own.shape[0])),
        in_specs=[SM] + [VM] * 4,
        out_specs=VM,
        compiler_params=params(16),
        cost_estimate=cost(10**9, 5 * 10**6),
        name="attend",
    )(meta, own, other, weights, other_weights)


def up_kernel(adds, meta, tokens, *refs):
    own, other = refs[:adds], refs[adds : 2 * adds]
    gain, weights, lifted, middle_part, first, last, middle, hidden, scale_b = refs[2 * adds :]
    features, count = middle.shape
    half = features // 2
    step = 160
    for side, parts in ((meta[CORE], own), (1 - meta[CORE], other)):

        @pl.loop(0, half // step)
        def _(r):
            rows = pl.ds(pl.multiple_of(r * step, 32), step)
            target = pl.ds(pl.multiple_of(side * half + r * step, 32), step)
            total = tokens[target, :].astype(f32)
            for ref in parts:
                total = total + ref[rows, :].astype(f32)
            middle[target, :] = total.astype(bf16).astype(f32)

    squares = scale_pass(middle, lambda at, size: gain[:, at : at + size], hidden)
    fill_columns(inverse_of(squares, features), scale_b)
    part = middle_part.shape[0]
    middle_part[...] = middle[pl.ds(pl.multiple_of(meta[ME] * part, 8), part), :]
    width = lifted.shape[1]
    for start in range(0, width, 256):
        size = min(256, width - start)
        cols = slice(start, start + size)
        scale = doubled(scale_b[...])[:, :size]
        lifted[:, cols] = (dot(hidden[...], weights[:, cols]) * scale).astype(bf16)
    first[...] = lifted[0:1, :]
    last[...] = lifted[count - 1 : count, :]


def up_project(meta, tokens, own, other, gain, weights, part):
    features, hidden = weights.shape
    count = tokens.shape[1]
    return pl.pallas_call(
        functools.partial(up_kernel, len(own)),
        out_shape=(
            shape_of((count, hidden)),
            shape_of((part, count), f32),
            shape_of((1, hidden)),
            shape_of((1, hidden)),
        ),
        in_specs=[SM] + [VM] * (3 + 2 * len(own)),
        out_specs=[VM] * 4,
        scratch_shapes=[
            pltpu.VMEM((features, count), f32),
            pltpu.VMEM((count, features), bf16),
            pltpu.VMEM((count, DK), f32),
        ],
        compiler_params=params(20),
        cost_estimate=cost(2 * 10**9, 8 * 10**6),
        name="up_project",
    )(meta, tokens, *own, *other, gain, weights)


def gelu_of(x):
    inner = 0.7978845608028654 * (x + 0.044715 * (x * x * x))
    return 0.5 * x * (1.0 + jnp.tanh(inner))


def act_kernel(late, meta, outer, inside, before, after, taps, act_t, padded, act):
    count = act.shape[0]
    if late:
        padded[7:8, :] = inside[BLOCK - 1 : BLOCK, :].astype(f32)
        padded[8 : 8 + BLOCK, :] = inside[BLOCK:, :].astype(f32)
        padded[8 + BLOCK : 8 + count, :] = outer[BLOCK:, :].astype(f32)
        padded[8 + count : 9 + count, :] = after[...].astype(f32)
    else:
        padded[7:8, :] = before[...].astype(f32)
        padded[8 : 8 + BLOCK, :] = outer[:BLOCK, :].astype(f32)
        padded[8 + BLOCK : 8 + count, :] = inside[:BLOCK, :].astype(f32)
        padded[8 + count : 9 + count, :] = inside[BLOCK : BLOCK + 1, :].astype(f32)

    @pl.loop(0, count // 32)
    def _(r):
        base = pl.multiple_of(r * 32, 32)
        window = padded[pl.ds(base, 48), :]
        value = (
            taps[0:1, :] * window[7:39, :]
            + taps[1:2, :] * window[8:40, :]
            + taps[2:3, :] * window[9:41, :]
        )
        act[pl.ds(base, 32), :] = gelu_of(value).astype(bf16)

    act_t[...] = act[...].T


def activate(meta, outer, inside, before, after, taps, late):
    hidden = outer.shape[1]
    count = (outer.shape[0] + inside.shape[0]) // 2
    return pl.pallas_call(
        functools.partial(act_kernel, late),
        out_shape=shape_of((hidden, count)),
        in_specs=[SM] + [VM] * 5,
        out_specs=VM,
        scratch_shapes=[pltpu.VMEM((count + 16, hidden), f32), pltpu.VMEM((count, hidden), bf16)],
        compiler_params=params(12),
        cost_estimate=cost(10**9, 2 * 10**6),
        name="activate",
    )(meta, outer, inside, before, after, taps)


def far_kernel(ys, meta, own, other, weights, other_weights, *outs):
    for i, out in enumerate(outs):
        chip = meta[CHIP + ys + i]
        block = 2 * chip + meta[CORE]
        total = dot(weights[block], own[...]) + dot(other_weights[chip], other[...])
        out[...] = total.astype(bf16)


def far_project(meta, ys, own, other, weights, other_weights):
    part = weights.shape[1]
    return pl.pallas_call(
        functools.partial(far_kernel, ys),
        out_shape=[shape_of((part, own.shape[1]))] * (ys - 1),
        in_specs=[SM] + [VM] * 4,
        out_specs=[VM] * (ys - 1),
        compiler_params=params(16),
        cost_estimate=cost(10**9, 4 * 10**6),
        name="far_project",
    )(meta, own, other, weights, other_weights)


def near_kernel(meta, own_a, other_a, own_b, other_b, middle_a, middle_b, weights, other_weights, after, base):
    size = own_a.shape[1]
    middle = (
        jnp.concatenate([middle_a[:, :BLOCK], middle_b[:, :BLOCK]], axis=1),
        jnp.concatenate([middle_b[:, BLOCK:], middle_a[:, BLOCK:]], axis=1),
    )
    for i, (own, other) in enumerate(((own_a, other_a), (own_b, other_b))):
        total = dot(weights[meta[ME]], own[...])
        total = total + dot(other_weights[meta[CHIP]], other[...])
        base[:, i * size : (i + 1) * size] = total + middle[i]


def near_project(meta, own, other, middle_a, middle_b, weights, other_weights, after):
    part = weights.shape[1]
    return pl.pallas_call(
        near_kernel,
        out_shape=shape_of((part, 2 * own[0].shape[1]), f32),
        in_specs=[SM] + [VM] * 8 + [ANY],
        out_specs=VM,
        compiler_params=params(20),
        cost_estimate=cost(2 * 10**9, 6 * 10**6),
        name="near_project",
    )(meta, own[0], other[0], own[1], other[1], middle_a, middle_b, weights, other_weights, after)


def core_swap(value, n):
    return lax.ppermute(value, "head", [(i, i ^ 1) for i in range(n)])


def y_shift(value, n, step):
    return lax.ppermute(value, "head", [(i, (i + 2 * step) % n) for i in range(n)])


def pair_swap(value, n):
    return lax.ppermute(value, "seq", [(i, i ^ 1) for i in range(n)])


def later(value, n, step):
    return lax.ppermute(value, "seq", [(i, i + 2 * step) for i in range(n - 2 * step)])


def shards(
    tokens,
    norm_gain,
    w_query,
    w_key,
    w_value,
    w_decay,
    w_beta,
    head_rates,
    head_gain,
    w_out,
    ffn_gain,
    w_up,
    conv_taps,
    w_down,
):
    n = lax.axis_size("head")
    seqs = lax.axis_size("seq")
    me = lax.axis_index("head")
    at = lax.axis_index("seq")
    core = me % 2
    parity = at % 2
    ys = n // 2
    count, part = tokens.shape
    heads = w_query.shape[1] // DK
    hidden = w_up.shape[1]
    features = n * part

    mine = tokens.T
    shifted = [mine] + [y_shift(mine, n, d) for d in range(1, ys)]

    def group_of(piece):
        partner = core_swap(piece, n)
        if part % 16:
            first = jnp.where(core == 0, piece, partner)
            second = jnp.where(core == 0, partner, piece)
            return [jnp.concatenate([first, second], axis=0)]
        return [piece, partner]

    groups = [group_of(mine)]
    chip = me // 2
    here = [parity, core, me]
    sources = [(chip + ys - d) % ys for d in range(ys)]
    targets = [(chip + d) % ys for d in range(1, ys)]
    meta = jnp.stack(here + sources + targets).astype(jnp.int32)

    w_out_t = w_out.T
    w_parts = w_down.T.reshape(n, part, hidden)

    gates = jnp.concatenate([w_decay.T, w_beta.T], axis=0)
    gates = jnp.pad(gates, ((0, 16 - 2 * heads), (0, 0)))
    gates = gates.reshape(16, ys, 2 * part).transpose(1, 0, 2)
    rates = jnp.pad(head_rates.reshape(2 * heads, 1), ((0, 16 - 2 * heads), (0, 0)))
    rates = jnp.broadcast_to(rates, (16, 128))
    gain = norm_gain.astype(f32).reshape(ys, 1, 2 * part)

    def ours(rows, d):
        return lax.dynamic_index_in_dim(rows, sources[d], 0, False)

    ffn_scale = ffn_gain.astype(f32).reshape(1, features)
    taps = conv_taps.astype(f32)

    early = None
    for d in range(ys - 1):
        early = early_project(
            meta, CHIP + d, groups[d], ours(gain, d), ours(gates, d), w_key, w_value, w_query, w_parts, early
        )
        if d == 0:
            sent_w_down, early = early[5], early[:5]
        piece, _ = lax.optimization_barrier((shifted[d + 1], early[4]))
        groups.append(group_of(piece))
    scaled, scale_b, keys, erased, entry, own_maps, sent_maps, totals = block_maps(
        meta, CHIP + ys - 1, groups[-1], ours(gain, -1), rates, ours(gates, -1), w_key, w_value, early
    )

    sent_w_out, sent_w_down, _ = lax.optimization_barrier((w_out_t, sent_w_down, groups[-1][-1]))
    other_w_out, other_w_down = core_swap(sent_w_out, n), core_swap(sent_w_down, n)
    acc_query, other_w_out, other_w_down = lax.optimization_barrier(
        (early[2], other_w_out, other_w_down)
    )

    other_maps = pair_swap(sent_maps, seqs)
    query, tokens_a, tokens_b, query_done = queries(
        meta, ys, scaled, scale_b, w_query, acc_query, sum(groups, [])
    )
    pair, first, done = pair_maps(meta, own_maps, other_maps, query_done)
    pairs = [later(pair, seqs, d) for d in range(seqs // 2 - 1, 0, -1)]
    shard_query, free, out_done = block_outputs(query, keys, erased, entry, totals, done)
    kept_state, given_state = start_states(meta, first, pairs, out_done)
    other_state = pair_swap(given_state, seqs)

    mixed = mixed_heads(meta, kept_state, other_state, shard_query, free, head_gain.reshape(1, DK))
    sums = []
    for own_mixed in mixed:
        summed = attend(meta, own_mixed, core_swap(own_mixed, n), w_out_t, other_w_out)
        sums.append([summed] + [y_shift(summed, n, d) for d in range(1, ys)])
    ups = []
    for own, own_tokens in zip(sums, (tokens_a, tokens_b)):
        ahead = ups[0][2] if ups else sums[1][0]
        own = own[:1] + list(lax.optimization_barrier((tuple(own[1:]), ahead))[0])
        other = [core_swap(value, n) for value in own]
        ups.append(up_project(meta, own_tokens, own, other, ffn_scale, w_up, part))
    (outer, middle_a, first_row, last_row), (inside, middle_b, _, _) = ups
    before = lax.ppermute(last_row, "seq", [(i, i + 1) for i in range(seqs - 1)])
    after = lax.ppermute(first_row, "seq", [(i + 1, i) for i in range(seqs - 1)])

    acts = [activate(meta, outer, inside, before, after, taps, late) for late in (False, True)]
    partner_acts = [core_swap(act, n) for act in acts]
    fars = [
        far_project(meta, ys, act, partner, w_parts, other_w_down)
        for act, partner in zip(acts, partner_acts)
    ]
    total = near_project(
        meta, acts, partner_acts, middle_a, middle_b, w_parts, other_w_down, fars[1][0]
    )
    for d in range(1, ys):
        halves = [y_shift(far[d - 1], n, d) for far in fars]
        total = total + jnp.concatenate(halves, axis=1).astype(f32)
    return total.astype(bf16).T


def solution(mesh):
    placed = (
        P("seq", "head"),
        P(),
        P(None, "head"),
        P(None, "head"),
        P(None, "head"),
        P(None, "head"),
        P(None, "head"),
        P(None, "head"),
        P(),
        P("head", None),
        P(),
        P(None, "head"),
        P(None, "head"),
        P("head", None),
    )
    return jax.shard_map(
        shards, mesh=mesh, in_specs=placed, out_specs=P("seq", "head"), check_vma=False
    )
```

```python
import functools

import jax
import jax.numpy as jnp
from jax import lax
from jax.experimental import pallas as pl
from jax.experimental.pallas import tpu as pltpu
from jax.sharding import PartitionSpec as P

DK = 128
BLOCK = 128
epsilon = 1e-06
f32 = jnp.float32
bf16 = jnp.bfloat16

PARITY, CORE, ME, CHIP = 0, 1, 2, 3

VM = pl.BlockSpec(memory_space=pltpu.VMEM)
SM = pl.BlockSpec(memory_space=pltpu.SMEM)
ANY = pl.BlockSpec(memory_space=pl.ANY)


def params(mebibytes):
    return pltpu.CompilerParams(vmem_limit_bytes=mebibytes * 1024 * 1024)


def cost(flops, moved):
    return pl.CostEstimate(flops=flops, bytes_accessed=moved, transcendentals=0)


def shape_of(shape, dtype=bf16):
    return jax.ShapeDtypeStruct(shape, dtype)


def dot(a, b):
    return jnp.dot(a, b, preferred_element_type=f32)


def dot_nt(a, b):
    return lax.dot_general(a, b, (((1,), (1,)), ((), ())), preferred_element_type=f32)


def dot_tn(a, b):
    return lax.dot_general(a, b, (((0,), (0,)), ((), ())), preferred_element_type=f32)


def iotas(shape):
    return lax.broadcasted_iota(jnp.int32, shape, 0), lax.broadcasted_iota(jnp.int32, shape, 1)


def column_of(row, lanes=128):
    return jnp.broadcast_to(row, (lanes, row.shape[1])).T


def scale_pass(source, gain_at, target):
    features, tokens = source.shape
    squares = jnp.zeros((8, tokens), f32)
    for start in range(0, features, 128):
        size = min(128, features - start)
        value = source[start : start + size, :].astype(f32)
        scale = column_of(gain_at(start, size))
        scale = jnp.concatenate([scale] * (tokens // 128), axis=1)
        target[:, start : start + size] = (value * scale).astype(bf16).T
        value = value * value
        for r in range(0, size, 8):
            squares = squares + value[r : r + 8]
    return squares


def inverse_of(squares, features):
    return lax.rsqrt(jnp.sum(squares, axis=0, keepdims=True) / features + epsilon)


def fill_columns(row, target):
    for start in range(0, row.shape[1], 128):
        target[start : start + 128, :] = column_of(row[:, start : start + 128])


def doubled(tile):
    return jnp.concatenate([tile, tile], axis=1)


def slots_of(meta, n):
    return [meta[CORE], 1 - meta[CORE]] if n == 2 else [0]


def load_pair(meta, pieces, whole, sem):
    part = pieces[0].shape[0]
    copies = [
        pltpu.make_async_copy(
            piece, whole.at[pl.ds(pl.multiple_of(slot * part, 16), part)], sem.at[p]
        )
        for p, (piece, slot) in enumerate(zip(pieces, slots_of(meta, len(pieces))))
    ]
    for copy in copies:
        copy.start()
    for copy in copies:
        copy.wait()


def held_rows(meta, at, weights, held, sem):
    span = held.shape[1]
    rows = pl.ds(pl.multiple_of(meta[at] * span, 16), span)
    copies = [
        pltpu.make_async_copy(ref.at[rows], held.at[i], sem.at[i]) for i, ref in enumerate(weights)
    ]
    for copy in copies:
        copy.start()
    return copies


def early_kernel(count_in, at, meta, *refs):
    first = at == CHIP
    pieces = refs[:count_in]
    gain, gates, w_key, w_value, w_query, w_down = refs[count_in : count_in + 6]
    refs = refs[count_in + 6 :]
    before, refs = (None, refs) if first else (refs[:5], refs[5:])
    acc_k, acc_v, acc_q, acc_g, squares = refs[:5]
    partner_w, whole, scaled, held, held_sem, sem = refs[5:] if first else (None, *refs[5:])
    rows_copies = held_rows(meta, at, (w_key, w_value, w_query), held, held_sem)
    copies = [
        pltpu.make_async_copy(
            w_down.at[2 * y + 1 - meta[CORE]], partner_w.at[y], sem.at[count_in + y]
        )
        for y in range(partner_w.shape[0] if first else 0)
    ]
    for copy in copies:
        copy.start()
    load_pair(meta, pieces, whole, sem)
    sums = scale_pass(whole, lambda at, size: gain[:, at : at + size], scaled)
    gate = dot_nt(gates[...], scaled[...])
    squares[...] = sums if first else before[4][...] + sums
    acc_g[...] = gate if first else before[3][...] + gate
    for i, out in enumerate((acc_k, acc_v, acc_q)):
        rows_copies[i].wait()
        product = dot(scaled[...], held[i])
        out[...] = product if first else before[i][...] + product
    for copy in copies:
        copy.wait()


def early_project(meta, at, pieces, gain, gates, w_key, w_value, w_query, w_down, before):
    first = before is None
    blocks, part, hidden = w_down.shape
    ys = blocks // 2
    span = gain.shape[1]
    count = pieces[0].shape[1]
    inner = w_key.shape[1]
    return pl.pallas_call(
        functools.partial(early_kernel, len(pieces), at),
        out_shape=[shape_of((count, inner), f32)] * 3
        + [shape_of((16, count), f32), shape_of((8, count), f32)]
        + [shape_of((ys, part, hidden))] * first,
        in_specs=[SM] + [ANY] * len(pieces) + [VM] * 2 + [ANY] * 4 + [VM] * (0 if first else 5),
        out_specs=[VM] * 5 + [ANY] * first,
        scratch_shapes=[
            pltpu.VMEM((span, count), bf16),
            pltpu.VMEM((count, span), bf16),
            pltpu.VMEM((3, span, inner), bf16),
            pltpu.SemaphoreType.DMA((3,)),
            pltpu.SemaphoreType.DMA((len(pieces) + ys,)),
        ],
        compiler_params=params(54),
        cost_estimate=cost(3 * 10**9, 8 * 10**6),
        name="early_project",
    )(meta, *pieces, gain, gates, w_key, w_value, w_query, w_down, *(before or ()))


def maps_kernel(n, heads, at, meta, *refs):
    pieces = refs[:n]
    gain, rates, gates, w_key, w_value, acc_k, acc_v, acc_g, squares = refs[n : n + 9]
    scaled, scale_b, keys, erased, entry, own, sent, totals = refs[n + 9 : n + 17]
    whole, raw_k, raw_v, rows_at_head, total_b, beta_b, held, held_sem, acc, acc_sem, sem = refs[
        n + 17 :
    ]
    span, count = whole.shape
    blocks = count // BLOCK
    inner = heads * DK
    features = w_key.shape[0]
    parity = meta[PARITY]
    rows_copies = held_rows(meta, at, (w_key, w_value), held, held_sem)
    rows_copies += [
        pltpu.make_async_copy(ref, acc.at[i], acc_sem.at[i]) for i, ref in enumerate((acc_k, acc_v))
    ]
    for copy in rows_copies[2:]:
        copy.start()
    load_pair(meta, pieces, whole, sem)
    sums = scale_pass(whole, lambda at, size: gain[:, at : at + size], scaled)
    inverse = inverse_of(sums + squares[...], features)
    fill_columns(inverse, scale_b)

    pre = (acc_g[...] + dot_nt(gates[...], scaled[...])) * inverse
    soft = jnp.maximum(pre, 0.0) + jnp.log1p(jnp.exp(-jnp.abs(pre)))
    rate = jnp.concatenate([rates[...]] * (count // 128), axis=1)
    decay = -rate * soft
    beta = jax.nn.sigmoid(pre + rate)
    row_at, col_at = iotas((BLOCK, BLOCK))
    upper = (row_at <= col_at).astype(f32)
    rows_at_head[...] = jnp.zeros_like(rows_at_head)
    for c in range(blocks):
        tokens = slice(c * BLOCK, (c + 1) * BLOCK)
        total = jnp.dot(
            decay[:, tokens], upper, precision=lax.Precision.HIGHEST, preferred_element_type=f32
        )
        totals[c] = total
        rows_at_head[0:16, :] = total
        rows_at_head[16:32, :] = beta[:, tokens]
        columns = rows_at_head[...].T
        for h in range(heads):
            total_b[h, tokens, :] = jnp.broadcast_to(columns[:, h : h + 1], (BLOCK, DK))
            lane = 16 + heads + h
            beta_b[h, tokens, :] = jnp.broadcast_to(columns[:, lane : lane + 1], (BLOCK, DK))

    for copy in rows_copies:
        copy.wait()
    for start in range(0, inner, 256):
        cols = slice(start, start + 256)
        scale = doubled(scale_b[...])
        raw_k[:, cols] = ((acc[0, :, cols] + dot(scaled[...], held[0, :, cols])) * scale).astype(bf16)
        raw_v[:, cols] = ((acc[1, :, cols] + dot(scaled[...], held[1, :, cols])) * scale).astype(bf16)

    xor = jnp.where(row_at > col_at, row_at ^ col_at, 0)
    eye = jnp.where(row_at == col_at, 1.0, 0.0)
    group = 2 if heads % 2 == 0 else 1

    @pl.loop(0, heads // group)
    def _(batch):
        lows, solved = [], []
        chains = []
        for g in range(group):
            h = batch * group + g
            cols = pl.ds(pl.multiple_of(h * DK, DK), DK)
            wide = pl.ds(pl.multiple_of(h * 2 * DK, 2 * DK), 2 * DK)
            raw = raw_k[:, cols].astype(f32)
            unit = raw * lax.rsqrt(jnp.sum(raw * raw, axis=1, keepdims=True) + epsilon)
            keys[:, cols] = unit.astype(bf16)
            for c in range(blocks):
                chains.append((h, cols, wide, c, slice(c * BLOCK, (c + 1) * BLOCK)))
        for h, cols, wide, c, rows in chains:
            k = keys[rows, cols]
            fade = jnp.exp(jnp.minimum(total_b[h, rows, :] - totals[c, pl.ds(h, 1), :], 0.0))
            low = jnp.where(xor > 0, beta_b[h, rows, :] * fade * dot_nt(k, k), 0.0)
            lows.append(low)
            solved.append(eye - jnp.where(xor == 1, low, 0.0))
        size = 2
        while size < BLOCK:
            mask = (xor >= size) & (xor < 2 * size)
            first = []
            for i in range(len(chains)):
                link = jnp.where(mask, lows[i], 0.0).astype(bf16)
                first.append(dot(link, solved[i].astype(bf16)).astype(bf16))
            solved = [
                solved[i] - dot(solved[i].astype(bf16), first[i]) for i in range(len(chains))
            ]
            size *= 2
        grown = []
        for i, (h, cols, wide, c, rows) in enumerate(chains):
            k = keys[rows, cols].astype(f32)
            t_col = total_b[h, rows, :]
            b_col = beta_b[h, rows, :]
            right = jnp.concatenate(
                [
                    (b_col * jnp.exp(t_col) * k).astype(bf16),
                    (b_col * raw_v[rows, cols].astype(f32)).astype(bf16),
                ],
                axis=1,
            )
            both = dot(solved[i].astype(bf16), right).astype(bf16)
            erased[rows, wide] = both
            t_end = t_col[BLOCK - 1 : BLOCK, :]
            faded = (jnp.exp(t_end - t_col) * k).astype(bf16)
            grown.append((jnp.exp(t_end), dot_tn(faded, both)))
        states = [None] * group
        for c in range(blocks):
            for g in range(group):
                h, cols, wide = chains[g * blocks][:3]
                end, product = grown[g * blocks + c]
                erase, write = product[:, :DK], product[:, DK:]
                if c == 0:
                    state = jnp.concatenate([end * eye - erase, write], axis=1)
                else:
                    step = dot(erase.astype(bf16), states[g].astype(bf16))
                    state = (
                        jnp.concatenate([end, end], axis=1) * states[g]
                        - step
                        + jnp.concatenate([jnp.zeros_like(write), write], axis=1)
                    )
                if c < blocks - 1:
                    entry[c, :, wide] = state.astype(bf16)
                states[g] = state
        for g in range(group):
            h = batch * group + g
            half = heads // 2
            mine = (h >= half) == (parity == 1)
            slot = lax.rem(h, half)

            @pl.when(mine)
            def _():
                own[slot] = states[g].astype(bf16)

            @pl.when(jnp.logical_not(mine))
            def _():
                sent[slot] = states[g].astype(bf16)


def block_maps(meta, at, pieces, gain, rates, gates, w_key, w_value, early):
    n = len(pieces)
    acc_k, acc_v, acc_q, acc_g, squares = early
    count = pieces[0].shape[1]
    span = gain.shape[1]
    inner = w_key.shape[1]
    heads = inner // DK
    blocks = count // BLOCK
    return pl.pallas_call(
        functools.partial(maps_kernel, n, heads, at),
        out_shape=(
            shape_of((count, span)),
            shape_of((count, DK), f32),
            shape_of((count, inner)),
            shape_of((count, 2 * inner)),
            shape_of((blocks - 1, DK, 2 * inner)),
            shape_of((heads // 2, DK, 2 * DK)),
            shape_of((heads // 2, DK, 2 * DK)),
            shape_of((blocks, 16, 128), f32),
        ),
        in_specs=[SM] + [ANY] * n + [VM] * 3 + [ANY] * 4 + [VM] * 2,
        out_specs=[VM] * 8,
        scratch_shapes=[
            pltpu.VMEM((span, count), bf16),
            pltpu.VMEM((count, inner), bf16),
            pltpu.VMEM((count, inner), bf16),
            pltpu.VMEM((128, BLOCK), f32),
            pltpu.VMEM((heads, count, DK), f32),
            pltpu.VMEM((heads, count, DK), f32),
            pltpu.VMEM((2, span, inner), bf16),
            pltpu.SemaphoreType.DMA((2,)),
            pltpu.VMEM((2, count, inner), f32),
            pltpu.SemaphoreType.DMA((2,)),
            pltpu.SemaphoreType.DMA((n,)),
        ],
        compiler_params=params(54),
        cost_estimate=cost(10 * 10**9, 14 * 10**6),
        name="block_maps",
    )(meta, *pieces, gain, rates, gates, w_key, w_value, acc_k, acc_v, acc_g, squares)


def query_kernel(n, ys, meta, scaled, scale_b, weights, acc, *refs):
    pieces, (query, tokens_a, tokens_b, done, held, sem) = refs[: n * ys], refs[n * ys :]
    (copy,) = held_rows(meta, CHIP + ys - 1, (weights,), held, sem)
    span = scaled.shape[1]
    part, count = pieces[0].shape
    for d in range(ys):
        for p, slot in enumerate(slots_of(meta, n)):
            piece = pieces[d * n + p]
            base = meta[CHIP + d] * span + slot * part
            step = part // 7

            @pl.loop(0, 7)
            def _(r):
                rows = pl.ds(pl.multiple_of(r * step, 8), step)
                target = pl.ds(pl.multiple_of(base + r * step, 8), step)
                tokens_a[target, :BLOCK] = piece[rows, :BLOCK]
                tokens_a[target, BLOCK:] = piece[rows, count - BLOCK :]
                tokens_b[target, :] = piece[rows, BLOCK : count - BLOCK]

    done[...] = jnp.zeros_like(done)
    copy.wait()
    for start in range(0, query.shape[1], 256):
        cols = slice(start, start + 256)
        product = acc[:, cols] + dot(scaled[...], held[0, :, cols])
        query[:, cols] = (product * doubled(scale_b[...])).astype(bf16)


def queries(meta, ys, scaled, scale_b, weights, acc, pieces):
    n = len(pieces) // ys
    features = weights.shape[0]
    count = acc.shape[0]
    return pl.pallas_call(
        functools.partial(query_kernel, n, ys),
        out_shape=(
            shape_of(acc.shape),
            shape_of((features, 2 * BLOCK)),
            shape_of((features, count - 2 * BLOCK)),
            shape_of((8, 128), f32),
        ),
        in_specs=[SM] + [VM] * 2 + [ANY] + [VM] * (1 + len(pieces)),
        out_specs=[VM] * 4,
        scratch_shapes=[
            pltpu.VMEM((1, scaled.shape[1], acc.shape[1]), bf16),
            pltpu.SemaphoreType.DMA((1,)),
        ],
        compiler_params=params(12),
        cost_estimate=cost(10**9, 8 * 10**6),
        name="queries",
    )(meta, scaled, scale_b, weights, acc, *pieces)


def outputs_kernel(heads, query, keys, erased, entry, totals, after, shard_query, free, done, rows_at_head):
    count = query.shape[0]
    blocks = count // BLOCK
    row_at, col_at = iotas((BLOCK, BLOCK))
    done[...] = jnp.zeros_like(done)
    rows_at_head[...] = jnp.zeros_like(rows_at_head)
    for c in range(blocks):
        rows = slice(c * BLOCK, (c + 1) * BLOCK)
        rows_at_head[0:16, :] = totals[c]
        columns = rows_at_head[...].T
        for h in range(heads):
            cols = slice(h * DK, (h + 1) * DK)
            wide = slice(h * 2 * DK, (h + 1) * 2 * DK)
            t_col = jnp.broadcast_to(columns[:, h : h + 1], (BLOCK, BLOCK))
            t_row = totals[c, h : h + 1, :]
            fade = jnp.where(row_at >= col_at, jnp.exp(jnp.minimum(t_col - t_row, 0.0)), 0.0)
            q = query[rows, cols]
            scores = (fade * dot_nt(q, keys[rows, cols])).astype(bf16)
            both = dot(scores, erased[rows, wide])
            reach = jnp.exp(t_col) * q.astype(f32) - both[:, :DK]
            local = both[:, DK:]
            if c > 0:
                product = dot(reach.astype(bf16), entry[c - 1, :, wide])
                reach = product[:, :DK]
                local = local + product[:, DK:]
            shard_query[rows, cols] = reach.astype(bf16)
            free[rows, cols] = local


def block_outputs(query, keys, erased, entry, totals, after):
    heads = query.shape[1] // DK
    return pl.pallas_call(
        functools.partial(outputs_kernel, heads),
        out_shape=(shape_of(query.shape), shape_of(query.shape, f32), shape_of((8, 128), f32)),
        in_specs=[VM] * 5 + [ANY],
        out_specs=[VM] * 3,
        scratch_shapes=[pltpu.VMEM((128, BLOCK), f32)],
        compiler_params=params(8),
        cost_estimate=cost(3 * 10**9, 4 * 10**6),
        name="block_outputs",
    )(query, keys, erased, entry, totals, after)


def pair_kernel(meta, own, other, after, pair, first, done):
    even = meta[PARITY] == 0
    for h in range(own.shape[0]):
        mine, theirs = own[h], other[h]
        early = jnp.where(even, mine, theirs)
        late = jnp.where(even, theirs, mine)
        product = dot(late[:, :DK], early)
        shift = late[:, DK:].astype(f32)
        pair[h] = (product + jnp.concatenate([jnp.zeros_like(shift), shift], axis=1)).astype(bf16)
        first[h] = early
    done[...] = jnp.zeros_like(done)


def pair_maps(meta, own, other, after):
    return pl.pallas_call(
        pair_kernel,
        out_shape=(shape_of(own.shape), shape_of(own.shape), shape_of((8, 128), f32)),
        in_specs=[SM, VM, VM, ANY],
        out_specs=[VM] * 3,
        compiler_params=params(4),
        name="pair_maps",
    )(meta, own, other, after)


def apply_map(whole, state):
    high = state.astype(bf16)
    low = (state - high.astype(f32)).astype(bf16)
    product = dot(whole[:, :DK], jnp.concatenate([high, low], axis=1))
    return product[:, :DK] + product[:, DK:] + whole[:, DK:].astype(f32)


def start_kernel(steps, meta, first, *refs):
    pairs, (after, keep, give) = refs[:steps], refs[steps:]
    even = meta[PARITY] == 0
    for h in range(first.shape[0]):
        state = pairs[0][h][:, DK:].astype(f32)
        for pair in pairs[1:]:
            state = apply_map(pair[h], state)
        later = apply_map(first[h], state)
        keep[h] = jnp.where(even, state, later).astype(bf16)
        give[h] = jnp.where(even, later, state).astype(bf16)


def start_states(meta, first, pairs, after):
    heads = first.shape[0]
    shape = shape_of((heads, DK, DK))
    return pl.pallas_call(
        functools.partial(start_kernel, len(pairs)),
        out_shape=(shape, shape),
        in_specs=[SM] + [VM] * (1 + len(pairs)) + [ANY],
        out_specs=[VM] * 2,
        compiler_params=params(4),
        name="start_states",
    )(meta, first, *pairs, after)


def mixed_kernel(heads, meta, own, other, shard_query, free, gain, mixed_a, mixed_b):
    even = meta[PARITY] == 0
    half = heads // 2
    blocks = shard_query.shape[0] // BLOCK
    for h in range(heads):
        cols = slice(h * DK, (h + 1) * DK)
        if h < half:
            state = jnp.where(even, own[h], other[h])
        else:
            state = jnp.where(even, other[h - half], own[h - half])
        for unit in range(blocks):
            rows = slice(unit * BLOCK, (unit + 1) * BLOCK)
            out = dot(shard_query[rows, cols], state) + free[rows, cols]
            scale = lax.rsqrt(jnp.mean(out * out, axis=1, keepdims=True) + epsilon)
            value = (out * scale * gain[...].astype(f32)).astype(bf16)
            if unit == 0:
                mixed_a[:BLOCK, cols] = value
            elif unit == blocks - 1:
                mixed_a[BLOCK:, cols] = value
            else:
                mixed_b[(unit - 1) * BLOCK : unit * BLOCK, cols] = value


def mixed_heads(meta, own, other, shard_query, free, gain):
    count, inner = shard_query.shape
    return pl.pallas_call(
        functools.partial(mixed_kernel, inner // DK),
        out_shape=(shape_of((2 * BLOCK, inner)), shape_of((count - 2 * BLOCK, inner))),
        in_specs=[SM] + [VM] * 5,
        out_specs=[VM] * 2,
        compiler_params=params(6),
        cost_estimate=cost(10**9, 3 * 10**6),
        name="mixed_heads",
    )(meta, own, other, shard_query, free, gain)


def attend_kernel(meta, own, other, weights, other_weights, chip):
    rows = pl.ds(pl.multiple_of(meta[CORE] * chip.shape[0], 16), chip.shape[0])
    total = dot_nt(weights[rows, :], own[...]) + dot_nt(other_weights[rows, :], other[...])
    chip[...] = total.astype(bf16)


def attend(meta, own, other, weights, other_weights):
    return pl.pallas_call(
        attend_kernel,
        out_shape=shape_of((weights.shape[0] // 2, own.shape[0])),
        in_specs=[SM] + [VM] * 4,
        out_specs=VM,
        compiler_params=params(10),
        cost_estimate=cost(10**9, 5 * 10**6),
        name="attend",
    )(meta, own, other, weights, other_weights)


def up_kernel(adds, meta, tokens, *refs):
    own, other = refs[:adds], refs[adds : 2 * adds]
    gain, weights, lifted, middle_part, first, last, middle, hidden, scale_b = refs[2 * adds :]
    features, count = middle.shape
    half = features // 2
    step = 160
    for side, parts in ((meta[CORE], own), (1 - meta[CORE], other)):

        @pl.loop(0, half // step)
        def _(r):
            rows = pl.ds(pl.multiple_of(r * step, 32), step)
            target = pl.ds(pl.multiple_of(side * half + r * step, 32), step)
            total = tokens[target, :].astype(f32)
            for ref in parts:
                total = total + ref[rows, :].astype(f32)
            middle[target, :] = total.astype(bf16).astype(f32)

    squares = scale_pass(middle, lambda at, size: gain[:, at : at + size], hidden)
    fill_columns(inverse_of(squares, features), scale_b)
    part = middle_part.shape[0]
    middle_part[...] = middle[pl.ds(pl.multiple_of(meta[ME] * part, 8), part), :]
    width = lifted.shape[1]
    for start in range(0, width, 256):
        size = min(256, width - start)
        cols = slice(start, start + size)
        scale = doubled(scale_b[...])[:, :size]
        lifted[:, cols] = (dot(hidden[...], weights[:, cols]) * scale).astype(bf16)
    first[...] = lifted[0:1, :]
    last[...] = lifted[count - 1 : count, :]


def up_project(meta, tokens, own, other, gain, weights, part):
    features, hidden = weights.shape
    count = tokens.shape[1]
    return pl.pallas_call(
        functools.partial(up_kernel, len(own)),
        out_shape=(
            shape_of((count, hidden)),
            shape_of((part, count), f32),
            shape_of((1, hidden)),
            shape_of((1, hidden)),
        ),
        in_specs=[SM] + [VM] * (3 + 2 * len(own)),
        out_specs=[VM] * 4,
        scratch_shapes=[
            pltpu.VMEM((features, count), f32),
            pltpu.VMEM((count, features), bf16),
            pltpu.VMEM((count, DK), f32),
        ],
        compiler_params=params(16),
        cost_estimate=cost(2 * 10**9, 8 * 10**6),
        name="up_project",
    )(meta, tokens, *own, *other, gain, weights)


def gelu_of(x):
    inner = 0.7978845608028654 * (x + 0.044715 * (x * x * x))
    return 0.5 * x * (1.0 + jnp.tanh(inner))


def act_kernel(late, meta, outer, inside, before, after, taps, act_t, padded, act):
    count = act.shape[0]
    if late:
        padded[7:8, :] = inside[BLOCK - 1 : BLOCK, :].astype(f32)
        padded[8 : 8 + BLOCK, :] = inside[BLOCK:, :].astype(f32)
        padded[8 + BLOCK : 8 + count, :] = outer[BLOCK:, :].astype(f32)
        padded[8 + count : 9 + count, :] = after[...].astype(f32)
    else:
        padded[7:8, :] = before[...].astype(f32)
        padded[8 : 8 + BLOCK, :] = outer[:BLOCK, :].astype(f32)
        padded[8 + BLOCK : 8 + count, :] = inside[:BLOCK, :].astype(f32)
        padded[8 + count : 9 + count, :] = inside[BLOCK : BLOCK + 1, :].astype(f32)

    @pl.loop(0, count // 32)
    def _(r):
        base = pl.multiple_of(r * 32, 32)
        window = padded[pl.ds(base, 48), :]
        value = (
            taps[0:1, :] * window[7:39, :]
            + taps[1:2, :] * window[8:40, :]
            + taps[2:3, :] * window[9:41, :]
        )
        act[pl.ds(base, 32), :] = gelu_of(value).astype(bf16)

    act_t[...] = act[...].T


def activate(meta, outer, inside, before, after, taps, late):
    hidden = outer.shape[1]
    count = (outer.shape[0] + inside.shape[0]) // 2
    return pl.pallas_call(
        functools.partial(act_kernel, late),
        out_shape=shape_of((hidden, count)),
        in_specs=[SM] + [VM] * 5,
        out_specs=VM,
        scratch_shapes=[pltpu.VMEM((count + 16, hidden), f32), pltpu.VMEM((count, hidden), bf16)],
        compiler_params=params(8),
        cost_estimate=cost(10**9, 2 * 10**6),
        name="activate",
    )(meta, outer, inside, before, after, taps)


def far_kernel(ys, meta, own, other, weights, other_weights, *outs):
    for i, out in enumerate(outs):
        chip = meta[CHIP + ys + i]
        block = 2 * chip + meta[CORE]
        total = dot(weights[block], own[...]) + dot(other_weights[chip], other[...])
        out[...] = total.astype(bf16)


def far_project(meta, ys, own, other, weights, other_weights):
    part = weights.shape[1]
    return pl.pallas_call(
        functools.partial(far_kernel, ys),
        out_shape=[shape_of((part, own.shape[1]))] * (ys - 1),
        in_specs=[SM] + [VM] * 4,
        out_specs=[VM] * (ys - 1),
        compiler_params=params(8),
        cost_estimate=cost(10**9, 4 * 10**6),
        name="far_project",
    )(meta, own, other, weights, other_weights)


def near_kernel(meta, own_a, other_a, own_b, other_b, middle_a, middle_b, weights, other_weights, after, base):
    size = own_a.shape[1]
    middle = (
        jnp.concatenate([middle_a[:, :BLOCK], middle_b[:, :BLOCK]], axis=1),
        jnp.concatenate([middle_b[:, BLOCK:], middle_a[:, BLOCK:]], axis=1),
    )
    for i, (own, other) in enumerate(((own_a, other_a), (own_b, other_b))):
        total = dot(weights[meta[ME]], own[...])
        total = total + dot(other_weights[meta[CHIP]], other[...])
        base[:, i * size : (i + 1) * size] = total + middle[i]


def near_project(meta, own, other, middle_a, middle_b, weights, other_weights, after):
    part = weights.shape[1]
    return pl.pallas_call(
        near_kernel,
        out_shape=shape_of((part, 2 * own[0].shape[1]), f32),
        in_specs=[SM] + [VM] * 8 + [ANY],
        out_specs=VM,
        compiler_params=params(10),
        cost_estimate=cost(2 * 10**9, 6 * 10**6),
        name="near_project",
    )(meta, own[0], other[0], own[1], other[1], middle_a, middle_b, weights, other_weights, after)


def core_swap(value, n):
    return lax.ppermute(value, "head", [(i, i ^ 1) for i in range(n)])


def y_shift(value, n, step):
    return lax.ppermute(value, "head", [(i, (i + 2 * step) % n) for i in range(n)])


def pair_swap(value, n):
    return lax.ppermute(value, "seq", [(i, i ^ 1) for i in range(n)])


def later(value, n, step):
    return lax.ppermute(value, "seq", [(i, i + 2 * step) for i in range(n - 2 * step)])


def shards(
    tokens,
    norm_gain,
    w_query,
    w_key,
    w_value,
    w_decay,
    w_beta,
    head_rates,
    head_gain,
    w_out,
    ffn_gain,
    w_up,
    conv_taps,
    w_down,
):
    n = lax.axis_size("head")
    seqs = lax.axis_size("seq")
    me = lax.axis_index("head")
    at = lax.axis_index("seq")
    core = me % 2
    parity = at % 2
    ys = n // 2
    count, part = tokens.shape
    heads = w_query.shape[1] // DK
    hidden = w_up.shape[1]
    features = n * part

    mine = tokens.T
    shifted = [mine] + [y_shift(mine, n, d) for d in range(1, ys)]

    def group_of(piece):
        partner = core_swap(piece, n)
        if part % 16:
            first = jnp.where(core == 0, piece, partner)
            second = jnp.where(core == 0, partner, piece)
            return [jnp.concatenate([first, second], axis=0)]
        return [piece, partner]

    groups = [group_of(mine)]
    chip = me // 2
    here = [parity, core, me]
    sources = [(chip + ys - d) % ys for d in range(ys)]
    targets = [(chip + d) % ys for d in range(1, ys)]
    meta = jnp.stack(here + sources + targets).astype(jnp.int32)

    w_out_t = w_out.T
    w_parts = w_down.T.reshape(n, part, hidden)

    gates = jnp.concatenate([w_decay.T, w_beta.T], axis=0)
    gates = jnp.pad(gates, ((0, 16 - 2 * heads), (0, 0)))
    gates = gates.reshape(16, ys, 2 * part).transpose(1, 0, 2)
    rates = jnp.pad(head_rates.reshape(2 * heads, 1), ((0, 16 - 2 * heads), (0, 0)))
    rates = jnp.broadcast_to(rates, (16, 128))
    gain = norm_gain.astype(f32).reshape(ys, 1, 2 * part)

    def ours(rows, d):
        return lax.dynamic_index_in_dim(rows, sources[d], 0, False)

    ffn_scale = ffn_gain.astype(f32).reshape(1, features)
    taps = conv_taps.astype(f32)

    early = None
    for d in range(ys - 1):
        early = early_project(
            meta, CHIP + d, groups[d], ours(gain, d), ours(gates, d), w_key, w_value, w_query, w_parts, early
        )
        if d == 0:
            sent_w_down, early = early[5], early[:5]
        piece, _ = lax.optimization_barrier((shifted[d + 1], early[4]))
        groups.append(group_of(piece))
    scaled, scale_b, keys, erased, entry, own_maps, sent_maps, totals = block_maps(
        meta, CHIP + ys - 1, groups[-1], ours(gain, -1), rates, ours(gates, -1), w_key, w_value, early
    )

    sent_w_out, sent_w_down, _ = lax.optimization_barrier((w_out_t, sent_w_down, groups[-1][-1]))
    other_w_out, other_w_down = core_swap(sent_w_out, n), core_swap(sent_w_down, n)
    acc_query, other_w_out, other_w_down = lax.optimization_barrier(
        (early[2], other_w_out, other_w_down)
    )

    other_maps = pair_swap(sent_maps, seqs)
    query, tokens_a, tokens_b, query_done = queries(
        meta, ys, scaled, scale_b, w_query, acc_query, sum(groups, [])
    )
    pair, first, done = pair_maps(meta, own_maps, other_maps, query_done)
    pairs = [later(pair, seqs, d) for d in range(seqs // 2 - 1, 0, -1)]
    shard_query, free, out_done = block_outputs(query, keys, erased, entry, totals, done)
    kept_state, given_state = start_states(meta, first, pairs, out_done)
    other_state = pair_swap(given_state, seqs)

    mixed = mixed_heads(meta, kept_state, other_state, shard_query, free, head_gain.reshape(1, DK))
    sums = []
    for own_mixed in mixed:
        summed = attend(meta, own_mixed, core_swap(own_mixed, n), w_out_t, other_w_out)
        sums.append([summed] + [y_shift(summed, n, d) for d in range(1, ys)])
    ups = []
    for own, own_tokens in zip(sums, (tokens_a, tokens_b)):
        ahead = ups[0][2] if ups else sums[1][0]
        own = own[:1] + list(lax.optimization_barrier((tuple(own[1:]), ahead))[0])
        other = [core_swap(value, n) for value in own]
        ups.append(up_project(meta, own_tokens, own, other, ffn_scale, w_up, part))
    (outer, middle_a, first_row, last_row), (inside, middle_b, _, _) = ups
    before = lax.ppermute(last_row, "seq", [(i, i + 1) for i in range(seqs - 1)])
    after = lax.ppermute(first_row, "seq", [(i + 1, i) for i in range(seqs - 1)])

    acts = [activate(meta, outer, inside, before, after, taps, late) for late in (False, True)]
    partner_acts = [core_swap(act, n) for act in acts]
    fars = [
        far_project(meta, ys, act, partner, w_parts, other_w_down)
        for act, partner in zip(acts, partner_acts)
    ]
    total = near_project(
        meta, acts, partner_acts, middle_a, middle_b, w_parts, other_w_down, fars[1][0]
    )
    for d in range(1, ys):
        halves = [y_shift(far[d - 1], n, d) for far in fars]
        total = total + jnp.concatenate(halves, axis=1).astype(f32)
    return total.astype(bf16).T


def solution(mesh):
    placed = (
        P("seq", "head"),
        P(),
        P(None, "head"),
        P(None, "head"),
        P(None, "head"),
        P(None, "head"),
        P(None, "head"),
        P(None, "head"),
        P(),
        P("head", None),
        P(),
        P(None, "head"),
        P(None, "head"),
        P("head", None),
    )
    return jax.shard_map(
        shards, mesh=mesh, in_specs=placed, out_specs=P("seq", "head"), check_vma=False
    )
```

```python
import functools

import jax
import jax.numpy as jnp
from jax import lax
from jax.experimental import pallas as pl
from jax.experimental.pallas import tpu as pltpu
from jax.sharding import PartitionSpec as P

DK = 128
BLOCK = 128
epsilon = 1e-06
f32 = jnp.float32
bf16 = jnp.bfloat16

PARITY, CORE, ME, CHIP = 0, 1, 2, 3

VM = pl.BlockSpec(memory_space=pltpu.VMEM)
SM = pl.BlockSpec(memory_space=pltpu.SMEM)
ANY = pl.BlockSpec(memory_space=pl.ANY)


def params(mebibytes):
    return pltpu.CompilerParams(vmem_limit_bytes=mebibytes * 1024 * 1024)


def cost(flops, moved):
    return pl.CostEstimate(flops=flops, bytes_accessed=moved, transcendentals=0)


def shape_of(shape, dtype=bf16):
    return jax.ShapeDtypeStruct(shape, dtype)


def dot(a, b):
    return jnp.dot(a, b, preferred_element_type=f32)


def dot_nt(a, b):
    return lax.dot_general(a, b, (((1,), (1,)), ((), ())), preferred_element_type=f32)


def dot_tn(a, b):
    return lax.dot_general(a, b, (((0,), (0,)), ((), ())), preferred_element_type=f32)


def iotas(shape):
    return lax.broadcasted_iota(jnp.int32, shape, 0), lax.broadcasted_iota(jnp.int32, shape, 1)


def column_of(row, lanes=128):
    return jnp.broadcast_to(row, (lanes, row.shape[1])).T


def scale_pass(source, gain_at, target):
    features, tokens = source.shape
    squares = jnp.zeros((8, tokens), f32)
    for start in range(0, features, 128):
        size = min(128, features - start)
        value = source[start : start + size, :].astype(f32)
        scale = column_of(gain_at(start, size))
        scale = jnp.concatenate([scale] * (tokens // 128), axis=1)
        target[:, start : start + size] = (value * scale).astype(bf16).T
        value = value * value
        for r in range(0, size, 8):
            squares = squares + value[r : r + 8]
    return squares


def inverse_of(squares, features):
    return lax.rsqrt(jnp.sum(squares, axis=0, keepdims=True) / features + epsilon)


def fill_columns(row, target):
    for start in range(0, row.shape[1], 128):
        target[start : start + 128, :] = column_of(row[:, start : start + 128])


def doubled(tile):
    return jnp.concatenate([tile, tile], axis=1)


def slots_of(meta, n):
    return [meta[CORE], 1 - meta[CORE]] if n == 2 else [0]


def load_pair(meta, pieces, whole, sem):
    part = pieces[0].shape[0]
    copies = [
        pltpu.make_async_copy(
            piece, whole.at[pl.ds(pl.multiple_of(slot * part, 16), part)], sem.at[p]
        )
        for p, (piece, slot) in enumerate(zip(pieces, slots_of(meta, len(pieces))))
    ]
    for copy in copies:
        copy.start()
    for copy in copies:
        copy.wait()


def held_rows(meta, at, weights, held, sem):
    span = held.shape[1]
    rows = pl.ds(pl.multiple_of(meta[at] * span, 16), span)
    copies = [
        pltpu.make_async_copy(ref.at[rows], held.at[i], sem.at[i]) for i, ref in enumerate(weights)
    ]
    for copy in copies:
        copy.start()
    return copies


def early_kernel(count_in, at, meta, *refs):
    first = at == CHIP
    pieces = refs[:count_in]
    gain, gates, w_key, w_value, w_query, w_down = refs[count_in : count_in + 6]
    refs = refs[count_in + 6 :]
    before, refs = (None, refs) if first else (refs[:5], refs[5:])
    acc_k, acc_v, acc_q, acc_g, squares = refs[:5]
    partner_w, whole, scaled, held, held_sem, sem = refs[5:] if first else (None, *refs[5:])
    rows_copies = held_rows(meta, at, (w_key, w_value, w_query), held, held_sem)
    copies = [
        pltpu.make_async_copy(
            w_down.at[2 * y + 1 - meta[CORE]], partner_w.at[y], sem.at[count_in + y]
        )
        for y in range(partner_w.shape[0] if first else 0)
    ]
    for copy in copies:
        copy.start()
    load_pair(meta, pieces, whole, sem)
    sums = scale_pass(whole, lambda at, size: gain[:, at : at + size], scaled)
    gate = dot_nt(gates[...], scaled[...])
    squares[...] = sums if first else before[4][...] + sums
    acc_g[...] = gate if first else before[3][...] + gate
    for i, out in enumerate((acc_k, acc_v, acc_q)):
        rows_copies[i].wait()
        product = dot(scaled[...], held[i])
        out[...] = product if first else before[i][...] + product
    for copy in copies:
        copy.wait()


def early_project(meta, at, pieces, gain, gates, w_key, w_value, w_query, w_down, before):
    first = before is None
    blocks, part, hidden = w_down.shape
    ys = blocks // 2
    span = gain.shape[1]
    count = pieces[0].shape[1]
    inner = w_key.shape[1]
    return pl.pallas_call(
        functools.partial(early_kernel, len(pieces), at),
        out_shape=[shape_of((count, inner), f32)] * 3
        + [shape_of((16, count), f32), shape_of((8, count), f32)]
        + [shape_of((ys, part, hidden))] * first,
        in_specs=[SM] + [ANY] * len(pieces) + [VM] * 2 + [ANY] * 4 + [VM] * (0 if first else 5),
        out_specs=[VM] * (5 + first),
        scratch_shapes=[
            pltpu.VMEM((span, count), bf16),
            pltpu.VMEM((count, span), bf16),
            pltpu.VMEM((3, span, inner), bf16),
            pltpu.SemaphoreType.DMA((3,)),
            pltpu.SemaphoreType.DMA((len(pieces) + ys,)),
        ],
        compiler_params=params(48),
        cost_estimate=cost(3 * 10**9, 8 * 10**6),
        name="early_project",
    )(meta, *pieces, gain, gates, w_key, w_value, w_query, w_down, *(before or ()))


def maps_kernel(n, heads, at, meta, *refs):
    pieces = refs[:n]
    gain, rates, gates, w_key, w_value, acc_k, acc_v, acc_g, squares = refs[n : n + 9]
    scaled, scale_b, keys, erased, entry, own, sent, totals = refs[n + 9 : n + 17]
    whole, raw_k, raw_v, rows_at_head, total_b, beta_b, held, held_sem, acc, acc_sem, sem = refs[
        n + 17 :
    ]
    span, count = whole.shape
    blocks = count // BLOCK
    inner = heads * DK
    features = w_key.shape[0]
    parity = meta[PARITY]
    rows_copies = held_rows(meta, at, (w_key, w_value), held, held_sem)
    rows_copies += [
        pltpu.make_async_copy(ref, acc.at[i], acc_sem.at[i]) for i, ref in enumerate((acc_k, acc_v))
    ]
    for copy in rows_copies[2:]:
        copy.start()
    load_pair(meta, pieces, whole, sem)
    sums = scale_pass(whole, lambda at, size: gain[:, at : at + size], scaled)
    inverse = inverse_of(sums + squares[...], features)
    fill_columns(inverse, scale_b)

    pre = (acc_g[...] + dot_nt(gates[...], scaled[...])) * inverse
    soft = jnp.maximum(pre, 0.0) + jnp.log1p(jnp.exp(-jnp.abs(pre)))
    rate = jnp.concatenate([rates[...]] * (count // 128), axis=1)
    decay = -rate * soft
    beta = jax.nn.sigmoid(pre + rate)
    row_at, col_at = iotas((BLOCK, BLOCK))
    upper = (row_at <= col_at).astype(f32)
    rows_at_head[...] = jnp.zeros_like(rows_at_head)
    for c in range(blocks):
        tokens = slice(c * BLOCK, (c + 1) * BLOCK)
        total = jnp.dot(
            decay[:, tokens], upper, precision=lax.Precision.HIGHEST, preferred_element_type=f32
        )
        totals[c] = total
        rows_at_head[0:16, :] = total
        rows_at_head[16:32, :] = beta[:, tokens]
        columns = rows_at_head[...].T
        for h in range(heads):
            total_b[h, tokens, :] = jnp.broadcast_to(columns[:, h : h + 1], (BLOCK, DK))
            lane = 16 + heads + h
            beta_b[h, tokens, :] = jnp.broadcast_to(columns[:, lane : lane + 1], (BLOCK, DK))

    for copy in rows_copies:
        copy.wait()
    for start in range(0, inner, 256):
        cols = slice(start, start + 256)
        scale = doubled(scale_b[...])
        raw_k[:, cols] = ((acc[0, :, cols] + dot(scaled[...], held[0, :, cols])) * scale).astype(bf16)
        raw_v[:, cols] = ((acc[1, :, cols] + dot(scaled[...], held[1, :, cols])) * scale).astype(bf16)

    xor = jnp.where(row_at > col_at, row_at ^ col_at, 0)
    eye = jnp.where(row_at == col_at, 1.0, 0.0)
    group = 2 if heads % 2 == 0 else 1

    @pl.loop(0, heads // group)
    def _(batch):
        lows, solved = [], []
        chains = []
        for g in range(group):
            h = batch * group + g
            cols = pl.ds(pl.multiple_of(h * DK, DK), DK)
            wide = pl.ds(pl.multiple_of(h * 2 * DK, 2 * DK), 2 * DK)
            raw = raw_k[:, cols].astype(f32)
            unit = raw * lax.rsqrt(jnp.sum(raw * raw, axis=1, keepdims=True) + epsilon)
            keys[:, cols] = unit.astype(bf16)
            for c in range(blocks):
                chains.append((h, cols, wide, c, slice(c * BLOCK, (c + 1) * BLOCK)))
        for h, cols, wide, c, rows in chains:
            k = keys[rows, cols]
            fade = jnp.exp(jnp.minimum(total_b[h, rows, :] - totals[c, pl.ds(h, 1), :], 0.0))
            low = jnp.where(xor > 0, beta_b[h, rows, :] * fade * dot_nt(k, k), 0.0)
            lows.append(low)
            solved.append(eye - jnp.where(xor == 1, low, 0.0))
        size = 2
        while size < BLOCK:
            mask = (xor >= size) & (xor < 2 * size)
            first = []
            for i in range(len(chains)):
                link = jnp.where(mask, lows[i], 0.0).astype(bf16)
                first.append(dot(link, solved[i].astype(bf16)).astype(bf16))
            solved = [
                solved[i] - dot(solved[i].astype(bf16), first[i]) for i in range(len(chains))
            ]
            size *= 2
        grown = []
        for i, (h, cols, wide, c, rows) in enumerate(chains):
            k = keys[rows, cols].astype(f32)
            t_col = total_b[h, rows, :]
            b_col = beta_b[h, rows, :]
            right = jnp.concatenate(
                [
                    (b_col * jnp.exp(t_col) * k).astype(bf16),
                    (b_col * raw_v[rows, cols].astype(f32)).astype(bf16),
                ],
                axis=1,
            )
            both = dot(solved[i].astype(bf16), right).astype(bf16)
            erased[rows, wide] = both
            t_end = t_col[BLOCK - 1 : BLOCK, :]
            faded = (jnp.exp(t_end - t_col) * k).astype(bf16)
            grown.append((jnp.exp(t_end), dot_tn(faded, both)))
        states = [None] * group
        for c in range(blocks):
            for g in range(group):
                h, cols, wide = chains[g * blocks][:3]
                end, product = grown[g * blocks + c]
                erase, write = product[:, :DK], product[:, DK:]
                if c == 0:
                    state = jnp.concatenate([end * eye - erase, write], axis=1)
                else:
                    step = dot(erase.astype(bf16), states[g].astype(bf16))
                    state = (
                        jnp.concatenate([end, end], axis=1) * states[g]
                        - step
                        + jnp.concatenate([jnp.zeros_like(write), write], axis=1)
                    )
                if c < blocks - 1:
                    entry[c, :, wide] = state.astype(bf16)
                states[g] = state
        for g in range(group):
            h = batch * group + g
            half = heads // 2
            mine = (h >= half) == (parity == 1)
            slot = lax.rem(h, half)

            @pl.when(mine)
            def _():
                own[slot] = states[g].astype(bf16)

            @pl.when(jnp.logical_not(mine))
            def _():
                sent[slot] = states[g].astype(bf16)


def block_maps(meta, at, pieces, gain, rates, gates, w_key, w_value, early):
    n = len(pieces)
    acc_k, acc_v, acc_q, acc_g, squares = early
    count = pieces[0].shape[1]
    span = gain.shape[1]
    inner = w_key.shape[1]
    heads = inner // DK
    blocks = count // BLOCK
    return pl.pallas_call(
        functools.partial(maps_kernel, n, heads, at),
        out_shape=(
            shape_of((count, span)),
            shape_of((count, DK), f32),
            shape_of((count, inner)),
            shape_of((count, 2 * inner)),
            shape_of((blocks - 1, DK, 2 * inner)),
            shape_of((heads // 2, DK, 2 * DK)),
            shape_of((heads // 2, DK, 2 * DK)),
            shape_of((blocks, 16, 128), f32),
        ),
        in_specs=[SM] + [ANY] * n + [VM] * 3 + [ANY] * 4 + [VM] * 2,
        out_specs=[VM] * 8,
        scratch_shapes=[
            pltpu.VMEM((span, count), bf16),
            pltpu.VMEM((count, inner), bf16),
            pltpu.VMEM((count, inner), bf16),
            pltpu.VMEM((128, BLOCK), f32),
            pltpu.VMEM((heads, count, DK), f32),
            pltpu.VMEM((heads, count, DK), f32),
            pltpu.VMEM((2, span, inner), bf16),
            pltpu.SemaphoreType.DMA((2,)),
            pltpu.VMEM((2, count, inner), f32),
            pltpu.SemaphoreType.DMA((2,)),
            pltpu.SemaphoreType.DMA((n,)),
        ],
        compiler_params=params(16),
        cost_estimate=cost(10 * 10**9, 14 * 10**6),
        name="block_maps",
    )(meta, *pieces, gain, rates, gates, w_key, w_value, acc_k, acc_v, acc_g, squares)


def query_kernel(n, ys, meta, scaled, scale_b, weights, acc, *refs):
    pieces, (query, tokens_a, tokens_b, done, held, sem) = refs[: n * ys], refs[n * ys :]
    (copy,) = held_rows(meta, CHIP + ys - 1, (weights,), held, sem)
    span = scaled.shape[1]
    part, count = pieces[0].shape
    for d in range(ys):
        for p, slot in enumerate(slots_of(meta, n)):
            piece = pieces[d * n + p]
            base = meta[CHIP + d] * span + slot * part
            step = part // 7

            @pl.loop(0, 7)
            def _(r):
                rows = pl.ds(pl.multiple_of(r * step, 8), step)
                target = pl.ds(pl.multiple_of(base + r * step, 8), step)
                tokens_a[target, :BLOCK] = piece[rows, :BLOCK]
                tokens_a[target, BLOCK:] = piece[rows, count - BLOCK :]
                tokens_b[target, :] = piece[rows, BLOCK : count - BLOCK]

    done[...] = jnp.zeros_like(done)
    copy.wait()
    for start in range(0, query.shape[1], 256):
        cols = slice(start, start + 256)
        product = acc[:, cols] + dot(scaled[...], held[0, :, cols])
        query[:, cols] = (product * doubled(scale_b[...])).astype(bf16)


def queries(meta, ys, scaled, scale_b, weights, acc, pieces):
    n = len(pieces) // ys
    features = weights.shape[0]
    count = acc.shape[0]
    return pl.pallas_call(
        functools.partial(query_kernel, n, ys),
        out_shape=(
            shape_of(acc.shape),
            shape_of((features, 2 * BLOCK)),
            shape_of((features, count - 2 * BLOCK)),
            shape_of((8, 128), f32),
        ),
        in_specs=[SM] + [VM] * 2 + [ANY] + [VM] * (1 + len(pieces)),
        out_specs=[VM] * 4,
        scratch_shapes=[
            pltpu.VMEM((1, scaled.shape[1], acc.shape[1]), bf16),
            pltpu.SemaphoreType.DMA((1,)),
        ],
        compiler_params=params(12),
        cost_estimate=cost(10**9, 8 * 10**6),
        name="queries",
    )(meta, scaled, scale_b, weights, acc, *pieces)


def outputs_kernel(heads, query, keys, erased, entry, totals, after, shard_query, free, done, rows_at_head):
    count = query.shape[0]
    blocks = count // BLOCK
    row_at, col_at = iotas((BLOCK, BLOCK))
    done[...] = jnp.zeros_like(done)
    rows_at_head[...] = jnp.zeros_like(rows_at_head)
    for c in range(blocks):
        rows = slice(c * BLOCK, (c + 1) * BLOCK)
        rows_at_head[0:16, :] = totals[c]
        columns = rows_at_head[...].T
        for h in range(heads):
            cols = slice(h * DK, (h + 1) * DK)
            wide = slice(h * 2 * DK, (h + 1) * 2 * DK)
            t_col = jnp.broadcast_to(columns[:, h : h + 1], (BLOCK, BLOCK))
            t_row = totals[c, h : h + 1, :]
            fade = jnp.where(row_at >= col_at, jnp.exp(jnp.minimum(t_col - t_row, 0.0)), 0.0)
            q = query[rows, cols]
            scores = (fade * dot_nt(q, keys[rows, cols])).astype(bf16)
            both = dot(scores, erased[rows, wide])
            reach = jnp.exp(t_col) * q.astype(f32) - both[:, :DK]
            local = both[:, DK:]
            if c > 0:
                product = dot(reach.astype(bf16), entry[c - 1, :, wide])
                reach = product[:, :DK]
                local = local + product[:, DK:]
            shard_query[rows, cols] = reach.astype(bf16)
            free[rows, cols] = local


def block_outputs(query, keys, erased, entry, totals, after):
    heads = query.shape[1] // DK
    return pl.pallas_call(
        functools.partial(outputs_kernel, heads),
        out_shape=(shape_of(query.shape), shape_of(query.shape, f32), shape_of((8, 128), f32)),
        in_specs=[VM] * 5 + [ANY],
        out_specs=[VM] * 3,
        scratch_shapes=[pltpu.VMEM((128, BLOCK), f32)],
        compiler_params=params(8),
        cost_estimate=cost(3 * 10**9, 4 * 10**6),
        name="block_outputs",
    )(query, keys, erased, entry, totals, after)


def pair_kernel(meta, own, other, after, pair, first, done):
    even = meta[PARITY] == 0
    for h in range(own.shape[0]):
        mine, theirs = own[h], other[h]
        early = jnp.where(even, mine, theirs)
        late = jnp.where(even, theirs, mine)
        product = dot(late[:, :DK], early)
        shift = late[:, DK:].astype(f32)
        pair[h] = (product + jnp.concatenate([jnp.zeros_like(shift), shift], axis=1)).astype(bf16)
        first[h] = early
    done[...] = jnp.zeros_like(done)


def pair_maps(meta, own, other, after):
    return pl.pallas_call(
        pair_kernel,
        out_shape=(shape_of(own.shape), shape_of(own.shape), shape_of((8, 128), f32)),
        in_specs=[SM, VM, VM, ANY],
        out_specs=[VM] * 3,
        compiler_params=params(4),
        name="pair_maps",
    )(meta, own, other, after)


def apply_map(whole, state):
    high = state.astype(bf16)
    low = (state - high.astype(f32)).astype(bf16)
    product = dot(whole[:, :DK], jnp.concatenate([high, low], axis=1))
    return product[:, :DK] + product[:, DK:] + whole[:, DK:].astype(f32)


def start_kernel(steps, meta, first, *refs):
    pairs, (after, keep, give) = refs[:steps], refs[steps:]
    even = meta[PARITY] == 0
    for h in range(first.shape[0]):
        state = pairs[0][h][:, DK:].astype(f32)
        for pair in pairs[1:]:
            state = apply_map(pair[h], state)
        later = apply_map(first[h], state)
        keep[h] = jnp.where(even, state, later).astype(bf16)
        give[h] = jnp.where(even, later, state).astype(bf16)


def start_states(meta, first, pairs, after):
    heads = first.shape[0]
    shape = shape_of((heads, DK, DK))
    return pl.pallas_call(
        functools.partial(start_kernel, len(pairs)),
        out_shape=(shape, shape),
        in_specs=[SM] + [VM] * (1 + len(pairs)) + [ANY],
        out_specs=[VM] * 2,
        compiler_params=params(4),
        name="start_states",
    )(meta, first, *pairs, after)


def mixed_kernel(heads, meta, own, other, shard_query, free, gain, mixed_a, mixed_b):
    even = meta[PARITY] == 0
    half = heads // 2
    blocks = shard_query.shape[0] // BLOCK
    for h in range(heads):
        cols = slice(h * DK, (h + 1) * DK)
        if h < half:
            state = jnp.where(even, own[h], other[h])
        else:
            state = jnp.where(even, other[h - half], own[h - half])
        for unit in range(blocks):
            rows = slice(unit * BLOCK, (unit + 1) * BLOCK)
            out = dot(shard_query[rows, cols], state) + free[rows, cols]
            scale = lax.rsqrt(jnp.mean(out * out, axis=1, keepdims=True) + epsilon)
            value = (out * scale * gain[...].astype(f32)).astype(bf16)
            if unit == 0:
                mixed_a[:BLOCK, cols] = value
            elif unit == blocks - 1:
                mixed_a[BLOCK:, cols] = value
            else:
                mixed_b[(unit - 1) * BLOCK : unit * BLOCK, cols] = value


def mixed_heads(meta, own, other, shard_query, free, gain):
    count, inner = shard_query.shape
    return pl.pallas_call(
        functools.partial(mixed_kernel, inner // DK),
        out_shape=(shape_of((2 * BLOCK, inner)), shape_of((count - 2 * BLOCK, inner))),
        in_specs=[SM] + [VM] * 5,
        out_specs=[VM] * 2,
        compiler_params=params(6),
        cost_estimate=cost(10**9, 3 * 10**6),
        name="mixed_heads",
    )(meta, own, other, shard_query, free, gain)


def attend_kernel(meta, own, other, weights, other_weights, chip):
    rows = pl.ds(pl.multiple_of(meta[CORE] * chip.shape[0], 16), chip.shape[0])
    total = dot_nt(weights[rows, :], own[...]) + dot_nt(other_weights[rows, :], other[...])
    chip[...] = total.astype(bf16)


def attend(meta, own, other, weights, other_weights):
    return pl.pallas_call(
        attend_kernel,
        out_shape=shape_of((weights.shape[0] // 2, own.shape[0])),
        in_specs=[SM] + [VM] * 4,
        out_specs=VM,
        compiler_params=params(10),
        cost_estimate=cost(10**9, 5 * 10**6),
        name="attend",
    )(meta, own, other, weights, other_weights)


def up_kernel(adds, meta, tokens, *refs):
    own, other = refs[:adds], refs[adds : 2 * adds]
    gain, weights, lifted, middle_part, first, last, middle, hidden, scale_b = refs[2 * adds :]
    features, count = middle.shape
    half = features // 2
    step = 160
    for side, parts in ((meta[CORE], own), (1 - meta[CORE], other)):

        @pl.loop(0, half // step)
        def _(r):
            rows = pl.ds(pl.multiple_of(r * step, 32), step)
            target = pl.ds(pl.multiple_of(side * half + r * step, 32), step)
            total = tokens[target, :].astype(f32)
            for ref in parts:
                total = total + ref[rows, :].astype(f32)
            middle[target, :] = total.astype(bf16).astype(f32)

    squares = scale_pass(middle, lambda at, size: gain[:, at : at + size], hidden)
    fill_columns(inverse_of(squares, features), scale_b)
    part = middle_part.shape[0]
    middle_part[...] = middle[pl.ds(pl.multiple_of(meta[ME] * part, 8), part), :]
    width = lifted.shape[1]
    for start in range(0, width, 256):
        size = min(256, width - start)
        cols = slice(start, start + size)
        scale = doubled(scale_b[...])[:, :size]
        lifted[:, cols] = (dot(hidden[...], weights[:, cols]) * scale).astype(bf16)
    first[...] = lifted[0:1, :]
    last[...] = lifted[count - 1 : count, :]


def up_project(meta, tokens, own, other, gain, weights, part):
    features, hidden = weights.shape
    count = tokens.shape[1]
    return pl.pallas_call(
        functools.partial(up_kernel, len(own)),
        out_shape=(
            shape_of((count, hidden)),
            shape_of((part, count), f32),
            shape_of((1, hidden)),
            shape_of((1, hidden)),
        ),
        in_specs=[SM] + [VM] * (3 + 2 * len(own)),
        out_specs=[VM] * 4,
        scratch_shapes=[
            pltpu.VMEM((features, count), f32),
            pltpu.VMEM((count, features), bf16),
            pltpu.VMEM((count, DK), f32),
        ],
        compiler_params=params(16),
        cost_estimate=cost(2 * 10**9, 8 * 10**6),
        name="up_project",
    )(meta, tokens, *own, *other, gain, weights)


def gelu_of(x):
    inner = 0.7978845608028654 * (x + 0.044715 * (x * x * x))
    return 0.5 * x * (1.0 + jnp.tanh(inner))


def act_kernel(late, meta, outer, inside, before, after, taps, act_t, padded, act):
    count = act.shape[0]
    if late:
        padded[7:8, :] = inside[BLOCK - 1 : BLOCK, :].astype(f32)
        padded[8 : 8 + BLOCK, :] = inside[BLOCK:, :].astype(f32)
        padded[8 + BLOCK : 8 + count, :] = outer[BLOCK:, :].astype(f32)
        padded[8 + count : 9 + count, :] = after[...].astype(f32)
    else:
        padded[7:8, :] = before[...].astype(f32)
        padded[8 : 8 + BLOCK, :] = outer[:BLOCK, :].astype(f32)
        padded[8 + BLOCK : 8 + count, :] = inside[:BLOCK, :].astype(f32)
        padded[8 + count : 9 + count, :] = inside[BLOCK : BLOCK + 1, :].astype(f32)

    @pl.loop(0, count // 32)
    def _(r):
        base = pl.multiple_of(r * 32, 32)
        window = padded[pl.ds(base, 48), :]
        value = (
            taps[0:1, :] * window[7:39, :]
            + taps[1:2, :] * window[8:40, :]
            + taps[2:3, :] * window[9:41, :]
        )
        act[pl.ds(base, 32), :] = gelu_of(value).astype(bf16)

    act_t[...] = act[...].T


def activate(meta, outer, inside, before, after, taps, late):
    hidden = outer.shape[1]
    count = (outer.shape[0] + inside.shape[0]) // 2
    return pl.pallas_call(
        functools.partial(act_kernel, late),
        out_shape=shape_of((hidden, count)),
        in_specs=[SM] + [VM] * 5,
        out_specs=VM,
        scratch_shapes=[pltpu.VMEM((count + 16, hidden), f32), pltpu.VMEM((count, hidden), bf16)],
        compiler_params=params(8),
        cost_estimate=cost(10**9, 2 * 10**6),
        name="activate",
    )(meta, outer, inside, before, after, taps)


def far_kernel(ys, meta, own, other, weights, other_weights, *outs):
    for i, out in enumerate(outs):
        chip = meta[CHIP + ys + i]
        block = 2 * chip + meta[CORE]
        total = dot(weights[block], own[...]) + dot(other_weights[chip], other[...])
        out[...] = total.astype(bf16)


def far_project(meta, ys, own, other, weights, other_weights):
    part = weights.shape[1]
    return pl.pallas_call(
        functools.partial(far_kernel, ys),
        out_shape=[shape_of((part, own.shape[1]))] * (ys - 1),
        in_specs=[SM] + [VM] * 4,
        out_specs=[VM] * (ys - 1),
        compiler_params=params(8),
        cost_estimate=cost(10**9, 4 * 10**6),
        name="far_project",
    )(meta, own, other, weights, other_weights)


def near_kernel(meta, own_a, other_a, own_b, other_b, middle_a, middle_b, weights, other_weights, after, base):
    size = own_a.shape[1]
    middle = (
        jnp.concatenate([middle_a[:, :BLOCK], middle_b[:, :BLOCK]], axis=1),
        jnp.concatenate([middle_b[:, BLOCK:], middle_a[:, BLOCK:]], axis=1),
    )
    for i, (own, other) in enumerate(((own_a, other_a), (own_b, other_b))):
        total = dot(weights[meta[ME]], own[...])
        total = total + dot(other_weights[meta[CHIP]], other[...])
        base[:, i * size : (i + 1) * size] = total + middle[i]


def near_project(meta, own, other, middle_a, middle_b, weights, other_weights, after):
    part = weights.shape[1]
    return pl.pallas_call(
        near_kernel,
        out_shape=shape_of((part, 2 * own[0].shape[1]), f32),
        in_specs=[SM] + [VM] * 8 + [ANY],
        out_specs=VM,
        compiler_params=params(10),
        cost_estimate=cost(2 * 10**9, 6 * 10**6),
        name="near_project",
    )(meta, own[0], other[0], own[1], other[1], middle_a, middle_b, weights, other_weights, after)


def core_swap(value, n):
    return lax.ppermute(value, "head", [(i, i ^ 1) for i in range(n)])


def y_shift(value, n, step):
    return lax.ppermute(value, "head", [(i, (i + 2 * step) % n) for i in range(n)])


def pair_swap(value, n):
    return lax.ppermute(value, "seq", [(i, i ^ 1) for i in range(n)])


def later(value, n, step):
    return lax.ppermute(value, "seq", [(i, i + 2 * step) for i in range(n - 2 * step)])


def shards(
    tokens,
    norm_gain,
    w_query,
    w_key,
    w_value,
    w_decay,
    w_beta,
    head_rates,
    head_gain,
    w_out,
    ffn_gain,
    w_up,
    conv_taps,
    w_down,
):
    n = lax.axis_size("head")
    seqs = lax.axis_size("seq")
    me = lax.axis_index("head")
    at = lax.axis_index("seq")
    core = me % 2
    parity = at % 2
    ys = n // 2
    count, part = tokens.shape
    heads = w_query.shape[1] // DK
    hidden = w_up.shape[1]
    features = n * part

    mine = tokens.T
    shifted = [mine] + [y_shift(mine, n, d) for d in range(1, ys)]

    def group_of(piece):
        partner = core_swap(piece, n)
        if part % 16:
            first = jnp.where(core == 0, piece, partner)
            second = jnp.where(core == 0, partner, piece)
            return [jnp.concatenate([first, second], axis=0)]
        return [piece, partner]

    groups = [group_of(mine)]
    chip = me // 2
    here = [parity, core, me]
    sources = [(chip + ys - d) % ys for d in range(ys)]
    targets = [(chip + d) % ys for d in range(1, ys)]
    meta = jnp.stack(here + sources + targets).astype(jnp.int32)

    w_out_t = w_out.T
    w_parts = w_down.T.reshape(n, part, hidden)

    gates = jnp.concatenate([w_decay.T, w_beta.T], axis=0)
    gates = jnp.pad(gates, ((0, 16 - 2 * heads), (0, 0)))
    gates = gates.reshape(16, ys, 2 * part).transpose(1, 0, 2)
    rates = jnp.pad(head_rates.reshape(2 * heads, 1), ((0, 16 - 2 * heads), (0, 0)))
    rates = jnp.broadcast_to(rates, (16, 128))
    gain = norm_gain.astype(f32).reshape(ys, 1, 2 * part)

    def ours(rows, d):
        return lax.dynamic_index_in_dim(rows, sources[d], 0, False)

    ffn_scale = ffn_gain.astype(f32).reshape(1, features)
    taps = conv_taps.astype(f32)

    gains = [ours(gain, d) for d in range(ys)]
    gate_rows = [ours(gates, d) for d in range(ys)]
    gains, gate_rows, rates, taps, ffn_scale, head_scale, meta = lax.optimization_barrier(
        (gains, gate_rows, rates, taps, ffn_scale, head_gain.reshape(1, DK), meta)
    )

    early = None
    for d in range(ys - 1):
        early = early_project(
            meta, CHIP + d, groups[d], gains[d], gate_rows[d], w_key, w_value, w_query, w_parts, early
        )
        if d == 0:
            sent_w_down, early = early[5], early[:5]
        piece, _ = lax.optimization_barrier((shifted[d + 1], early[4]))
        groups.append(group_of(piece))
    scaled, scale_b, keys, erased, entry, own_maps, sent_maps, totals = block_maps(
        meta, CHIP + ys - 1, groups[-1], gains[-1], rates, gate_rows[-1], w_key, w_value, early
    )

    sent_w_out, sent_w_down, _ = lax.optimization_barrier((w_out_t, sent_w_down, groups[-1][-1]))
    other_w_out, other_w_down = core_swap(sent_w_out, n), core_swap(sent_w_down, n)
    acc_query, other_w_out, other_w_down = lax.optimization_barrier(
        (early[2], other_w_out, other_w_down)
    )

    other_maps = pair_swap(sent_maps, seqs)
    query, tokens_a, tokens_b, query_done = queries(
        meta, ys, scaled, scale_b, w_query, acc_query, sum(groups, [])
    )
    pair, first, done = pair_maps(meta, own_maps, other_maps, query_done)
    pairs = [later(pair, seqs, d) for d in range(seqs // 2 - 1, 0, -1)]
    shard_query, free, out_done = block_outputs(query, keys, erased, entry, totals, done)
    kept_state, given_state = start_states(meta, first, pairs, out_done)
    other_state = pair_swap(given_state, seqs)

    mixed = mixed_heads(meta, kept_state, other_state, shard_query, free, head_scale)
    sums = []
    for own_mixed in mixed:
        summed = attend(meta, own_mixed, core_swap(own_mixed, n), w_out_t, other_w_out)
        sums.append([summed] + [y_shift(summed, n, d) for d in range(1, ys)])
    ups = []
    for own, own_tokens in zip(sums, (tokens_a, tokens_b)):
        ahead = ups[0][2] if ups else sums[1][0]
        own = own[:1] + list(lax.optimization_barrier((tuple(own[1:]), ahead))[0])
        other = [core_swap(value, n) for value in own]
        ups.append(up_project(meta, own_tokens, own, other, ffn_scale, w_up, part))
    (outer, middle_a, first_row, last_row), (inside, middle_b, _, _) = ups
    before = lax.ppermute(last_row, "seq", [(i, i + 1) for i in range(seqs - 1)])
    after = lax.ppermute(first_row, "seq", [(i + 1, i) for i in range(seqs - 1)])

    acts = [activate(meta, outer, inside, before, after, taps, late) for late in (False, True)]
    partner_acts = [core_swap(act, n) for act in acts]
    fars = [
        far_project(meta, ys, act, partner, w_parts, other_w_down)
        for act, partner in zip(acts, partner_acts)
    ]
    total = near_project(
        meta, acts, partner_acts, middle_a, middle_b, w_parts, other_w_down, fars[1][0]
    )
    for d in range(1, ys):
        halves = [y_shift(far[d - 1], n, d) for far in fars]
        total = total + jnp.concatenate(halves, axis=1).astype(f32)
    return total.astype(bf16).T


def solution(mesh):
    placed = (
        P("seq", "head"),
        P(),
        P(None, "head"),
        P(None, "head"),
        P(None, "head"),
        P(None, "head"),
        P(None, "head"),
        P(None, "head"),
        P(),
        P("head", None),
        P(),
        P(None, "head"),
        P(None, "head"),
        P("head", None),
    )
    return jax.shard_map(
        shards, mesh=mesh, in_specs=placed, out_specs=P("seq", "head"), check_vma=False
    )
```

```python
import functools

import jax
import jax.numpy as jnp
from jax import lax
from jax.experimental import pallas as pl
from jax.experimental.pallas import tpu as pltpu
from jax.sharding import PartitionSpec as P

DK = 128
BLOCK = 128
epsilon = 1e-06
f32 = jnp.float32
bf16 = jnp.bfloat16

PARITY, CORE, ME, CHIP = 0, 1, 2, 3

VM = pl.BlockSpec(memory_space=pltpu.VMEM)
SM = pl.BlockSpec(memory_space=pltpu.SMEM)
ANY = pl.BlockSpec(memory_space=pl.ANY)


def params(mebibytes):
    return pltpu.CompilerParams(vmem_limit_bytes=mebibytes * 1024 * 1024)


def cost(flops, moved):
    return pl.CostEstimate(flops=flops, bytes_accessed=moved, transcendentals=0)


def shape_of(shape, dtype=bf16):
    return jax.ShapeDtypeStruct(shape, dtype)


def dot(a, b):
    return jnp.dot(a, b, preferred_element_type=f32)


def dot_nt(a, b):
    return lax.dot_general(a, b, (((1,), (1,)), ((), ())), preferred_element_type=f32)


def dot_tn(a, b):
    return lax.dot_general(a, b, (((0,), (0,)), ((), ())), preferred_element_type=f32)


def iotas(shape):
    return lax.broadcasted_iota(jnp.int32, shape, 0), lax.broadcasted_iota(jnp.int32, shape, 1)


def column_of(row, lanes=128):
    return jnp.broadcast_to(row, (lanes, row.shape[1])).T


def scale_pass(source, gain_at, target):
    features, tokens = source.shape
    squares = jnp.zeros((8, tokens), f32)
    for start in range(0, features, 128):
        size = min(128, features - start)
        value = source[start : start + size, :].astype(f32)
        scale = column_of(gain_at(start, size))
        scale = jnp.concatenate([scale] * (tokens // 128), axis=1)
        target[:, start : start + size] = (value * scale).astype(bf16).T
        value = value * value
        for r in range(0, size, 8):
            squares = squares + value[r : r + 8]
    return squares


def inverse_of(squares, features):
    return lax.rsqrt(jnp.sum(squares, axis=0, keepdims=True) / features + epsilon)


def fill_columns(row, target):
    for start in range(0, row.shape[1], 128):
        target[start : start + 128, :] = column_of(row[:, start : start + 128])


def doubled(tile):
    return jnp.concatenate([tile, tile], axis=1)


def slots_of(meta, n):
    return [meta[CORE], 1 - meta[CORE]] if n == 2 else [0]


def load_pair(meta, pieces, whole, sem):
    part = pieces[0].shape[0]
    copies = [
        pltpu.make_async_copy(
            piece, whole.at[pl.ds(pl.multiple_of(slot * part, 16), part)], sem.at[p]
        )
        for p, (piece, slot) in enumerate(zip(pieces, slots_of(meta, len(pieces))))
    ]
    for copy in copies:
        copy.start()
    for copy in copies:
        copy.wait()


def held_rows(meta, at, weights, held, sem):
    span = held.shape[1]
    rows = pl.ds(pl.multiple_of(meta[at] * span, 16), span)
    copies = [
        pltpu.make_async_copy(ref.at[rows], held.at[i], sem.at[i]) for i, ref in enumerate(weights)
    ]
    for copy in copies:
        copy.start()
    return copies


def early_kernel(count_in, at, meta, *refs):
    first = at == CHIP
    pieces = refs[:count_in]
    gain, gates, w_key, w_value, w_query, w_down, w_out = refs[count_in : count_in + 7]
    refs = refs[count_in + 7 :]
    before, refs = (None, refs) if first else (refs[:5], refs[5:])
    acc_k, acc_v, acc_q, acc_g, squares = refs[:5]
    sent, (whole, scaled, held, held_sem, sem) = (refs[5:8], refs[8:]) if first else ((), refs[5:])
    rows_copies = held_rows(meta, at, (w_key, w_value, w_query), held, held_sem)
    copies = []
    if first:
        partner_w, their_rows, my_rows = sent
        ys = partner_w.shape[0]
        copies = [
            pltpu.make_async_copy(
                w_down.at[2 * y + 1 - meta[CORE]], partner_w.at[y], sem.at[count_in + y]
            )
            for y in range(ys)
        ]
        for i, (start, target) in enumerate(
            (
                ((1 - meta[CORE]) * 2 * my_rows.shape[0], their_rows),
                ((2 * meta[CORE] + meta[PARITY]) * my_rows.shape[0], my_rows),
            )
        ):
            rows = pl.ds(pl.multiple_of(start, 16), target.shape[0])
            copies.append(
                pltpu.make_async_copy(w_out.at[rows], target, sem.at[count_in + ys + i])
            )
    for copy in copies:
        copy.start()
    load_pair(meta, pieces, whole, sem)
    sums = scale_pass(whole, lambda at, size: gain[:, at : at + size], scaled)
    gate = dot_nt(gates[...], scaled[...])
    squares[...] = sums if first else before[4][...] + sums
    acc_g[...] = gate if first else before[3][...] + gate
    for i, out in enumerate((acc_k, acc_v, acc_q)):
        rows_copies[i].wait()
        product = dot(scaled[...], held[i])
        out[...] = product if first else before[i][...] + product
    for copy in copies:
        copy.wait()


def early_project(meta, at, pieces, gain, gates, w_key, w_value, w_query, w_down, w_out, before):
    first = before is None
    blocks, part, hidden = w_down.shape
    ys = blocks // 2
    span = gain.shape[1]
    count = pieces[0].shape[1]
    features, inner = w_key.shape
    return pl.pallas_call(
        functools.partial(early_kernel, len(pieces), at),
        out_shape=[shape_of((count, inner), f32)] * 3
        + [shape_of((16, count), f32), shape_of((8, count), f32)]
        + [
            shape_of((ys, part, hidden)),
            shape_of((features // 2, inner)),
            shape_of((features // 4, inner)),
        ]
        * first,
        in_specs=[SM] + [ANY] * len(pieces) + [VM] * 2 + [ANY] * 5 + [VM] * (0 if first else 5),
        out_specs=[VM] * (8 if first else 5),
        scratch_shapes=[
            pltpu.VMEM((span, count), bf16),
            pltpu.VMEM((count, span), bf16),
            pltpu.VMEM((3, span, inner), bf16),
            pltpu.SemaphoreType.DMA((3,)),
            pltpu.SemaphoreType.DMA((len(pieces) + ys + 2,)),
        ],
        compiler_params=params(48),
        cost_estimate=cost(3 * 10**9, 8 * 10**6),
        name="early_project",
    )(meta, *pieces, gain, gates, w_key, w_value, w_query, w_down, w_out, *(before or ()))


def maps_kernel(n, heads, at, meta, *refs):
    pieces = refs[:n]
    gain, rates, gates, w_key, w_value, acc_k, acc_v, acc_g, squares = refs[n : n + 9]
    scaled, scale_b, keys, erased, entry, own, sent, totals = refs[n + 9 : n + 17]
    whole, raw_k, raw_v, rows_at_head, total_b, beta_b, held, held_sem, acc, acc_sem, sem = refs[
        n + 17 :
    ]
    span, count = whole.shape
    blocks = count // BLOCK
    inner = heads * DK
    features = w_key.shape[0]
    parity = meta[PARITY]
    rows_copies = held_rows(meta, at, (w_key, w_value), held, held_sem)
    rows_copies += [
        pltpu.make_async_copy(ref, acc.at[i], acc_sem.at[i]) for i, ref in enumerate((acc_k, acc_v))
    ]
    for copy in rows_copies[2:]:
        copy.start()
    load_pair(meta, pieces, whole, sem)
    sums = scale_pass(whole, lambda at, size: gain[:, at : at + size], scaled)
    inverse = inverse_of(sums + squares[...], features)
    fill_columns(inverse, scale_b)

    pre = (acc_g[...] + dot_nt(gates[...], scaled[...])) * inverse
    soft = jnp.maximum(pre, 0.0) + jnp.log1p(jnp.exp(-jnp.abs(pre)))
    rate = jnp.concatenate([rates[...]] * (count // 128), axis=1)
    decay = -rate * soft
    beta = jax.nn.sigmoid(pre + rate)
    row_at, col_at = iotas((BLOCK, BLOCK))
    upper = (row_at <= col_at).astype(f32)
    rows_at_head[...] = jnp.zeros_like(rows_at_head)
    for c in range(blocks):
        tokens = slice(c * BLOCK, (c + 1) * BLOCK)
        total = jnp.dot(
            decay[:, tokens], upper, precision=lax.Precision.HIGHEST, preferred_element_type=f32
        )
        totals[c] = total
        rows_at_head[0:16, :] = total
        rows_at_head[16:32, :] = beta[:, tokens]
        columns = rows_at_head[...].T
        for h in range(heads):
            total_b[h, tokens, :] = jnp.broadcast_to(columns[:, h : h + 1], (BLOCK, DK))
            lane = 16 + heads + h
            beta_b[h, tokens, :] = jnp.broadcast_to(columns[:, lane : lane + 1], (BLOCK, DK))

    for copy in rows_copies:
        copy.wait()
    for start in range(0, inner, 256):
        cols = slice(start, start + 256)
        scale = doubled(scale_b[...])
        raw_k[:, cols] = ((acc[0, :, cols] + dot(scaled[...], held[0, :, cols])) * scale).astype(bf16)
        raw_v[:, cols] = ((acc[1, :, cols] + dot(scaled[...], held[1, :, cols])) * scale).astype(bf16)

    xor = jnp.where(row_at > col_at, row_at ^ col_at, 0)
    eye = jnp.where(row_at == col_at, 1.0, 0.0)
    group = 2 if heads % 2 == 0 else 1

    @pl.loop(0, heads // group)
    def _(batch):
        lows, solved = [], []
        chains = []
        for g in range(group):
            h = batch * group + g
            cols = pl.ds(pl.multiple_of(h * DK, DK), DK)
            wide = pl.ds(pl.multiple_of(h * 2 * DK, 2 * DK), 2 * DK)
            raw = raw_k[:, cols].astype(f32)
            unit = raw * lax.rsqrt(jnp.sum(raw * raw, axis=1, keepdims=True) + epsilon)
            keys[:, cols] = unit.astype(bf16)
            for c in range(blocks):
                chains.append((h, cols, wide, c, slice(c * BLOCK, (c + 1) * BLOCK)))
        for h, cols, wide, c, rows in chains:
            k = keys[rows, cols]
            fade = jnp.exp(jnp.minimum(total_b[h, rows, :] - totals[c, pl.ds(h, 1), :], 0.0))
            low = jnp.where(xor > 0, beta_b[h, rows, :] * fade * dot_nt(k, k), 0.0)
            lows.append(low)
            solved.append(eye - jnp.where(xor == 1, low, 0.0))
        size = 2
        while size < BLOCK:
            mask = (xor >= size) & (xor < 2 * size)
            first = []
            for i in range(len(chains)):
                link = jnp.where(mask, lows[i], 0.0).astype(bf16)
                first.append(dot(link, solved[i].astype(bf16)).astype(bf16))
            solved = [
                solved[i] - dot(solved[i].astype(bf16), first[i]) for i in range(len(chains))
            ]
            size *= 2
        grown = []
        for i, (h, cols, wide, c, rows) in enumerate(chains):
            k = keys[rows, cols].astype(f32)
            t_col = total_b[h, rows, :]
            b_col = beta_b[h, rows, :]
            right = jnp.concatenate(
                [
                    (b_col * jnp.exp(t_col) * k).astype(bf16),
                    (b_col * raw_v[rows, cols].astype(f32)).astype(bf16),
                ],
                axis=1,
            )
            both = dot(solved[i].astype(bf16), right).astype(bf16)
            erased[rows, wide] = both
            t_end = t_col[BLOCK - 1 : BLOCK, :]
            faded = (jnp.exp(t_end - t_col) * k).astype(bf16)
            grown.append((jnp.exp(t_end), dot_tn(faded, both)))
        states = [None] * group
        for c in range(blocks):
            for g in range(group):
                h, cols, wide = chains[g * blocks][:3]
                end, product = grown[g * blocks + c]
                erase, write = product[:, :DK], product[:, DK:]
                if c == 0:
                    state = jnp.concatenate([end * eye - erase, write], axis=1)
                else:
                    step = dot(erase.astype(bf16), states[g].astype(bf16))
                    state = (
                        jnp.concatenate([end, end], axis=1) * states[g]
                        - step
                        + jnp.concatenate([jnp.zeros_like(write), write], axis=1)
                    )
                if c < blocks - 1:
                    entry[c, :, wide] = state.astype(bf16)
                states[g] = state
        for g in range(group):
            h = batch * group + g
            half = heads // 2
            mine = (h >= half) == (parity == 1)
            slot = lax.rem(h, half)

            @pl.when(mine)
            def _():
                own[slot] = states[g].astype(bf16)

            @pl.when(jnp.logical_not(mine))
            def _():
                sent[slot] = states[g].astype(bf16)


def block_maps(meta, at, pieces, gain, rates, gates, w_key, w_value, early):
    n = len(pieces)
    acc_k, acc_v, acc_q, acc_g, squares = early
    count = pieces[0].shape[1]
    span = gain.shape[1]
    inner = w_key.shape[1]
    heads = inner // DK
    blocks = count // BLOCK
    return pl.pallas_call(
        functools.partial(maps_kernel, n, heads, at),
        out_shape=(
            shape_of((count, span)),
            shape_of((count, DK), f32),
            shape_of((count, inner)),
            shape_of((count, 2 * inner)),
            shape_of((blocks - 1, DK, 2 * inner)),
            shape_of((heads // 2, DK, 2 * DK)),
            shape_of((heads // 2, DK, 2 * DK)),
            shape_of((blocks, 16, 128), f32),
        ),
        in_specs=[SM] + [ANY] * n + [VM] * 3 + [ANY] * 4 + [VM] * 2,
        out_specs=[VM] * 8,
        scratch_shapes=[
            pltpu.VMEM((span, count), bf16),
            pltpu.VMEM((count, inner), bf16),
            pltpu.VMEM((count, inner), bf16),
            pltpu.VMEM((128, BLOCK), f32),
            pltpu.VMEM((heads, count, DK), f32),
            pltpu.VMEM((heads, count, DK), f32),
            pltpu.VMEM((2, span, inner), bf16),
            pltpu.SemaphoreType.DMA((2,)),
            pltpu.VMEM((2, count, inner), f32),
            pltpu.SemaphoreType.DMA((2,)),
            pltpu.SemaphoreType.DMA((n,)),
        ],
        compiler_params=params(16),
        cost_estimate=cost(10 * 10**9, 14 * 10**6),
        name="block_maps",
    )(meta, *pieces, gain, rates, gates, w_key, w_value, acc_k, acc_v, acc_g, squares)


def query_kernel(n, ys, meta, scaled, scale_b, weights, acc, *refs):
    pieces, (query, tokens_a, tokens_b, done, held, sem) = refs[: n * ys], refs[n * ys :]
    (copy,) = held_rows(meta, CHIP + ys - 1, (weights,), held, sem)
    span = scaled.shape[1]
    part, count = pieces[0].shape
    for d in range(ys):
        for p, slot in enumerate(slots_of(meta, n)):
            piece = pieces[d * n + p]
            base = meta[CHIP + d] * span + slot * part
            step = part // 7

            @pl.loop(0, 7)
            def _(r):
                rows = pl.ds(pl.multiple_of(r * step, 8), step)
                target = pl.ds(pl.multiple_of(base + r * step, 8), step)
                tokens_a[target, :BLOCK] = piece[rows, :BLOCK]
                tokens_a[target, BLOCK:] = piece[rows, count - BLOCK :]
                tokens_b[target, :] = piece[rows, BLOCK : count - BLOCK]

    done[...] = jnp.zeros_like(done)
    copy.wait()
    for start in range(0, query.shape[1], 256):
        cols = slice(start, start + 256)
        product = acc[:, cols] + dot(scaled[...], held[0, :, cols])
        query[:, cols] = (product * doubled(scale_b[...])).astype(bf16)


def queries(meta, ys, scaled, scale_b, weights, acc, pieces):
    n = len(pieces) // ys
    features = weights.shape[0]
    count = acc.shape[0]
    return pl.pallas_call(
        functools.partial(query_kernel, n, ys),
        out_shape=(
            shape_of(acc.shape),
            shape_of((features, 2 * BLOCK)),
            shape_of((features, count - 2 * BLOCK)),
            shape_of((8, 128), f32),
        ),
        in_specs=[SM] + [VM] * 2 + [ANY] + [VM] * (1 + len(pieces)),
        out_specs=[VM] * 4,
        scratch_shapes=[
            pltpu.VMEM((1, scaled.shape[1], acc.shape[1]), bf16),
            pltpu.SemaphoreType.DMA((1,)),
        ],
        compiler_params=params(12),
        cost_estimate=cost(10**9, 8 * 10**6),
        name="queries",
    )(meta, scaled, scale_b, weights, acc, *pieces)


def outputs_kernel(heads, query, keys, erased, entry, totals, after, shard_query, free, done, rows_at_head):
    count = query.shape[0]
    blocks = count // BLOCK
    row_at, col_at = iotas((BLOCK, BLOCK))
    done[...] = jnp.zeros_like(done)
    rows_at_head[...] = jnp.zeros_like(rows_at_head)
    for c in range(blocks):
        rows = slice(c * BLOCK, (c + 1) * BLOCK)
        rows_at_head[0:16, :] = totals[c]
        columns = rows_at_head[...].T
        for h in range(heads):
            cols = slice(h * DK, (h + 1) * DK)
            wide = slice(h * 2 * DK, (h + 1) * 2 * DK)
            t_col = jnp.broadcast_to(columns[:, h : h + 1], (BLOCK, BLOCK))
            t_row = totals[c, h : h + 1, :]
            fade = jnp.where(row_at >= col_at, jnp.exp(jnp.minimum(t_col - t_row, 0.0)), 0.0)
            q = query[rows, cols]
            scores = (fade * dot_nt(q, keys[rows, cols])).astype(bf16)
            both = dot(scores, erased[rows, wide])
            reach = jnp.exp(t_col) * q.astype(f32) - both[:, :DK]
            local = both[:, DK:]
            if c > 0:
                product = dot(reach.astype(bf16), entry[c - 1, :, wide])
                reach = product[:, :DK]
                local = local + product[:, DK:]
            shard_query[rows, cols] = reach.astype(bf16)
            free[rows, cols] = local


def block_outputs(query, keys, erased, entry, totals, after):
    heads = query.shape[1] // DK
    return pl.pallas_call(
        functools.partial(outputs_kernel, heads),
        out_shape=(shape_of(query.shape), shape_of(query.shape, f32), shape_of((8, 128), f32)),
        in_specs=[VM] * 5 + [ANY],
        out_specs=[VM] * 3,
        scratch_shapes=[pltpu.VMEM((128, BLOCK), f32)],
        compiler_params=params(8),
        cost_estimate=cost(3 * 10**9, 4 * 10**6),
        name="block_outputs",
    )(query, keys, erased, entry, totals, after)


def pair_kernel(meta, own, other, after, pair, first, done):
    even = meta[PARITY] == 0
    for h in range(own.shape[0]):
        mine, theirs = own[h], other[h]
        early = jnp.where(even, mine, theirs)
        late = jnp.where(even, theirs, mine)
        product = dot(late[:, :DK], early)
        shift = late[:, DK:].astype(f32)
        pair[h] = (product + jnp.concatenate([jnp.zeros_like(shift), shift], axis=1)).astype(bf16)
        first[h] = early
    done[...] = jnp.zeros_like(done)


def pair_maps(meta, own, other, after):
    return pl.pallas_call(
        pair_kernel,
        out_shape=(shape_of(own.shape), shape_of(own.shape), shape_of((8, 128), f32)),
        in_specs=[SM, VM, VM, ANY],
        out_specs=[VM] * 3,
        compiler_params=params(4),
        name="pair_maps",
    )(meta, own, other, after)


def apply_map(whole, state):
    high = state.astype(bf16)
    low = (state - high.astype(f32)).astype(bf16)
    product = dot(whole[:, :DK], jnp.concatenate([high, low], axis=1))
    return product[:, :DK] + product[:, DK:] + whole[:, DK:].astype(f32)


def start_kernel(steps, meta, first, *refs):
    pairs, (after, keep, give) = refs[:steps], refs[steps:]
    even = meta[PARITY] == 0
    for h in range(first.shape[0]):
        state = pairs[0][h][:, DK:].astype(f32)
        for pair in pairs[1:]:
            state = apply_map(pair[h], state)
        later = apply_map(first[h], state)
        keep[h] = jnp.where(even, state, later).astype(bf16)
        give[h] = jnp.where(even, later, state).astype(bf16)


def start_states(meta, first, pairs, after):
    heads = first.shape[0]
    shape = shape_of((heads, DK, DK))
    return pl.pallas_call(
        functools.partial(start_kernel, len(pairs)),
        out_shape=(shape, shape),
        in_specs=[SM] + [VM] * (1 + len(pairs)) + [ANY],
        out_specs=[VM] * 2,
        compiler_params=params(4),
        name="start_states",
    )(meta, first, *pairs, after)


def mixed_kernel(heads, meta, own, other, shard_query, free, gain, mixed_a, mixed_b):
    even = meta[PARITY] == 0
    half = heads // 2
    blocks = shard_query.shape[0] // BLOCK
    for h in range(heads):
        cols = slice(h * DK, (h + 1) * DK)
        if h < half:
            state = jnp.where(even, own[h], other[h])
        else:
            state = jnp.where(even, other[h - half], own[h - half])
        for unit in range(blocks):
            rows = slice(unit * BLOCK, (unit + 1) * BLOCK)
            out = dot(shard_query[rows, cols], state) + free[rows, cols]
            scale = lax.rsqrt(jnp.mean(out * out, axis=1, keepdims=True) + epsilon)
            value = (out * scale * gain[...].astype(f32)).astype(bf16)
            if unit == 0:
                mixed_a[:BLOCK, cols] = value
            elif unit == blocks - 1:
                mixed_a[BLOCK:, cols] = value
            else:
                mixed_b[(unit - 1) * BLOCK : unit * BLOCK, cols] = value


def mixed_heads(meta, own, other, shard_query, free, gain):
    count, inner = shard_query.shape
    return pl.pallas_call(
        functools.partial(mixed_kernel, inner // DK),
        out_shape=(shape_of((2 * BLOCK, inner)), shape_of((count - 2 * BLOCK, inner))),
        in_specs=[SM] + [VM] * 5,
        out_specs=[VM] * 2,
        compiler_params=params(6),
        cost_estimate=cost(10**9, 3 * 10**6),
        name="mixed_heads",
    )(meta, own, other, shard_query, free, gain)


def attend_kernel(ys, meta, tokens, own, partner, weights, partner_weights, *refs):
    far, middle = refs[:-1], refs[-1]
    half = middle.shape[0]
    size = half // 2
    for i in range(2):
        quarter = meta[PARITY] if i == 0 else 1 - meta[PARITY]
        base = meta[CORE] * half + quarter * size
        here = pl.ds(pl.multiple_of(base, 16), size)
        rows = pl.ds(pl.multiple_of(quarter * size, 16), size)
        total = tokens[here, :].astype(f32)
        total = total + dot_nt(weights[here, :], own[...])
        total = total + dot_nt(partner_weights[rows, :], partner[...])
        for d in range(ys - 1):
            same, diagonal, fetched, swapped, far_weights = far[5 * d : 5 * d + 5]
            total = total + dot_nt((fetched if i == 0 else swapped)[...], same[...])
            total = total + dot_nt(far_weights[rows, :], diagonal[...])
        middle[rows, :] = total.astype(bf16)


def attend(meta, ys, tokens, own, partner, weights, partner_weights, far):
    return pl.pallas_call(
        functools.partial(attend_kernel, ys),
        out_shape=shape_of((weights.shape[0] // 2, own.shape[0])),
        in_specs=[SM] + [VM] * (5 + len(far)),
        out_specs=VM,
        compiler_params=params(12),
        cost_estimate=cost(2 * 10**9, 7 * 10**6),
        name="attend",
    )(meta, tokens, own, partner, weights, partner_weights, *far)


def up_kernel(meta, own, other, gain, weights, lifted, middle_part, first, last, middle, hidden, scale_b):
    features, count = middle.shape
    half = features // 2
    step = 160
    for side, source in ((meta[CORE], own), (1 - meta[CORE], other)):

        @pl.loop(0, half // step)
        def _(r):
            rows = pl.ds(pl.multiple_of(r * step, 32), step)
            target = pl.ds(pl.multiple_of(side * half + r * step, 32), step)
            middle[target, :] = source[rows, :].astype(f32)

    squares = scale_pass(middle, lambda at, size: gain[:, at : at + size], hidden)
    fill_columns(inverse_of(squares, features), scale_b)
    part = middle_part.shape[0]
    middle_part[...] = middle[pl.ds(pl.multiple_of(meta[ME] * part, 8), part), :]
    width = lifted.shape[1]
    for start in range(0, width, 256):
        size = min(256, width - start)
        cols = slice(start, start + size)
        scale = doubled(scale_b[...])[:, :size]
        lifted[:, cols] = (dot(hidden[...], weights[:, cols]) * scale).astype(bf16)
    first[...] = lifted[0:1, :]
    last[...] = lifted[count - 1 : count, :]


def up_project(meta, own, other, gain, weights, part):
    features, hidden = weights.shape
    count = own.shape[1]
    return pl.pallas_call(
        up_kernel,
        out_shape=(
            shape_of((count, hidden)),
            shape_of((part, count), f32),
            shape_of((1, hidden)),
            shape_of((1, hidden)),
        ),
        in_specs=[SM] + [VM] * 4,
        out_specs=[VM] * 4,
        scratch_shapes=[
            pltpu.VMEM((features, count), f32),
            pltpu.VMEM((count, features), bf16),
            pltpu.VMEM((count, DK), f32),
        ],
        compiler_params=params(16),
        cost_estimate=cost(2 * 10**9, 8 * 10**6),
        name="up_project",
    )(meta, own, other, gain, weights)


def gelu_of(x):
    inner = 0.7978845608028654 * (x + 0.044715 * (x * x * x))
    return 0.5 * x * (1.0 + jnp.tanh(inner))


def act_kernel(late, meta, outer, inside, before, after, taps, act_t, padded, act):
    count = act.shape[0]
    if late:
        padded[7:8, :] = inside[BLOCK - 1 : BLOCK, :].astype(f32)
        padded[8 : 8 + BLOCK, :] = inside[BLOCK:, :].astype(f32)
        padded[8 + BLOCK : 8 + count, :] = outer[BLOCK:, :].astype(f32)
        padded[8 + count : 9 + count, :] = after[...].astype(f32)
    else:
        padded[7:8, :] = before[...].astype(f32)
        padded[8 : 8 + BLOCK, :] = outer[:BLOCK, :].astype(f32)
        padded[8 + BLOCK : 8 + count, :] = inside[:BLOCK, :].astype(f32)
        padded[8 + count : 9 + count, :] = inside[BLOCK : BLOCK + 1, :].astype(f32)

    @pl.loop(0, count // 32)
    def _(r):
        base = pl.multiple_of(r * 32, 32)
        window = padded[pl.ds(base, 48), :]
        value = (
            taps[0:1, :] * window[7:39, :]
            + taps[1:2, :] * window[8:40, :]
            + taps[2:3, :] * window[9:41, :]
        )
        act[pl.ds(base, 32), :] = gelu_of(value).astype(bf16)

    act_t[...] = act[...].T


def activate(meta, outer, inside, before, after, taps, late):
    hidden = outer.shape[1]
    count = (outer.shape[0] + inside.shape[0]) // 2
    return pl.pallas_call(
        functools.partial(act_kernel, late),
        out_shape=shape_of((hidden, count)),
        in_specs=[SM] + [VM] * 5,
        out_specs=VM,
        scratch_shapes=[pltpu.VMEM((count + 16, hidden), f32), pltpu.VMEM((count, hidden), bf16)],
        compiler_params=params(8),
        cost_estimate=cost(10**9, 2 * 10**6),
        name="activate",
    )(meta, outer, inside, before, after, taps)


def far_kernel(ys, meta, own, other, weights, other_weights, *outs):
    for i, out in enumerate(outs):
        chip = meta[CHIP + ys + i]
        block = 2 * chip + meta[CORE]
        total = dot(weights[block], own[...]) + dot(other_weights[chip], other[...])
        out[...] = total.astype(bf16)


def far_project(meta, ys, own, other, weights, other_weights):
    part = weights.shape[1]
    return pl.pallas_call(
        functools.partial(far_kernel, ys),
        out_shape=[shape_of((part, own.shape[1]))] * (ys - 1),
        in_specs=[SM] + [VM] * 4,
        out_specs=[VM] * (ys - 1),
        compiler_params=params(8),
        cost_estimate=cost(10**9, 4 * 10**6),
        name="far_project",
    )(meta, own, other, weights, other_weights)


def near_kernel(meta, own_a, other_a, own_b, other_b, middle_a, middle_b, weights, other_weights, after, base):
    size = own_a.shape[1]
    middle = (
        jnp.concatenate([middle_a[:, :BLOCK], middle_b[:, :BLOCK]], axis=1),
        jnp.concatenate([middle_b[:, BLOCK:], middle_a[:, BLOCK:]], axis=1),
    )
    for i, (own, other) in enumerate(((own_a, other_a), (own_b, other_b))):
        total = dot(weights[meta[ME]], own[...])
        total = total + dot(other_weights[meta[CHIP]], other[...])
        base[:, i * size : (i + 1) * size] = total + middle[i]


def near_project(meta, own, other, middle_a, middle_b, weights, other_weights, after):
    part = weights.shape[1]
    return pl.pallas_call(
        near_kernel,
        out_shape=shape_of((part, 2 * own[0].shape[1]), f32),
        in_specs=[SM] + [VM] * 8 + [ANY],
        out_specs=VM,
        compiler_params=params(10),
        cost_estimate=cost(2 * 10**9, 6 * 10**6),
        name="near_project",
    )(meta, own[0], other[0], own[1], other[1], middle_a, middle_b, weights, other_weights, after)


def core_swap(value, n):
    return lax.ppermute(value, "head", [(i, i ^ 1) for i in range(n)])


def y_shift(value, n, step):
    return lax.ppermute(value, "head", [(i, (i + 2 * step) % n) for i in range(n)])


def pair_swap(value, n):
    return lax.ppermute(value, "seq", [(i, i ^ 1) for i in range(n)])


def later(value, n, step):
    return lax.ppermute(value, "seq", [(i, i + 2 * step) for i in range(n - 2 * step)])


def shards(
    tokens,
    norm_gain,
    w_query,
    w_key,
    w_value,
    w_decay,
    w_beta,
    head_rates,
    head_gain,
    w_out,
    ffn_gain,
    w_up,
    conv_taps,
    w_down,
):
    n = lax.axis_size("head")
    seqs = lax.axis_size("seq")
    me = lax.axis_index("head")
    at = lax.axis_index("seq")
    core = me % 2
    parity = at % 2
    ys = n // 2
    count, part = tokens.shape
    heads = w_query.shape[1] // DK
    hidden = w_up.shape[1]
    features = n * part

    mine = tokens.T
    shifted = [mine] + [y_shift(mine, n, d) for d in range(1, ys)]

    def group_of(piece):
        partner = core_swap(piece, n)
        if part % 16:
            first = jnp.where(core == 0, piece, partner)
            second = jnp.where(core == 0, partner, piece)
            return [jnp.concatenate([first, second], axis=0)]
        return [piece, partner]

    groups = [group_of(mine)]
    chip = me // 2
    here = [parity, core, me]
    sources = [(chip + ys - d) % ys for d in range(ys)]
    targets = [(chip + d) % ys for d in range(1, ys)]
    meta = jnp.stack(here + sources + targets).astype(jnp.int32)

    w_out_t = w_out.T
    w_parts = w_down.T.reshape(n, part, hidden)

    gates = jnp.concatenate([w_decay.T, w_beta.T], axis=0)
    gates = jnp.pad(gates, ((0, 16 - 2 * heads), (0, 0)))
    gates = gates.reshape(16, ys, 2 * part).transpose(1, 0, 2)
    rates = jnp.pad(head_rates.reshape(2 * heads, 1), ((0, 16 - 2 * heads), (0, 0)))
    rates = jnp.broadcast_to(rates, (16, 128))
    gain = norm_gain.astype(f32).reshape(ys, 1, 2 * part)

    def ours(rows, d):
        return lax.dynamic_index_in_dim(rows, sources[d], 0, False)

    ffn_scale = ffn_gain.astype(f32).reshape(1, features)
    taps = conv_taps.astype(f32)

    gains = [ours(gain, d) for d in range(ys)]
    gate_rows = [ours(gates, d) for d in range(ys)]
    gains, gate_rows, rates, taps, ffn_scale, head_scale, meta = lax.optimization_barrier(
        (gains, gate_rows, rates, taps, ffn_scale, head_gain.reshape(1, DK), meta)
    )

    early = None
    for d in range(ys - 1):
        early = early_project(
            meta, CHIP + d, groups[d], gains[d], gate_rows[d], w_key, w_value, w_query, w_parts, w_out_t, early
        )
        if d == 0:
            sent, early = early[5:], early[:5]
        piece, _ = lax.optimization_barrier((shifted[d + 1], early[4]))
        groups.append(group_of(piece))
    scaled, scale_b, keys, erased, entry, own_maps, sent_maps, totals = block_maps(
        meta, CHIP + ys - 1, groups[-1], gains[-1], rates, gate_rows[-1], w_key, w_value, early
    )

    sent, _ = lax.optimization_barrier((sent, groups[-1][-1]))
    sent_w_down, their_rows, my_rows = sent
    other_w_down = core_swap(sent_w_down, n)
    fetched = [y_shift(my_rows, n, d) for d in range(1, ys)]
    partner_w_out = core_swap(their_rows, n)
    acc_query, partner_w_out, other_w_down = lax.optimization_barrier(
        (early[2], partner_w_out, other_w_down)
    )
    their_rows, fetched, _ = lax.optimization_barrier((their_rows, fetched, totals))
    diagonal = [
        lax.ppermute(their_rows, "head", [(i, ((i + 2 * d) % n) ^ 1) for i in range(n)])
        for d in range(1, ys)
    ]

    other_maps = pair_swap(sent_maps, seqs)
    query, tokens_a, tokens_b, query_done = queries(
        meta, ys, scaled, scale_b, w_query, acc_query, sum(groups, [])
    )
    pair, first, done = pair_maps(meta, own_maps, other_maps, query_done)
    fetched, _ = lax.optimization_barrier((fetched, done))
    swapped = [pair_swap(value, seqs) for value in fetched]
    pairs = [later(pair, seqs, d) for d in range(seqs // 2 - 1, 0, -1)]
    shard_query, free, out_done = block_outputs(query, keys, erased, entry, totals, done)
    kept_state, given_state = start_states(meta, first, pairs, out_done)
    other_state = pair_swap(given_state, seqs)

    other_state, swapped, diagonal = lax.optimization_barrier((other_state, swapped, diagonal))
    mixed = mixed_heads(meta, kept_state, other_state, shard_query, free, head_scale)
    far_mixed = [[y_shift(value, n, d) for d in range(1, ys)] for value in mixed]

    def middle_of(i, far):
        heads_far = [[value, core_swap(value, n)] for value in far]
        operands = []
        for pair_of, *weights in zip(heads_far, fetched, swapped, diagonal):
            operands += pair_of + weights
        own_tokens = (tokens_a, tokens_b)[i]
        return attend(
            meta, ys, own_tokens, mixed[i], core_swap(mixed[i], n), w_out_t, partner_w_out, operands
        )

    middle = middle_of(0, far_mixed[0])
    outer, middle_a, first_row, last_row = up_project(
        meta, middle, core_swap(middle, n), ffn_scale, w_up, part
    )
    before = lax.ppermute(last_row, "seq", [(i, i + 1) for i in range(seqs - 1)])
    after = lax.ppermute(first_row, "seq", [(i + 1, i) for i in range(seqs - 1)])
    middle = middle_of(1, far_mixed[1])
    inside, middle_b, _, _ = up_project(
        meta, middle, core_swap(middle, n), ffn_scale, w_up, part
    )

    acts = [activate(meta, outer, inside, before, after, taps, late) for late in (False, True)]
    partner_acts = [core_swap(act, n) for act in acts]
    fars = [
        far_project(meta, ys, act, partner, w_parts, other_w_down)
        for act, partner in zip(acts, partner_acts)
    ]
    total = near_project(
        meta, acts, partner_acts, middle_a, middle_b, w_parts, other_w_down, fars[1][0]
    )
    for d in range(1, ys):
        halves = [y_shift(far[d - 1], n, d) for far in fars]
        total = total + jnp.concatenate(halves, axis=1).astype(f32)
    return total.astype(bf16).T


def solution(mesh):
    placed = (
        P("seq", "head"),
        P(),
        P(None, "head"),
        P(None, "head"),
        P(None, "head"),
        P(None, "head"),
        P(None, "head"),
        P(None, "head"),
        P(),
        P("head", None),
        P(),
        P(None, "head"),
        P(None, "head"),
        P("head", None),
    )
    return jax.shard_map(
        shards, mesh=mesh, in_specs=placed, out_specs=P("seq", "head"), check_vma=False
    )
```

```python
import functools

import jax
import jax.numpy as jnp
from jax import lax
from jax.experimental import pallas as pl
from jax.experimental.pallas import tpu as pltpu
from jax.sharding import PartitionSpec as P

DK = 128
BLOCK = 128
epsilon = 1e-06
f32 = jnp.float32
bf16 = jnp.bfloat16

PARITY, CORE, ME, CHIP = 0, 1, 2, 3

VM = pl.BlockSpec(memory_space=pltpu.VMEM)
SM = pl.BlockSpec(memory_space=pltpu.SMEM)
ANY = pl.BlockSpec(memory_space=pl.ANY)


def params(mebibytes):
    return pltpu.CompilerParams(vmem_limit_bytes=mebibytes * 1024 * 1024)


def cost(flops, moved):
    return pl.CostEstimate(flops=flops, bytes_accessed=moved, transcendentals=0)


def shape_of(shape, dtype=bf16):
    return jax.ShapeDtypeStruct(shape, dtype)


def dot(a, b):
    return jnp.dot(a, b, preferred_element_type=f32)


def dot_nt(a, b):
    return lax.dot_general(a, b, (((1,), (1,)), ((), ())), preferred_element_type=f32)


def dot_tn(a, b):
    return lax.dot_general(a, b, (((0,), (0,)), ((), ())), preferred_element_type=f32)


def iotas(shape):
    return lax.broadcasted_iota(jnp.int32, shape, 0), lax.broadcasted_iota(jnp.int32, shape, 1)


def column_of(row, lanes=128):
    return jnp.broadcast_to(row, (lanes, row.shape[1])).T


def scale_pass(source, gain_at, target):
    features, tokens = source.shape
    squares = jnp.zeros((8, tokens), f32)
    for start in range(0, features, 128):
        size = min(128, features - start)
        value = source[start : start + size, :].astype(f32)
        scale = column_of(gain_at(start, size))
        scale = jnp.concatenate([scale] * (tokens // 128), axis=1)
        target[:, start : start + size] = (value * scale).astype(bf16).T
        value = value * value
        for r in range(0, size, 8):
            squares = squares + value[r : r + 8]
    return squares


def inverse_of(squares, features):
    return lax.rsqrt(jnp.sum(squares, axis=0, keepdims=True) / features + epsilon)


def fill_columns(row, target):
    for start in range(0, row.shape[1], 128):
        target[start : start + 128, :] = column_of(row[:, start : start + 128])


def doubled(tile):
    return jnp.concatenate([tile, tile], axis=1)


def slots_of(meta, n):
    return [meta[CORE], 1 - meta[CORE]] if n == 2 else [0]


def load_pair(meta, pieces, whole, sem):
    part = pieces[0].shape[0]
    copies = [
        pltpu.make_async_copy(
            piece, whole.at[pl.ds(pl.multiple_of(slot * part, 16), part)], sem.at[p]
        )
        for p, (piece, slot) in enumerate(zip(pieces, slots_of(meta, len(pieces))))
    ]
    for copy in copies:
        copy.start()
    for copy in copies:
        copy.wait()


def held_rows(meta, at, weights, held, sem):
    span = held.shape[1]
    rows = pl.ds(pl.multiple_of(meta[at] * span, 16), span)
    copies = [
        pltpu.make_async_copy(ref.at[rows], held.at[i], sem.at[i]) for i, ref in enumerate(weights)
    ]
    for copy in copies:
        copy.start()
    return copies


def early_kernel(count_in, at, meta, *refs):
    first = at == CHIP
    pieces = refs[:count_in]
    gain, gates, w_key, w_value, w_query, w_down, w_out = refs[count_in : count_in + 7]
    refs = refs[count_in + 7 :]
    before, refs = (None, refs) if first else (refs[:5], refs[5:])
    acc_k, acc_v, acc_q, acc_g, squares = refs[:5]
    sent, (whole, scaled, held, held_sem, sem) = (refs[5:8], refs[8:]) if first else ((), refs[5:])
    rows_copies = held_rows(meta, at, (w_key, w_value, w_query), held, held_sem)
    copies = []
    if first:
        partner_w, their_rows, my_rows = sent
        ys = partner_w.shape[0]
        copies = [
            pltpu.make_async_copy(
                w_down.at[2 * y + 1 - meta[CORE]], partner_w.at[y], sem.at[count_in + y]
            )
            for y in range(ys)
        ]
        for i, (start, target) in enumerate(
            (
                ((1 - meta[CORE]) * 2 * my_rows.shape[0], their_rows),
                ((2 * meta[CORE] + meta[PARITY]) * my_rows.shape[0], my_rows),
            )
        ):
            rows = pl.ds(pl.multiple_of(start, 16), target.shape[0])
            copies.append(
                pltpu.make_async_copy(w_out.at[rows], target, sem.at[count_in + ys + i])
            )
    for copy in copies:
        copy.start()
    load_pair(meta, pieces, whole, sem)
    sums = scale_pass(whole, lambda at, size: gain[:, at : at + size], scaled)
    gate = dot_nt(gates[...], scaled[...])
    squares[...] = sums if first else before[4][...] + sums
    acc_g[...] = gate if first else before[3][...] + gate
    for i, out in enumerate((acc_k, acc_v, acc_q)):
        rows_copies[i].wait()
        product = dot(scaled[...], held[i])
        out[...] = product if first else before[i][...] + product
    for copy in copies:
        copy.wait()


def early_project(meta, at, pieces, gain, gates, w_key, w_value, w_query, w_down, w_out, before):
    first = before is None
    blocks, part, hidden = w_down.shape
    ys = blocks // 2
    span = gain.shape[1]
    count = pieces[0].shape[1]
    features, inner = w_key.shape
    return pl.pallas_call(
        functools.partial(early_kernel, len(pieces), at),
        out_shape=[shape_of((count, inner), f32)] * 3
        + [shape_of((16, count), f32), shape_of((8, count), f32)]
        + [
            shape_of((ys, part, hidden)),
            shape_of((features // 2, inner)),
            shape_of((features // 4, inner)),
        ]
        * first,
        in_specs=[SM] + [ANY] * len(pieces) + [VM] * 2 + [ANY] * 5 + [VM] * (0 if first else 5),
        out_specs=[VM] * (8 if first else 5),
        scratch_shapes=[
            pltpu.VMEM((span, count), bf16),
            pltpu.VMEM((count, span), bf16),
            pltpu.VMEM((3, span, inner), bf16),
            pltpu.SemaphoreType.DMA((3,)),
            pltpu.SemaphoreType.DMA((len(pieces) + ys + 2,)),
        ],
        compiler_params=params(48),
        cost_estimate=cost(3 * 10**9, 8 * 10**6),
        name="early_project",
    )(meta, *pieces, gain, gates, w_key, w_value, w_query, w_down, w_out, *(before or ()))


def maps_kernel(n, heads, at, meta, *refs):
    pieces = refs[:n]
    gain, rates, gates, w_key, w_value, acc_k, acc_v, acc_g, squares = refs[n : n + 9]
    scaled, scale_b, keys, erased, entry, own, sent, totals = refs[n + 9 : n + 17]
    whole, raw_k, raw_v, rows_at_head, total_b, beta_b, held, held_sem, acc, acc_sem, sem = refs[
        n + 17 :
    ]
    span, count = whole.shape
    blocks = count // BLOCK
    inner = heads * DK
    features = w_key.shape[0]
    parity = meta[PARITY]
    rows_copies = held_rows(meta, at, (w_key, w_value), held, held_sem)
    rows_copies += [
        pltpu.make_async_copy(ref, acc.at[i], acc_sem.at[i]) for i, ref in enumerate((acc_k, acc_v))
    ]
    for copy in rows_copies[2:]:
        copy.start()
    load_pair(meta, pieces, whole, sem)
    sums = scale_pass(whole, lambda at, size: gain[:, at : at + size], scaled)
    inverse = inverse_of(sums + squares[...], features)
    fill_columns(inverse, scale_b)

    pre = (acc_g[...] + dot_nt(gates[...], scaled[...])) * inverse
    soft = jnp.maximum(pre, 0.0) + jnp.log1p(jnp.exp(-jnp.abs(pre)))
    rate = jnp.concatenate([rates[...]] * (count // 128), axis=1)
    decay = -rate * soft
    beta = jax.nn.sigmoid(pre + rate)
    row_at, col_at = iotas((BLOCK, BLOCK))
    upper = (row_at <= col_at).astype(f32)
    rows_at_head[...] = jnp.zeros_like(rows_at_head)
    for c in range(blocks):
        tokens = slice(c * BLOCK, (c + 1) * BLOCK)
        total = jnp.dot(
            decay[:, tokens], upper, precision=lax.Precision.HIGHEST, preferred_element_type=f32
        )
        totals[c] = total
        rows_at_head[0:16, :] = total
        rows_at_head[16:32, :] = beta[:, tokens]
        columns = rows_at_head[...].T
        for h in range(heads):
            total_b[h, tokens, :] = jnp.broadcast_to(columns[:, h : h + 1], (BLOCK, DK))
            lane = 16 + heads + h
            beta_b[h, tokens, :] = jnp.broadcast_to(columns[:, lane : lane + 1], (BLOCK, DK))

    for copy in rows_copies:
        copy.wait()
    for start in range(0, inner, 256):
        cols = slice(start, start + 256)
        scale = doubled(scale_b[...])
        raw_k[:, cols] = ((acc[0, :, cols] + dot(scaled[...], held[0, :, cols])) * scale).astype(bf16)
        raw_v[:, cols] = ((acc[1, :, cols] + dot(scaled[...], held[1, :, cols])) * scale).astype(bf16)

    xor = jnp.where(row_at > col_at, row_at ^ col_at, 0)
    eye = jnp.where(row_at == col_at, 1.0, 0.0)
    group = 2 if heads % 2 == 0 else 1

    @pl.loop(0, heads // group)
    def _(batch):
        lows, solved = [], []
        chains = []
        for g in range(group):
            h = batch * group + g
            cols = pl.ds(pl.multiple_of(h * DK, DK), DK)
            wide = pl.ds(pl.multiple_of(h * 2 * DK, 2 * DK), 2 * DK)
            raw = raw_k[:, cols].astype(f32)
            unit = raw * lax.rsqrt(jnp.sum(raw * raw, axis=1, keepdims=True) + epsilon)
            keys[:, cols] = unit.astype(bf16)
            for c in range(blocks):
                chains.append((h, cols, wide, c, slice(c * BLOCK, (c + 1) * BLOCK)))
        for h, cols, wide, c, rows in chains:
            k = keys[rows, cols]
            fade = jnp.exp(jnp.minimum(total_b[h, rows, :] - totals[c, pl.ds(h, 1), :], 0.0))
            low = jnp.where(xor > 0, beta_b[h, rows, :] * fade * dot_nt(k, k), 0.0)
            lows.append(low)
            solved.append(eye - jnp.where(xor == 1, low, 0.0))
        size = 2
        while size < BLOCK:
            mask = (xor >= size) & (xor < 2 * size)
            first = []
            for i in range(len(chains)):
                link = jnp.where(mask, lows[i], 0.0).astype(bf16)
                first.append(dot(link, solved[i].astype(bf16)).astype(bf16))
            solved = [
                solved[i] - dot(solved[i].astype(bf16), first[i]) for i in range(len(chains))
            ]
            size *= 2
        grown = []
        for i, (h, cols, wide, c, rows) in enumerate(chains):
            k = keys[rows, cols].astype(f32)
            t_col = total_b[h, rows, :]
            b_col = beta_b[h, rows, :]
            right = jnp.concatenate(
                [
                    (b_col * jnp.exp(t_col) * k).astype(bf16),
                    (b_col * raw_v[rows, cols].astype(f32)).astype(bf16),
                ],
                axis=1,
            )
            both = dot(solved[i].astype(bf16), right).astype(bf16)
            erased[rows, wide] = both
            t_end = t_col[BLOCK - 1 : BLOCK, :]
            faded = (jnp.exp(t_end - t_col) * k).astype(bf16)
            grown.append((jnp.exp(t_end), dot_tn(faded, both)))
        states = [None] * group
        for c in range(blocks):
            for g in range(group):
                h, cols, wide = chains[g * blocks][:3]
                end, product = grown[g * blocks + c]
                erase, write = product[:, :DK], product[:, DK:]
                if c == 0:
                    state = jnp.concatenate([end * eye - erase, write], axis=1)
                else:
                    step = dot(erase.astype(bf16), states[g].astype(bf16))
                    state = (
                        jnp.concatenate([end, end], axis=1) * states[g]
                        - step
                        + jnp.concatenate([jnp.zeros_like(write), write], axis=1)
                    )
                if c < blocks - 1:
                    entry[c, :, wide] = state.astype(bf16)
                states[g] = state
        for g in range(group):
            h = batch * group + g
            half = heads // 2
            mine = (h >= half) == (parity == 1)
            slot = lax.rem(h, half)

            @pl.when(mine)
            def _():
                own[slot] = states[g].astype(bf16)

            @pl.when(jnp.logical_not(mine))
            def _():
                sent[slot] = states[g].astype(bf16)


def block_maps(meta, at, pieces, gain, rates, gates, w_key, w_value, early):
    n = len(pieces)
    acc_k, acc_v, acc_q, acc_g, squares = early
    count = pieces[0].shape[1]
    span = gain.shape[1]
    inner = w_key.shape[1]
    heads = inner // DK
    blocks = count // BLOCK
    return pl.pallas_call(
        functools.partial(maps_kernel, n, heads, at),
        out_shape=(
            shape_of((count, span)),
            shape_of((count, DK), f32),
            shape_of((count, inner)),
            shape_of((count, 2 * inner)),
            shape_of((blocks - 1, DK, 2 * inner)),
            shape_of((heads // 2, DK, 2 * DK)),
            shape_of((heads // 2, DK, 2 * DK)),
            shape_of((blocks, 16, 128), f32),
        ),
        in_specs=[SM] + [ANY] * n + [VM] * 3 + [ANY] * 4 + [VM] * 2,
        out_specs=[VM] * 8,
        scratch_shapes=[
            pltpu.VMEM((span, count), bf16),
            pltpu.VMEM((count, inner), bf16),
            pltpu.VMEM((count, inner), bf16),
            pltpu.VMEM((128, BLOCK), f32),
            pltpu.VMEM((heads, count, DK), f32),
            pltpu.VMEM((heads, count, DK), f32),
            pltpu.VMEM((2, span, inner), bf16),
            pltpu.SemaphoreType.DMA((2,)),
            pltpu.VMEM((2, count, inner), f32),
            pltpu.SemaphoreType.DMA((2,)),
            pltpu.SemaphoreType.DMA((n,)),
        ],
        compiler_params=params(16),
        cost_estimate=cost(10 * 10**9, 14 * 10**6),
        name="block_maps",
    )(meta, *pieces, gain, rates, gates, w_key, w_value, acc_k, acc_v, acc_g, squares)


def query_kernel(n, ys, meta, scaled, scale_b, weights, acc, *refs):
    pieces, (query, tokens_a, tokens_b, done, held, sem) = refs[: n * ys], refs[n * ys :]
    (copy,) = held_rows(meta, CHIP + ys - 1, (weights,), held, sem)
    span = scaled.shape[1]
    part, count = pieces[0].shape
    for d in range(ys):
        for p, slot in enumerate(slots_of(meta, n)):
            piece = pieces[d * n + p]
            base = meta[CHIP + d] * span + slot * part
            step = part // 7

            @pl.loop(0, 7)
            def _(r):
                rows = pl.ds(pl.multiple_of(r * step, 8), step)
                target = pl.ds(pl.multiple_of(base + r * step, 8), step)
                tokens_a[target, :BLOCK] = piece[rows, :BLOCK]
                tokens_a[target, BLOCK:] = piece[rows, count - BLOCK :]
                tokens_b[target, :] = piece[rows, BLOCK : count - BLOCK]

    done[...] = jnp.zeros_like(done)
    copy.wait()
    for start in range(0, query.shape[1], 256):
        cols = slice(start, start + 256)
        product = acc[:, cols] + dot(scaled[...], held[0, :, cols])
        query[:, cols] = (product * doubled(scale_b[...])).astype(bf16)


def queries(meta, ys, scaled, scale_b, weights, acc, pieces):
    n = len(pieces) // ys
    features = weights.shape[0]
    count = acc.shape[0]
    return pl.pallas_call(
        functools.partial(query_kernel, n, ys),
        out_shape=(
            shape_of(acc.shape),
            shape_of((features, 2 * BLOCK)),
            shape_of((features, count - 2 * BLOCK)),
            shape_of((8, 128), f32),
        ),
        in_specs=[SM] + [VM] * 2 + [ANY] + [VM] * (1 + len(pieces)),
        out_specs=[VM] * 4,
        scratch_shapes=[
            pltpu.VMEM((1, scaled.shape[1], acc.shape[1]), bf16),
            pltpu.SemaphoreType.DMA((1,)),
        ],
        compiler_params=params(12),
        cost_estimate=cost(10**9, 8 * 10**6),
        name="queries",
    )(meta, scaled, scale_b, weights, acc, *pieces)


def outputs_kernel(heads, query, keys, erased, entry, totals, after, shard_query, free, done, rows_at_head):
    count = query.shape[0]
    blocks = count // BLOCK
    row_at, col_at = iotas((BLOCK, BLOCK))
    done[...] = jnp.zeros_like(done)
    rows_at_head[...] = jnp.zeros_like(rows_at_head)
    for c in range(blocks):
        rows = slice(c * BLOCK, (c + 1) * BLOCK)
        rows_at_head[0:16, :] = totals[c]
        columns = rows_at_head[...].T
        for h in range(heads):
            cols = slice(h * DK, (h + 1) * DK)
            wide = slice(h * 2 * DK, (h + 1) * 2 * DK)
            t_col = jnp.broadcast_to(columns[:, h : h + 1], (BLOCK, BLOCK))
            t_row = totals[c, h : h + 1, :]
            fade = jnp.where(row_at >= col_at, jnp.exp(jnp.minimum(t_col - t_row, 0.0)), 0.0)
            q = query[rows, cols]
            scores = (fade * dot_nt(q, keys[rows, cols])).astype(bf16)
            both = dot(scores, erased[rows, wide])
            reach = jnp.exp(t_col) * q.astype(f32) - both[:, :DK]
            local = both[:, DK:]
            if c > 0:
                product = dot(reach.astype(bf16), entry[c - 1, :, wide])
                reach = product[:, :DK]
                local = local + product[:, DK:]
            shard_query[rows, cols] = reach.astype(bf16)
            free[rows, cols] = local


def block_outputs(query, keys, erased, entry, totals, after):
    heads = query.shape[1] // DK
    return pl.pallas_call(
        functools.partial(outputs_kernel, heads),
        out_shape=(shape_of(query.shape), shape_of(query.shape, f32), shape_of((8, 128), f32)),
        in_specs=[VM] * 5 + [ANY],
        out_specs=[VM] * 3,
        scratch_shapes=[pltpu.VMEM((128, BLOCK), f32)],
        compiler_params=params(8),
        cost_estimate=cost(3 * 10**9, 4 * 10**6),
        name="block_outputs",
    )(query, keys, erased, entry, totals, after)


def pair_kernel(meta, own, other, pair, first, done):
    even = meta[PARITY] == 0
    for h in range(own.shape[0]):
        mine, theirs = own[h], other[h]
        early = jnp.where(even, mine, theirs)
        late = jnp.where(even, theirs, mine)
        product = dot(late[:, :DK], early)
        shift = late[:, DK:].astype(f32)
        pair[h] = (product + jnp.concatenate([jnp.zeros_like(shift), shift], axis=1)).astype(bf16)
        first[h] = early
    done[...] = jnp.zeros_like(done)


def pair_maps(meta, own, other):
    return pl.pallas_call(
        pair_kernel,
        out_shape=(shape_of(own.shape), shape_of(own.shape), shape_of((8, 128), f32)),
        in_specs=[SM, VM, VM],
        out_specs=[VM] * 3,
        compiler_params=params(4),
        name="pair_maps",
    )(meta, own, other)


def apply_map(whole, state):
    high = state.astype(bf16)
    low = (state - high.astype(f32)).astype(bf16)
    product = dot(whole[:, :DK], jnp.concatenate([high, low], axis=1))
    return product[:, :DK] + product[:, DK:] + whole[:, DK:].astype(f32)


def start_kernel(steps, meta, first, *refs):
    pairs, (after, keep, give) = refs[:steps], refs[steps:]
    even = meta[PARITY] == 0
    for h in range(first.shape[0]):
        state = pairs[0][h][:, DK:].astype(f32)
        for pair in pairs[1:]:
            state = apply_map(pair[h], state)
        later = apply_map(first[h], state)
        keep[h] = jnp.where(even, state, later).astype(bf16)
        give[h] = jnp.where(even, later, state).astype(bf16)


def start_states(meta, first, pairs, after):
    heads = first.shape[0]
    shape = shape_of((heads, DK, DK))
    return pl.pallas_call(
        functools.partial(start_kernel, len(pairs)),
        out_shape=(shape, shape),
        in_specs=[SM] + [VM] * (1 + len(pairs)) + [ANY],
        out_specs=[VM] * 2,
        compiler_params=params(4),
        name="start_states",
    )(meta, first, *pairs, after)


def mixed_kernel(heads, meta, own, other, shard_query, free, gain, mixed_a, mixed_b):
    even = meta[PARITY] == 0
    half = heads // 2
    blocks = shard_query.shape[0] // BLOCK
    for h in range(heads):
        cols = slice(h * DK, (h + 1) * DK)
        if h < half:
            state = jnp.where(even, own[h], other[h])
        else:
            state = jnp.where(even, other[h - half], own[h - half])
        for unit in range(blocks):
            rows = slice(unit * BLOCK, (unit + 1) * BLOCK)
            out = dot(shard_query[rows, cols], state) + free[rows, cols]
            scale = lax.rsqrt(jnp.mean(out * out, axis=1, keepdims=True) + epsilon)
            value = (out * scale * gain[...].astype(f32)).astype(bf16)
            if unit == 0:
                mixed_a[:BLOCK, cols] = value
            elif unit == blocks - 1:
                mixed_a[BLOCK:, cols] = value
            else:
                mixed_b[(unit - 1) * BLOCK : unit * BLOCK, cols] = value


def mixed_heads(meta, own, other, shard_query, free, gain):
    count, inner = shard_query.shape
    return pl.pallas_call(
        functools.partial(mixed_kernel, inner // DK),
        out_shape=(shape_of((2 * BLOCK, inner)), shape_of((count - 2 * BLOCK, inner))),
        in_specs=[SM] + [VM] * 5,
        out_specs=[VM] * 2,
        compiler_params=params(6),
        cost_estimate=cost(10**9, 3 * 10**6),
        name="mixed_heads",
    )(meta, own, other, shard_query, free, gain)


def attend_kernel(ys, meta, tokens, own, partner, weights, partner_weights, *refs):
    far, middle = refs[:-1], refs[-1]
    half = middle.shape[0]
    size = half // 2
    for i in range(2):
        quarter = meta[PARITY] if i == 0 else 1 - meta[PARITY]
        base = meta[CORE] * half + quarter * size
        here = pl.ds(pl.multiple_of(base, 16), size)
        rows = pl.ds(pl.multiple_of(quarter * size, 16), size)
        total = tokens[here, :].astype(f32)
        total = total + dot_nt(weights[here, :], own[...])
        total = total + dot_nt(partner_weights[rows, :], partner[...])
        for d in range(ys - 1):
            same, diagonal, fetched, swapped, far_weights = far[5 * d : 5 * d + 5]
            total = total + dot_nt((fetched if i == 0 else swapped)[...], same[...])
            total = total + dot_nt(far_weights[rows, :], diagonal[...])
        middle[rows, :] = total.astype(bf16)


def attend(meta, ys, tokens, own, partner, weights, partner_weights, far):
    return pl.pallas_call(
        functools.partial(attend_kernel, ys),
        out_shape=shape_of((weights.shape[0] // 2, own.shape[0])),
        in_specs=[SM] + [VM] * (5 + len(far)),
        out_specs=VM,
        compiler_params=params(12),
        cost_estimate=cost(2 * 10**9, 7 * 10**6),
        name="attend",
    )(meta, tokens, own, partner, weights, partner_weights, *far)


def up_kernel(meta, own, other, gain, weights, lifted, middle_part, first, last, middle, hidden, scale_b):
    features, count = middle.shape
    half = features // 2
    step = 160
    for side, source in ((meta[CORE], own), (1 - meta[CORE], other)):

        @pl.loop(0, half // step)
        def _(r):
            rows = pl.ds(pl.multiple_of(r * step, 32), step)
            target = pl.ds(pl.multiple_of(side * half + r * step, 32), step)
            middle[target, :] = source[rows, :].astype(f32)

    squares = scale_pass(middle, lambda at, size: gain[:, at : at + size], hidden)
    fill_columns(inverse_of(squares, features), scale_b)
    part = middle_part.shape[0]
    middle_part[...] = middle[pl.ds(pl.multiple_of(meta[ME] * part, 8), part), :]
    width = lifted.shape[1]
    for start in range(0, width, 256):
        size = min(256, width - start)
        cols = slice(start, start + size)
        scale = doubled(scale_b[...])[:, :size]
        lifted[:, cols] = (dot(hidden[...], weights[:, cols]) * scale).astype(bf16)
    first[...] = lifted[0:1, :]
    last[...] = lifted[count - 1 : count, :]


def up_project(meta, own, other, gain, weights, part):
    features, hidden = weights.shape
    count = own.shape[1]
    return pl.pallas_call(
        up_kernel,
        out_shape=(
            shape_of((count, hidden)),
            shape_of((part, count), f32),
            shape_of((1, hidden)),
            shape_of((1, hidden)),
        ),
        in_specs=[SM] + [VM] * 4,
        out_specs=[VM] * 4,
        scratch_shapes=[
            pltpu.VMEM((features, count), f32),
            pltpu.VMEM((count, features), bf16),
            pltpu.VMEM((count, DK), f32),
        ],
        compiler_params=params(16),
        cost_estimate=cost(2 * 10**9, 8 * 10**6),
        name="up_project",
    )(meta, own, other, gain, weights)


def gelu_of(x):
    inner = 0.7978845608028654 * (x + 0.044715 * (x * x * x))
    return 0.5 * x * (1.0 + jnp.tanh(inner))


def act_rows(taps, act, padded, start, count):
    @pl.loop(0, count // 32)
    def _(r):
        base = pl.multiple_of(r * 32, 32)
        window = padded[pl.ds(base, 48), :]
        value = (
            taps[0:1, :] * window[7:39, :]
            + taps[1:2, :] * window[8:40, :]
            + taps[2:3, :] * window[9:41, :]
        )
        act[pl.ds(start + base, 32), :] = gelu_of(value).astype(bf16)


def inner_kernel(meta, outer, inside, taps, act_t, padded, act):
    count = act.shape[0]
    padded[7:8, :] = outer[BLOCK - 1 : BLOCK, :].astype(f32)
    padded[8 : 8 + count, :] = inside[...].astype(f32)
    padded[8 + count : 9 + count, :] = outer[BLOCK : BLOCK + 1, :].astype(f32)
    act_rows(taps, act, padded, 0, count)
    act_t[...] = act[...].T


def outer_kernel(meta, outer, inside, before, after, taps, act_t, padded_a, padded_b, act):
    count = inside.shape[0]
    padded_a[7:8, :] = before[...].astype(f32)
    padded_a[8 : 8 + BLOCK, :] = outer[:BLOCK, :].astype(f32)
    padded_a[8 + BLOCK : 9 + BLOCK, :] = inside[0:1, :].astype(f32)
    padded_b[7:8, :] = inside[count - 1 : count, :].astype(f32)
    padded_b[8 : 8 + BLOCK, :] = outer[BLOCK:, :].astype(f32)
    padded_b[8 + BLOCK : 9 + BLOCK, :] = after[...].astype(f32)
    act_rows(taps, act, padded_a, 0, BLOCK)
    act_rows(taps, act, padded_b, BLOCK, BLOCK)
    act_t[...] = act[...].T


def activate(meta, outer, inside, taps, halo):
    hidden = outer.shape[1]
    count = outer.shape[0] if halo else inside.shape[0]
    padded = [BLOCK, BLOCK] if halo else [count]
    return pl.pallas_call(
        outer_kernel if halo else inner_kernel,
        out_shape=shape_of((hidden, count)),
        in_specs=[SM] + [VM] * (3 + len(halo)),
        out_specs=VM,
        scratch_shapes=[pltpu.VMEM((rows + 16, hidden), f32) for rows in padded]
        + [pltpu.VMEM((count, hidden), bf16)],
        compiler_params=params(8),
        cost_estimate=cost(10**9, 2 * 10**6),
        name="activate",
    )(meta, outer, inside, *halo, taps)


def far_kernel(ys, meta, own, other, weights, other_weights, *outs):
    for i, out in enumerate(outs):
        chip = meta[CHIP + ys + i]
        block = 2 * chip + meta[CORE]
        total = dot(weights[block], own[...]) + dot(other_weights[chip], other[...])
        out[...] = total.astype(bf16)


def far_project(meta, ys, own, other, weights, other_weights):
    part = weights.shape[1]
    return pl.pallas_call(
        functools.partial(far_kernel, ys),
        out_shape=[shape_of((part, own.shape[1]))] * (ys - 1),
        in_specs=[SM] + [VM] * 4,
        out_specs=[VM] * (ys - 1),
        compiler_params=params(8),
        cost_estimate=cost(10**9, 4 * 10**6),
        name="far_project",
    )(meta, own, other, weights, other_weights)


def near_kernel(meta, own_a, other_a, own_b, other_b, middle_a, middle_b, weights, other_weights, after, base):
    inside = own_b.shape[1]
    for own, other, middle, spans in (
        (own_b, other_b, middle_b, ((0, BLOCK, inside),)),
        (own_a, other_a, middle_a, ((0, 0, BLOCK), (BLOCK, BLOCK + inside, BLOCK))),
    ):
        total = dot(weights[meta[ME]], own[...])
        total = total + dot(other_weights[meta[CHIP]], other[...]) + middle[...]
        for source, target, size in spans:
            base[:, target : target + size] = total[:, source : source + size]


def near_project(meta, own, other, middle_a, middle_b, weights, other_weights, after):
    part = weights.shape[1]
    return pl.pallas_call(
        near_kernel,
        out_shape=shape_of((part, own[0].shape[1] + own[1].shape[1]), f32),
        in_specs=[SM] + [VM] * 8 + [ANY],
        out_specs=VM,
        compiler_params=params(10),
        cost_estimate=cost(2 * 10**9, 6 * 10**6),
        name="near_project",
    )(meta, own[0], other[0], own[1], other[1], middle_a, middle_b, weights, other_weights, after)


def finish_kernel(count, base, *refs):
    ends, inner, out = refs[:count], refs[count : 2 * count], refs[2 * count]
    inside = inner[0].shape[1]
    for target, size, refs_of, source in (
        (0, BLOCK, ends, 0),
        (BLOCK, inside, inner, 0),
        (BLOCK + inside, BLOCK, ends, BLOCK),
    ):
        total = base[:, target : target + size]
        for ref in refs_of:
            total = total + ref[:, source : source + size].astype(f32)
        out[:, target : target + size] = total.astype(bf16)


def finish(base, ends, inner):
    return pl.pallas_call(
        functools.partial(finish_kernel, len(ends)),
        out_shape=shape_of(base.shape),
        in_specs=[VM] * (1 + 2 * len(ends)),
        out_specs=VM,
        compiler_params=params(8),
        name="finish",
    )(base, *ends, *inner)


def core_swap(value, n):
    return lax.ppermute(value, "head", [(i, i ^ 1) for i in range(n)])


def y_shift(value, n, step):
    return lax.ppermute(value, "head", [(i, (i + 2 * step) % n) for i in range(n)])


def pair_swap(value, n):
    return lax.ppermute(value, "seq", [(i, i ^ 1) for i in range(n)])


def later(value, n, step):
    return lax.ppermute(value, "seq", [(i, i + 2 * step) for i in range(n - 2 * step)])


def shards(
    tokens,
    norm_gain,
    w_query,
    w_key,
    w_value,
    w_decay,
    w_beta,
    head_rates,
    head_gain,
    w_out,
    ffn_gain,
    w_up,
    conv_taps,
    w_down,
):
    n = lax.axis_size("head")
    seqs = lax.axis_size("seq")
    me = lax.axis_index("head")
    at = lax.axis_index("seq")
    core = me % 2
    parity = at % 2
    ys = n // 2
    count, part = tokens.shape
    heads = w_query.shape[1] // DK
    hidden = w_up.shape[1]
    features = n * part

    mine = tokens.T
    shifted = [mine] + [y_shift(mine, n, d) for d in range(1, ys)]

    def group_of(piece):
        partner = core_swap(piece, n)
        if part % 16:
            first = jnp.where(core == 0, piece, partner)
            second = jnp.where(core == 0, partner, piece)
            return [jnp.concatenate([first, second], axis=0)]
        return [piece, partner]

    groups = [group_of(mine)]
    chip = me // 2
    here = [parity, core, me]
    sources = [(chip + ys - d) % ys for d in range(ys)]
    targets = [(chip + d) % ys for d in range(1, ys)]
    meta = jnp.stack(here + sources + targets).astype(jnp.int32)

    w_out_t = w_out.T
    w_parts = w_down.T.reshape(n, part, hidden)

    gates = jnp.concatenate([w_decay.T, w_beta.T], axis=0)
    gates = jnp.pad(gates, ((0, 16 - 2 * heads), (0, 0)))
    gates = gates.reshape(16, ys, 2 * part).transpose(1, 0, 2)
    rates = jnp.pad(head_rates.reshape(2 * heads, 1), ((0, 16 - 2 * heads), (0, 0)))
    rates = jnp.broadcast_to(rates, (16, 128))
    gain = norm_gain.astype(f32).reshape(ys, 1, 2 * part)

    def ours(rows, d):
        return lax.dynamic_index_in_dim(rows, sources[d], 0, False)

    ffn_scale = ffn_gain.astype(f32).reshape(1, features)
    taps = conv_taps.astype(f32)

    gains = [ours(gain, d) for d in range(ys)]
    gate_rows = [ours(gates, d) for d in range(ys)]
    gains, gate_rows, rates, taps, ffn_scale, head_scale, meta = lax.optimization_barrier(
        (gains, gate_rows, rates, taps, ffn_scale, head_gain.reshape(1, DK), meta)
    )

    early = None
    for d in range(ys - 1):
        early = early_project(
            meta, CHIP + d, groups[d], gains[d], gate_rows[d], w_key, w_value, w_query, w_parts, w_out_t, early
        )
        if d == 0:
            sent, early = early[5:], early[:5]
        piece, _ = lax.optimization_barrier((shifted[d + 1], early[4]))
        groups.append(group_of(piece))
    scaled, scale_b, keys, erased, entry, own_maps, sent_maps, totals = block_maps(
        meta, CHIP + ys - 1, groups[-1], gains[-1], rates, gate_rows[-1], w_key, w_value, early
    )

    sent, _ = lax.optimization_barrier((sent, groups[-1][-1]))
    sent_w_down, their_rows, my_rows = sent
    other_w_down = core_swap(sent_w_down, n)
    fetched = [y_shift(my_rows, n, d) for d in range(1, ys)]
    partner_w_out = core_swap(their_rows, n)
    other_maps = pair_swap(sent_maps, seqs)
    their_rows, fetched, _ = lax.optimization_barrier((their_rows, fetched, other_maps))
    diagonal = [
        lax.ppermute(their_rows, "head", [(i, ((i + 2 * d) % n) ^ 1) for i in range(n)])
        for d in range(1, ys)
    ]
    pair, first, done = pair_maps(meta, own_maps, other_maps)
    fetched, _ = lax.optimization_barrier((fetched, done))
    swapped = [pair_swap(value, seqs) for value in fetched]
    pairs = [later(pair, seqs, d) for d in range(seqs // 2 - 1, 0, -1)]
    acc_query, partner_w_out, other_w_down, _ = lax.optimization_barrier(
        (early[2], partner_w_out, other_w_down, done)
    )
    query, tokens_a, tokens_b, _ = queries(
        meta, ys, scaled, scale_b, w_query, acc_query, sum(groups, [])
    )
    shard_query, free, out_done = block_outputs(query, keys, erased, entry, totals, done)
    kept_state, given_state = start_states(meta, first, pairs, out_done)
    other_state = pair_swap(given_state, seqs)

    other_state, swapped, diagonal = lax.optimization_barrier((other_state, swapped, diagonal))
    mixed = mixed_heads(meta, kept_state, other_state, shard_query, free, head_scale)
    far_mixed = [[y_shift(value, n, d) for d in range(1, ys)] for value in mixed]

    def middle_of(i, far):
        heads_far = [[value, core_swap(value, n)] for value in far]
        operands = []
        for pair_of, *weights in zip(heads_far, fetched, swapped, diagonal):
            operands += pair_of + weights
        own_tokens = (tokens_a, tokens_b)[i]
        return attend(
            meta, ys, own_tokens, mixed[i], core_swap(mixed[i], n), w_out_t, partner_w_out, operands
        )

    middle = middle_of(0, far_mixed[0])
    outer, middle_a, first_row, last_row = up_project(
        meta, middle, core_swap(middle, n), ffn_scale, w_up, part
    )
    middle = middle_of(1, far_mixed[1])
    inside, middle_b, _, _ = up_project(
        meta, middle, core_swap(middle, n), ffn_scale, w_up, part
    )

    act_b = activate(meta, outer, inside, taps, ())
    partner_b = core_swap(act_b, n)
    far_b = far_project(meta, ys, act_b, partner_b, w_parts, other_w_down)
    arrived_b = [y_shift(value, n, d + 1) for d, value in enumerate(far_b)]
    first_row, last_row, _ = lax.optimization_barrier((first_row, last_row, far_b))
    before = lax.ppermute(last_row, "seq", [(i, i + 1) for i in range(seqs - 1)])
    after = lax.ppermute(first_row, "seq", [(i + 1, i) for i in range(seqs - 1)])
    before, after, arrived_b = lax.optimization_barrier((before, after, arrived_b))
    act_a = activate(meta, outer, inside, taps, (before, after))
    partner_a = core_swap(act_a, n)
    far_a = far_project(meta, ys, act_a, partner_a, w_parts, other_w_down)
    arrived_a = [y_shift(value, n, d + 1) for d, value in enumerate(far_a)]
    total = near_project(
        meta,
        (act_a, act_b),
        (partner_a, partner_b),
        middle_a,
        middle_b,
        w_parts,
        other_w_down,
        far_a[0],
    )
    return finish(total, arrived_a, arrived_b).T


def solution(mesh):
    placed = (
        P("seq", "head"),
        P(),
        P(None, "head"),
        P(None, "head"),
        P(None, "head"),
        P(None, "head"),
        P(None, "head"),
        P(None, "head"),
        P(),
        P("head", None),
        P(),
        P(None, "head"),
        P(None, "head"),
        P("head", None),
    )
    return jax.shard_map(
        shards, mesh=mesh, in_specs=placed, out_specs=P("seq", "head"), check_vma=False
    )
```

```python
import functools

import jax
import jax.numpy as jnp
from jax import lax
from jax.experimental import pallas as pl
from jax.experimental.pallas import tpu as pltpu
from jax.sharding import PartitionSpec as P

DK = 128
BLOCK = 128
epsilon = 1e-06
f32 = jnp.float32
bf16 = jnp.bfloat16

PARITY, CORE, ME, CHIP = 0, 1, 2, 3

VM = pl.BlockSpec(memory_space=pltpu.VMEM)
SM = pl.BlockSpec(memory_space=pltpu.SMEM)
ANY = pl.BlockSpec(memory_space=pl.ANY)


def params(mebibytes):
    return pltpu.CompilerParams(vmem_limit_bytes=mebibytes * 1024 * 1024)


def cost(flops, moved):
    return pl.CostEstimate(flops=flops, bytes_accessed=moved, transcendentals=0)


def shape_of(shape, dtype=bf16):
    return jax.ShapeDtypeStruct(shape, dtype)


def dot(a, b):
    return jnp.dot(a, b, preferred_element_type=f32)


def dot_nt(a, b):
    return lax.dot_general(a, b, (((1,), (1,)), ((), ())), preferred_element_type=f32)


def dot_tn(a, b):
    return lax.dot_general(a, b, (((0,), (0,)), ((), ())), preferred_element_type=f32)


def iotas(shape):
    return lax.broadcasted_iota(jnp.int32, shape, 0), lax.broadcasted_iota(jnp.int32, shape, 1)


def column_of(row, lanes=128):
    return jnp.broadcast_to(row, (lanes, row.shape[1])).T


def scale_pass(source, gain_at, target):
    features, tokens = source.shape
    squares = jnp.zeros((8, tokens), f32)
    for start in range(0, features, 128):
        size = min(128, features - start)
        value = source[start : start + size, :].astype(f32)
        scale = column_of(gain_at(start, size))
        scale = jnp.concatenate([scale] * (tokens // 128), axis=1)
        target[:, start : start + size] = (value * scale).astype(bf16).T
        value = value * value
        for r in range(0, size, 8):
            squares = squares + value[r : r + 8]
    return squares


def inverse_of(squares, features):
    return lax.rsqrt(jnp.sum(squares, axis=0, keepdims=True) / features + epsilon)


def fill_columns(row, target):
    for start in range(0, row.shape[1], 128):
        target[start : start + 128, :] = column_of(row[:, start : start + 128])


def doubled(tile):
    return jnp.concatenate([tile, tile], axis=1)


def slots_of(meta, n):
    return [meta[CORE], 1 - meta[CORE]] if n == 2 else [0]


def load_pair(meta, pieces, whole, sem):
    part = pieces[0].shape[0]
    copies = [
        pltpu.make_async_copy(
            piece, whole.at[pl.ds(pl.multiple_of(slot * part, 16), part)], sem.at[p]
        )
        for p, (piece, slot) in enumerate(zip(pieces, slots_of(meta, len(pieces))))
    ]
    for copy in copies:
        copy.start()
    for copy in copies:
        copy.wait()


def held_rows(meta, at, weights, held, sem):
    span = held.shape[1]
    rows = pl.ds(pl.multiple_of(meta[at] * span, 16), span)
    copies = [
        pltpu.make_async_copy(ref.at[rows], held.at[i], sem.at[i]) for i, ref in enumerate(weights)
    ]
    for copy in copies:
        copy.start()
    return copies


def early_kernel(count_in, at, meta, *refs):
    first = at == CHIP
    pieces = refs[:count_in]
    gain, gates, w_key, w_value, w_query, w_down, w_out = refs[count_in : count_in + 7]
    refs = refs[count_in + 7 :]
    before, refs = (None, refs) if first else (refs[:5], refs[5:])
    acc_k, acc_v, acc_q, acc_g, squares = refs[:5]
    sent, (whole, scaled, held, held_sem, sem) = (refs[5:8], refs[8:]) if first else ((), refs[5:])
    rows_copies = held_rows(meta, at, (w_key, w_value, w_query), held, held_sem)
    copies = []
    if first:
        partner_w, their_rows, my_rows = sent
        ys = partner_w.shape[0]
        copies = [
            pltpu.make_async_copy(
                w_down.at[2 * y + 1 - meta[CORE]], partner_w.at[y], sem.at[count_in + y]
            )
            for y in range(ys)
        ]
        for i, (start, target) in enumerate(
            (
                ((1 - meta[CORE]) * 2 * my_rows.shape[0], their_rows),
                ((2 * meta[CORE] + meta[PARITY]) * my_rows.shape[0], my_rows),
            )
        ):
            rows = pl.ds(pl.multiple_of(start, 16), target.shape[0])
            copies.append(
                pltpu.make_async_copy(w_out.at[rows], target, sem.at[count_in + ys + i])
            )
    for copy in copies:
        copy.start()
    load_pair(meta, pieces, whole, sem)
    sums = scale_pass(whole, lambda at, size: gain[:, at : at + size], scaled)
    gate = dot_nt(gates[...], scaled[...])
    squares[...] = sums if first else before[4][...] + sums
    acc_g[...] = gate if first else before[3][...] + gate
    for i, out in enumerate((acc_k, acc_v, acc_q)):
        rows_copies[i].wait()
        product = dot(scaled[...], held[i])
        out[...] = product if first else before[i][...] + product
    for copy in copies:
        copy.wait()


def early_project(meta, at, pieces, gain, gates, w_key, w_value, w_query, w_down, w_out, before):
    first = before is None
    blocks, part, hidden = w_down.shape
    ys = blocks // 2
    span = gain.shape[1]
    count = pieces[0].shape[1]
    features, inner = w_key.shape
    return pl.pallas_call(
        functools.partial(early_kernel, len(pieces), at),
        out_shape=[shape_of((count, inner), f32)] * 3
        + [shape_of((16, count), f32), shape_of((8, count), f32)]
        + [
            shape_of((ys, part, hidden)),
            shape_of((features // 2, inner)),
            shape_of((features // 4, inner)),
        ]
        * first,
        in_specs=[SM] + [ANY] * len(pieces) + [VM] * 2 + [ANY] * 5 + [VM] * (0 if first else 5),
        out_specs=[VM] * (8 if first else 5),
        scratch_shapes=[
            pltpu.VMEM((span, count), bf16),
            pltpu.VMEM((count, span), bf16),
            pltpu.VMEM((3, span, inner), bf16),
            pltpu.SemaphoreType.DMA((3,)),
            pltpu.SemaphoreType.DMA((len(pieces) + ys + 2,)),
        ],
        compiler_params=params(48),
        cost_estimate=cost(3 * 10**9, 8 * 10**6),
        name="early_project",
    )(meta, *pieces, gain, gates, w_key, w_value, w_query, w_down, w_out, *(before or ()))


def maps_kernel(n, heads, at, meta, *refs):
    pieces = refs[:n]
    gain, rates, gates, w_key, w_value, acc_k, acc_v, acc_g, squares = refs[n : n + 9]
    scaled, scale_b, keys, erased, entry, own, sent, totals = refs[n + 9 : n + 17]
    whole, raw_k, raw_v, rows_at_head, total_b, beta_b, held, held_sem, acc, acc_sem, sem = refs[
        n + 17 :
    ]
    span, count = whole.shape
    blocks = count // BLOCK
    inner = heads * DK
    features = w_key.shape[0]
    parity = meta[PARITY]
    rows_copies = held_rows(meta, at, (w_key, w_value), held, held_sem)
    rows_copies += [
        pltpu.make_async_copy(ref, acc.at[i], acc_sem.at[i]) for i, ref in enumerate((acc_k, acc_v))
    ]
    for copy in rows_copies[2:]:
        copy.start()
    load_pair(meta, pieces, whole, sem)
    sums = scale_pass(whole, lambda at, size: gain[:, at : at + size], scaled)
    inverse = inverse_of(sums + squares[...], features)
    fill_columns(inverse, scale_b)

    pre = (acc_g[...] + dot_nt(gates[...], scaled[...])) * inverse
    soft = jnp.maximum(pre, 0.0) + jnp.log1p(jnp.exp(-jnp.abs(pre)))
    rate = jnp.concatenate([rates[...]] * (count // 128), axis=1)
    decay = -rate * soft
    beta = jax.nn.sigmoid(pre + rate)
    row_at, col_at = iotas((BLOCK, BLOCK))
    upper = (row_at <= col_at).astype(f32)
    rows_at_head[...] = jnp.zeros_like(rows_at_head)
    for c in range(blocks):
        tokens = slice(c * BLOCK, (c + 1) * BLOCK)
        total = jnp.dot(
            decay[:, tokens], upper, precision=lax.Precision.HIGHEST, preferred_element_type=f32
        )
        totals[c] = total
        rows_at_head[0:16, :] = total
        rows_at_head[16:32, :] = beta[:, tokens]
        columns = rows_at_head[...].T
        for h in range(heads):
            total_b[h, tokens, :] = jnp.broadcast_to(columns[:, h : h + 1], (BLOCK, DK))
            lane = 16 + heads + h
            beta_b[h, tokens, :] = jnp.broadcast_to(columns[:, lane : lane + 1], (BLOCK, DK))

    for copy in rows_copies:
        copy.wait()
    for start in range(0, inner, 256):
        cols = slice(start, start + 256)
        scale = doubled(scale_b[...])
        raw_k[:, cols] = ((acc[0, :, cols] + dot(scaled[...], held[0, :, cols])) * scale).astype(bf16)
        raw_v[:, cols] = ((acc[1, :, cols] + dot(scaled[...], held[1, :, cols])) * scale).astype(bf16)

    xor = jnp.where(row_at > col_at, row_at ^ col_at, 0)
    eye = jnp.where(row_at == col_at, 1.0, 0.0)
    group = 2 if heads % 2 == 0 else 1

    @pl.loop(0, heads // group)
    def _(batch):
        lows, solved = [], []
        chains = []
        for g in range(group):
            h = batch * group + g
            cols = pl.ds(pl.multiple_of(h * DK, DK), DK)
            wide = pl.ds(pl.multiple_of(h * 2 * DK, 2 * DK), 2 * DK)
            raw = raw_k[:, cols].astype(f32)
            unit = raw * lax.rsqrt(jnp.sum(raw * raw, axis=1, keepdims=True) + epsilon)
            keys[:, cols] = unit.astype(bf16)
            for c in range(blocks):
                chains.append((h, cols, wide, c, slice(c * BLOCK, (c + 1) * BLOCK)))
        for h, cols, wide, c, rows in chains:
            k = keys[rows, cols]
            fade = jnp.exp(jnp.minimum(total_b[h, rows, :] - totals[c, pl.ds(h, 1), :], 0.0))
            low = jnp.where(xor > 0, beta_b[h, rows, :] * fade * dot_nt(k, k), 0.0)
            lows.append(low)
            solved.append(eye - jnp.where(xor == 1, low, 0.0))
        size = 2
        while size < BLOCK:
            mask = (xor >= size) & (xor < 2 * size)
            first = []
            for i in range(len(chains)):
                link = jnp.where(mask, lows[i], 0.0).astype(bf16)
                first.append(dot(link, solved[i].astype(bf16)).astype(bf16))
            solved = [
                solved[i] - dot(solved[i].astype(bf16), first[i]) for i in range(len(chains))
            ]
            size *= 2
        grown = []
        for i, (h, cols, wide, c, rows) in enumerate(chains):
            k = keys[rows, cols].astype(f32)
            t_col = total_b[h, rows, :]
            b_col = beta_b[h, rows, :]
            right = jnp.concatenate(
                [
                    (b_col * jnp.exp(t_col) * k).astype(bf16),
                    (b_col * raw_v[rows, cols].astype(f32)).astype(bf16),
                ],
                axis=1,
            )
            both = dot(solved[i].astype(bf16), right).astype(bf16)
            erased[rows, wide] = both
            t_end = t_col[BLOCK - 1 : BLOCK, :]
            faded = (jnp.exp(t_end - t_col) * k).astype(bf16)
            grown.append((jnp.exp(t_end), dot_tn(faded, both)))
        states = [None] * group
        for c in range(blocks):
            for g in range(group):
                h, cols, wide = chains[g * blocks][:3]
                end, product = grown[g * blocks + c]
                erase, write = product[:, :DK], product[:, DK:]
                if c == 0:
                    state = jnp.concatenate([end * eye - erase, write], axis=1)
                else:
                    step = dot(erase.astype(bf16), states[g].astype(bf16))
                    state = (
                        jnp.concatenate([end, end], axis=1) * states[g]
                        - step
                        + jnp.concatenate([jnp.zeros_like(write), write], axis=1)
                    )
                if c < blocks - 1:
                    entry[c, :, wide] = state.astype(bf16)
                states[g] = state
        for g in range(group):
            h = batch * group + g
            half = heads // 2
            mine = (h >= half) == (parity == 1)
            slot = lax.rem(h, half)

            @pl.when(mine)
            def _():
                own[slot] = states[g].astype(bf16)

            @pl.when(jnp.logical_not(mine))
            def _():
                sent[slot] = states[g].astype(bf16)


def block_maps(meta, at, pieces, gain, rates, gates, w_key, w_value, early):
    n = len(pieces)
    acc_k, acc_v, acc_q, acc_g, squares = early
    count = pieces[0].shape[1]
    span = gain.shape[1]
    inner = w_key.shape[1]
    heads = inner // DK
    blocks = count // BLOCK
    return pl.pallas_call(
        functools.partial(maps_kernel, n, heads, at),
        out_shape=(
            shape_of((count, span)),
            shape_of((count, DK), f32),
            shape_of((count, inner)),
            shape_of((count, 2 * inner)),
            shape_of((blocks - 1, DK, 2 * inner)),
            shape_of((heads // 2, DK, 2 * DK)),
            shape_of((heads // 2, DK, 2 * DK)),
            shape_of((blocks, 16, 128), f32),
        ),
        in_specs=[SM] + [ANY] * n + [VM] * 3 + [ANY] * 4 + [VM] * 2,
        out_specs=[VM] * 8,
        scratch_shapes=[
            pltpu.VMEM((span, count), bf16),
            pltpu.VMEM((count, inner), bf16),
            pltpu.VMEM((count, inner), bf16),
            pltpu.VMEM((128, BLOCK), f32),
            pltpu.VMEM((heads, count, DK), f32),
            pltpu.VMEM((heads, count, DK), f32),
            pltpu.VMEM((2, span, inner), bf16),
            pltpu.SemaphoreType.DMA((2,)),
            pltpu.VMEM((2, count, inner), f32),
            pltpu.SemaphoreType.DMA((2,)),
            pltpu.SemaphoreType.DMA((n,)),
        ],
        compiler_params=params(16),
        cost_estimate=cost(10 * 10**9, 14 * 10**6),
        name="block_maps",
    )(meta, *pieces, gain, rates, gates, w_key, w_value, acc_k, acc_v, acc_g, squares)


def query_kernel(n, ys, meta, scaled, scale_b, weights, acc, *refs):
    pieces, (query, tokens_a, tokens_b, done, held, sem) = refs[: n * ys], refs[n * ys :]
    (copy,) = held_rows(meta, CHIP + ys - 1, (weights,), held, sem)
    span = scaled.shape[1]
    part, count = pieces[0].shape
    for d in range(ys):
        for p, slot in enumerate(slots_of(meta, n)):
            piece = pieces[d * n + p]
            base = meta[CHIP + d] * span + slot * part
            step = part // 7

            @pl.loop(0, 7)
            def _(r):
                rows = pl.ds(pl.multiple_of(r * step, 8), step)
                target = pl.ds(pl.multiple_of(base + r * step, 8), step)
                tokens_a[target, :BLOCK] = piece[rows, :BLOCK]
                tokens_a[target, BLOCK:] = piece[rows, count - BLOCK :]
                tokens_b[target, :] = piece[rows, BLOCK : count - BLOCK]

    done[...] = jnp.zeros_like(done)
    copy.wait()
    for start in range(0, query.shape[1], 256):
        cols = slice(start, start + 256)
        product = acc[:, cols] + dot(scaled[...], held[0, :, cols])
        query[:, cols] = (product * doubled(scale_b[...])).astype(bf16)


def queries(meta, ys, scaled, scale_b, weights, acc, pieces):
    n = len(pieces) // ys
    features = weights.shape[0]
    count = acc.shape[0]
    return pl.pallas_call(
        functools.partial(query_kernel, n, ys),
        out_shape=(
            shape_of(acc.shape),
            shape_of((features, 2 * BLOCK)),
            shape_of((features, count - 2 * BLOCK)),
            shape_of((8, 128), f32),
        ),
        in_specs=[SM] + [VM] * 2 + [ANY] + [VM] * (1 + len(pieces)),
        out_specs=[VM] * 4,
        scratch_shapes=[
            pltpu.VMEM((1, scaled.shape[1], acc.shape[1]), bf16),
            pltpu.SemaphoreType.DMA((1,)),
        ],
        compiler_params=params(12),
        cost_estimate=cost(10**9, 8 * 10**6),
        name="queries",
    )(meta, scaled, scale_b, weights, acc, *pieces)


def outputs_kernel(heads, query, keys, erased, entry, totals, after, shard_query, free, done, rows_at_head):
    count = query.shape[0]
    blocks = count // BLOCK
    row_at, col_at = iotas((BLOCK, BLOCK))
    done[...] = jnp.zeros_like(done)
    rows_at_head[...] = jnp.zeros_like(rows_at_head)
    for c in range(blocks):
        rows = slice(c * BLOCK, (c + 1) * BLOCK)
        rows_at_head[0:16, :] = totals[c]
        columns = rows_at_head[...].T
        for h in range(heads):
            cols = slice(h * DK, (h + 1) * DK)
            wide = slice(h * 2 * DK, (h + 1) * 2 * DK)
            t_col = jnp.broadcast_to(columns[:, h : h + 1], (BLOCK, BLOCK))
            t_row = totals[c, h : h + 1, :]
            fade = jnp.where(row_at >= col_at, jnp.exp(jnp.minimum(t_col - t_row, 0.0)), 0.0)
            q = query[rows, cols]
            scores = (fade * dot_nt(q, keys[rows, cols])).astype(bf16)
            both = dot(scores, erased[rows, wide])
            reach = jnp.exp(t_col) * q.astype(f32) - both[:, :DK]
            local = both[:, DK:]
            if c > 0:
                product = dot(reach.astype(bf16), entry[c - 1, :, wide])
                reach = product[:, :DK]
                local = local + product[:, DK:]
            shard_query[rows, cols] = reach.astype(bf16)
            free[rows, cols] = local


def block_outputs(query, keys, erased, entry, totals, after):
    heads = query.shape[1] // DK
    return pl.pallas_call(
        functools.partial(outputs_kernel, heads),
        out_shape=(shape_of(query.shape), shape_of(query.shape, f32), shape_of((8, 128), f32)),
        in_specs=[VM] * 5 + [ANY],
        out_specs=[VM] * 3,
        scratch_shapes=[pltpu.VMEM((128, BLOCK), f32)],
        compiler_params=params(8),
        cost_estimate=cost(3 * 10**9, 4 * 10**6),
        name="block_outputs",
    )(query, keys, erased, entry, totals, after)


def pair_kernel(meta, own, other, pair, first, done):
    even = meta[PARITY] == 0
    for h in range(own.shape[0]):
        mine, theirs = own[h], other[h]
        early = jnp.where(even, mine, theirs)
        late = jnp.where(even, theirs, mine)
        product = dot(late[:, :DK], early)
        shift = late[:, DK:].astype(f32)
        pair[h] = (product + jnp.concatenate([jnp.zeros_like(shift), shift], axis=1)).astype(bf16)
        first[h] = early
    done[...] = jnp.zeros_like(done)


def pair_maps(meta, own, other):
    return pl.pallas_call(
        pair_kernel,
        out_shape=(shape_of(own.shape), shape_of(own.shape), shape_of((8, 128), f32)),
        in_specs=[SM, VM, VM],
        out_specs=[VM] * 3,
        compiler_params=params(4),
        name="pair_maps",
    )(meta, own, other)


def apply_map(whole, state):
    high = state.astype(bf16)
    low = (state - high.astype(f32)).astype(bf16)
    product = dot(whole[:, :DK], jnp.concatenate([high, low], axis=1))
    return product[:, :DK] + product[:, DK:] + whole[:, DK:].astype(f32)


def start_kernel(steps, meta, first, *refs):
    pairs, (after, keep, give) = refs[:steps], refs[steps:]
    even = meta[PARITY] == 0
    for h in range(first.shape[0]):
        state = pairs[0][h][:, DK:].astype(f32)
        for pair in pairs[1:]:
            state = apply_map(pair[h], state)
        later = apply_map(first[h], state)
        keep[h] = jnp.where(even, state, later).astype(bf16)
        give[h] = jnp.where(even, later, state).astype(bf16)


def start_states(meta, first, pairs, after):
    heads = first.shape[0]
    shape = shape_of((heads, DK, DK))
    return pl.pallas_call(
        functools.partial(start_kernel, len(pairs)),
        out_shape=(shape, shape),
        in_specs=[SM] + [VM] * (1 + len(pairs)) + [ANY],
        out_specs=[VM] * 2,
        compiler_params=params(4),
        name="start_states",
    )(meta, first, *pairs, after)


def mixed_kernel(heads, meta, own, other, shard_query, free, gain, mixed_a, mixed_b):
    even = meta[PARITY] == 0
    half = heads // 2
    blocks = shard_query.shape[0] // BLOCK
    for h in range(heads):
        cols = slice(h * DK, (h + 1) * DK)
        if h < half:
            state = jnp.where(even, own[h], other[h])
        else:
            state = jnp.where(even, other[h - half], own[h - half])
        for unit in range(blocks):
            rows = slice(unit * BLOCK, (unit + 1) * BLOCK)
            out = dot(shard_query[rows, cols], state) + free[rows, cols]
            scale = lax.rsqrt(jnp.mean(out * out, axis=1, keepdims=True) + epsilon)
            value = (out * scale * gain[...].astype(f32)).astype(bf16)
            if unit == 0:
                mixed_a[:BLOCK, cols] = value
            elif unit == blocks - 1:
                mixed_a[BLOCK:, cols] = value
            else:
                mixed_b[(unit - 1) * BLOCK : unit * BLOCK, cols] = value


def mixed_heads(meta, own, other, shard_query, free, gain):
    count, inner = shard_query.shape
    return pl.pallas_call(
        functools.partial(mixed_kernel, inner // DK),
        out_shape=(shape_of((2 * BLOCK, inner)), shape_of((count - 2 * BLOCK, inner))),
        in_specs=[SM] + [VM] * 5,
        out_specs=[VM] * 2,
        compiler_params=params(6),
        cost_estimate=cost(10**9, 3 * 10**6),
        name="mixed_heads",
    )(meta, own, other, shard_query, free, gain)


def attend_kernel(ys, meta, tokens, own, partner, weights, partner_weights, *refs):
    far, middle = refs[:-1], refs[-1]
    half = middle.shape[0]
    size = half // 2
    for i in range(2):
        quarter = meta[PARITY] if i == 0 else 1 - meta[PARITY]
        base = meta[CORE] * half + quarter * size
        here = pl.ds(pl.multiple_of(base, 16), size)
        rows = pl.ds(pl.multiple_of(quarter * size, 16), size)
        total = tokens[here, :].astype(f32)
        total = total + dot_nt(weights[here, :], own[...])
        total = total + dot_nt(partner_weights[rows, :], partner[...])
        for d in range(ys - 1):
            same, diagonal, fetched, swapped, far_weights = far[5 * d : 5 * d + 5]
            total = total + dot_nt((fetched if i == 0 else swapped)[...], same[...])
            total = total + dot_nt(far_weights[rows, :], diagonal[...])
        middle[rows, :] = total.astype(bf16)


def attend(meta, ys, tokens, own, partner, weights, partner_weights, far):
    return pl.pallas_call(
        functools.partial(attend_kernel, ys),
        out_shape=shape_of((weights.shape[0] // 2, own.shape[0])),
        in_specs=[SM] + [VM] * (5 + len(far)),
        out_specs=VM,
        compiler_params=params(12),
        cost_estimate=cost(2 * 10**9, 7 * 10**6),
        name="attend",
    )(meta, tokens, own, partner, weights, partner_weights, *far)


def up_kernel(
    meta, own, other, gain, weights, lifted, middle_part, near_row, next_row, middle, hidden, scale_b
):
    features, count = middle.shape
    half = features // 2
    step = 160
    for side, source in ((meta[CORE], own), (1 - meta[CORE], other)):

        @pl.loop(0, half // step)
        def _(r):
            rows = pl.ds(pl.multiple_of(r * step, 32), step)
            target = pl.ds(pl.multiple_of(side * half + r * step, 32), step)
            middle[target, :] = source[rows, :].astype(f32)

    squares = scale_pass(middle, lambda at, size: gain[:, at : at + size], hidden)
    fill_columns(inverse_of(squares, features), scale_b)
    part = middle_part.shape[0]
    middle_part[...] = middle[pl.ds(pl.multiple_of(meta[ME] * part, 8), part), :]
    width = lifted.shape[1]
    for start in range(0, width, 256):
        size = min(256, width - start)
        cols = slice(start, start + size)
        scale = doubled(scale_b[...])[:, :size]
        lifted[:, cols] = (dot(hidden[...], weights[:, cols]) * scale).astype(bf16)
    even = meta[PARITY] == 0
    first, last = lifted[0:1, :], lifted[count - 1 : count, :]
    near_row[...] = jnp.where(even, last, first)
    next_row[...] = jnp.where(even, first, last)


def up_project(meta, own, other, gain, weights, part):
    features, hidden = weights.shape
    count = own.shape[1]
    return pl.pallas_call(
        up_kernel,
        out_shape=(
            shape_of((count, hidden)),
            shape_of((part, count), f32),
            shape_of((1, hidden)),
            shape_of((1, hidden)),
        ),
        in_specs=[SM] + [VM] * 4,
        out_specs=[VM] * 4,
        scratch_shapes=[
            pltpu.VMEM((features, count), f32),
            pltpu.VMEM((count, features), bf16),
            pltpu.VMEM((count, DK), f32),
        ],
        compiler_params=params(16),
        cost_estimate=cost(2 * 10**9, 8 * 10**6),
        name="up_project",
    )(meta, own, other, gain, weights)


def gelu_of(x):
    inner = 0.7978845608028654 * (x + 0.044715 * (x * x * x))
    return 0.5 * x * (1.0 + jnp.tanh(inner))


def act_kernel(late, meta, outer, inside, near_row, next_row, taps, act_t, padded, act):
    count = act.shape[0]
    even = meta[PARITY] == 0
    if late:
        padded[7:8, :] = inside[BLOCK - 1 : BLOCK, :].astype(f32)
        padded[8 : 8 + BLOCK, :] = inside[BLOCK:, :].astype(f32)
        padded[8 + BLOCK : 8 + count, :] = outer[BLOCK:, :].astype(f32)
        padded[8 + count : 9 + count, :] = jnp.where(even, near_row[...], next_row[...]).astype(f32)
    else:
        padded[7:8, :] = jnp.where(even, next_row[...], near_row[...]).astype(f32)
        padded[8 : 8 + BLOCK, :] = outer[:BLOCK, :].astype(f32)
        padded[8 + BLOCK : 8 + count, :] = inside[:BLOCK, :].astype(f32)
        padded[8 + count : 9 + count, :] = inside[BLOCK : BLOCK + 1, :].astype(f32)

    @pl.loop(0, count // 32)
    def _(r):
        base = pl.multiple_of(r * 32, 32)
        window = padded[pl.ds(base, 48), :]
        value = (
            taps[0:1, :] * window[7:39, :]
            + taps[1:2, :] * window[8:40, :]
            + taps[2:3, :] * window[9:41, :]
        )
        act[pl.ds(base, 32), :] = gelu_of(value).astype(bf16)

    act_t[...] = act[...].T


def activate(meta, outer, inside, near_row, next_row, taps, late):
    hidden = outer.shape[1]
    count = (outer.shape[0] + inside.shape[0]) // 2
    return pl.pallas_call(
        functools.partial(act_kernel, late),
        out_shape=shape_of((hidden, count)),
        in_specs=[SM] + [VM] * 5,
        out_specs=VM,
        scratch_shapes=[pltpu.VMEM((count + 16, hidden), f32), pltpu.VMEM((count, hidden), bf16)],
        compiler_params=params(8),
        cost_estimate=cost(10**9, 2 * 10**6),
        name="activate",
    )(meta, outer, inside, near_row, next_row, taps)


def far_kernel(ys, meta, own, other, weights, other_weights, *outs):
    for i, out in enumerate(outs):
        chip = meta[CHIP + ys + i]
        block = 2 * chip + meta[CORE]
        total = dot(weights[block], own[...]) + dot(other_weights[chip], other[...])
        out[...] = total.astype(bf16)


def far_project(meta, ys, own, other, weights, other_weights):
    part = weights.shape[1]
    return pl.pallas_call(
        functools.partial(far_kernel, ys),
        out_shape=[shape_of((part, own.shape[1]))] * (ys - 1),
        in_specs=[SM] + [VM] * 4,
        out_specs=[VM] * (ys - 1),
        compiler_params=params(8),
        cost_estimate=cost(10**9, 4 * 10**6),
        name="far_project",
    )(meta, own, other, weights, other_weights)


def near_kernel(meta, own_a, other_a, own_b, other_b, middle_a, middle_b, weights, other_weights, after, base):
    size = own_a.shape[1]
    middle = (
        jnp.concatenate([middle_a[:, :BLOCK], middle_b[:, :BLOCK]], axis=1),
        jnp.concatenate([middle_b[:, BLOCK:], middle_a[:, BLOCK:]], axis=1),
    )
    for i, (own, other) in enumerate(((own_a, other_a), (own_b, other_b))):
        total = dot(weights[meta[ME]], own[...])
        total = total + dot(other_weights[meta[CHIP]], other[...])
        base[:, i * size : (i + 1) * size] = total + middle[i]


def near_project(meta, own, other, middle_a, middle_b, weights, other_weights, after):
    part = weights.shape[1]
    return pl.pallas_call(
        near_kernel,
        out_shape=shape_of((part, 2 * own[0].shape[1]), f32),
        in_specs=[SM] + [VM] * 8 + [ANY],
        out_specs=VM,
        compiler_params=params(10),
        cost_estimate=cost(2 * 10**9, 6 * 10**6),
        name="near_project",
    )(meta, own[0], other[0], own[1], other[1], middle_a, middle_b, weights, other_weights, after)


def core_swap(value, n):
    return lax.ppermute(value, "head", [(i, i ^ 1) for i in range(n)])


def y_shift(value, n, step):
    return lax.ppermute(value, "head", [(i, (i + 2 * step) % n) for i in range(n)])


def pair_swap(value, n):
    return lax.ppermute(value, "seq", [(i, i ^ 1) for i in range(n)])


def later(value, n, step):
    return lax.ppermute(value, "seq", [(i, i + 2 * step) for i in range(n - 2 * step)])


def shards(
    tokens,
    norm_gain,
    w_query,
    w_key,
    w_value,
    w_decay,
    w_beta,
    head_rates,
    head_gain,
    w_out,
    ffn_gain,
    w_up,
    conv_taps,
    w_down,
):
    n = lax.axis_size("head")
    seqs = lax.axis_size("seq")
    me = lax.axis_index("head")
    at = lax.axis_index("seq")
    core = me % 2
    parity = at % 2
    ys = n // 2
    count, part = tokens.shape
    heads = w_query.shape[1] // DK
    hidden = w_up.shape[1]
    features = n * part

    mine = tokens.T
    shifted = [mine] + [y_shift(mine, n, d) for d in range(1, ys)]

    def group_of(piece):
        partner = core_swap(piece, n)
        if part % 16:
            first = jnp.where(core == 0, piece, partner)
            second = jnp.where(core == 0, partner, piece)
            return [jnp.concatenate([first, second], axis=0)]
        return [piece, partner]

    groups = [group_of(mine)]
    chip = me // 2
    here = [parity, core, me]
    sources = [(chip + ys - d) % ys for d in range(ys)]
    targets = [(chip + d) % ys for d in range(1, ys)]
    meta = jnp.stack(here + sources + targets).astype(jnp.int32)

    w_out_t = w_out.T
    w_parts = w_down.T.reshape(n, part, hidden)

    gates = jnp.concatenate([w_decay.T, w_beta.T], axis=0)
    gates = jnp.pad(gates, ((0, 16 - 2 * heads), (0, 0)))
    gates = gates.reshape(16, ys, 2 * part).transpose(1, 0, 2)
    rates = jnp.pad(head_rates.reshape(2 * heads, 1), ((0, 16 - 2 * heads), (0, 0)))
    rates = jnp.broadcast_to(rates, (16, 128))
    gain = norm_gain.astype(f32).reshape(ys, 1, 2 * part)

    def ours(rows, d):
        return lax.dynamic_index_in_dim(rows, sources[d], 0, False)

    ffn_scale = ffn_gain.astype(f32).reshape(1, features)
    taps = conv_taps.astype(f32)

    gains = [ours(gain, d) for d in range(ys)]
    gate_rows = [ours(gates, d) for d in range(ys)]
    gains, gate_rows, rates, taps, ffn_scale, head_scale, meta = lax.optimization_barrier(
        (gains, gate_rows, rates, taps, ffn_scale, head_gain.reshape(1, DK), meta)
    )

    early = None
    for d in range(ys - 1):
        early = early_project(
            meta, CHIP + d, groups[d], gains[d], gate_rows[d], w_key, w_value, w_query, w_parts, w_out_t, early
        )
        if d == 0:
            sent, early = early[5:], early[:5]
        piece, _ = lax.optimization_barrier((shifted[d + 1], early[4]))
        groups.append(group_of(piece))
    scaled, scale_b, keys, erased, entry, own_maps, sent_maps, totals = block_maps(
        meta, CHIP + ys - 1, groups[-1], gains[-1], rates, gate_rows[-1], w_key, w_value, early
    )

    sent, _ = lax.optimization_barrier((sent, groups[-1][-1]))
    sent_w_down, their_rows, my_rows = sent
    other_w_down = core_swap(sent_w_down, n)
    fetched = [y_shift(my_rows, n, d) for d in range(1, ys)]
    diagonal = [
        lax.ppermute(their_rows, "head", [(i, ((i + 2 * d) % n) ^ 1) for i in range(n)])
        for d in range(1, ys)
    ]
    partner_w_out = core_swap(their_rows, n)
    other_maps = pair_swap(sent_maps, seqs)
    pair, first, done = pair_maps(meta, own_maps, other_maps)
    pairs = [later(pair, seqs, d) for d in range(seqs // 2 - 1, 0, -1)]
    acc_query, partner_w_out, other_w_down, _ = lax.optimization_barrier(
        (early[2], partner_w_out, other_w_down, done)
    )
    query, tokens_a, tokens_b, _ = queries(
        meta, ys, scaled, scale_b, w_query, acc_query, sum(groups, [])
    )
    shard_query, free, out_done = block_outputs(query, keys, erased, entry, totals, done)
    kept_state, given_state = start_states(meta, first, pairs, out_done)
    other_state = pair_swap(given_state, seqs)

    mixed = mixed_heads(meta, kept_state, other_state, shard_query, free, head_scale)
    far_mixed = [[y_shift(value, n, d) for d in range(1, ys)] for value in mixed]

    fetched, _ = lax.optimization_barrier((fetched, mixed))
    swapped = [pair_swap(value, seqs) for value in fetched]

    def middle_of(i, far):
        heads_far = [[value, core_swap(value, n)] for value in far]
        operands = []
        for pair_of, *weights in zip(heads_far, fetched, swapped, diagonal):
            operands += pair_of + weights
        own_tokens = (tokens_a, tokens_b)[i]
        return attend(
            meta, ys, own_tokens, mixed[i], core_swap(mixed[i], n), w_out_t, partner_w_out, operands
        )

    middle = middle_of(0, far_mixed[0])
    outer, middle_a, near_row, next_row = up_project(
        meta, middle, core_swap(middle, n), ffn_scale, w_up, part
    )
    near_row = lax.ppermute(near_row, "seq", [(i, i ^ 1) for i in range(seqs)])
    next_row = lax.ppermute(
        next_row, "seq", [(i, ((i + 1) ^ 1) - 1) for i in range(1, seqs - 1)]
    )
    middle = middle_of(1, far_mixed[1])
    inside, middle_b, _, _ = up_project(
        meta, middle, core_swap(middle, n), ffn_scale, w_up, part
    )

    acts = [activate(meta, outer, inside, near_row, next_row, taps, late) for late in (False, True)]
    partner_acts = [core_swap(act, n) for act in acts]
    fars = [
        far_project(meta, ys, act, partner, w_parts, other_w_down)
        for act, partner in zip(acts, partner_acts)
    ]
    total = near_project(
        meta, acts, partner_acts, middle_a, middle_b, w_parts, other_w_down, fars[1][0]
    )
    for d in range(1, ys):
        halves = [y_shift(far[d - 1], n, d) for far in fars]
        total = total + jnp.concatenate(halves, axis=1).astype(f32)
    return total.astype(bf16).T


def solution(mesh):
    placed = (
        P("seq", "head"),
        P(),
        P(None, "head"),
        P(None, "head"),
        P(None, "head"),
        P(None, "head"),
        P(None, "head"),
        P(None, "head"),
        P(),
        P("head", None),
        P(),
        P(None, "head"),
        P(None, "head"),
        P("head", None),
    )
    return jax.shard_map(
        shards, mesh=mesh, in_specs=placed, out_specs=P("seq", "head"), check_vma=False
    )
```

```python
import functools

import jax
import jax.numpy as jnp
from jax import lax
from jax.experimental import pallas as pl
from jax.experimental.pallas import tpu as pltpu
from jax.sharding import PartitionSpec as P

DK = 128
BLOCK = 128
epsilon = 1e-06
f32 = jnp.float32
bf16 = jnp.bfloat16

PARITY, CORE, ME, CHIP = 0, 1, 2, 3

VM = pl.BlockSpec(memory_space=pltpu.VMEM)
SM = pl.BlockSpec(memory_space=pltpu.SMEM)
ANY = pl.BlockSpec(memory_space=pl.ANY)


def params(mebibytes):
    return pltpu.CompilerParams(vmem_limit_bytes=mebibytes * 1024 * 1024)


def cost(flops, moved):
    return pl.CostEstimate(flops=flops, bytes_accessed=moved, transcendentals=0)


def shape_of(shape, dtype=bf16):
    return jax.ShapeDtypeStruct(shape, dtype)


def dot(a, b):
    return jnp.dot(a, b, preferred_element_type=f32)


def dot_nt(a, b):
    return lax.dot_general(a, b, (((1,), (1,)), ((), ())), preferred_element_type=f32)


def dot_tn(a, b):
    return lax.dot_general(a, b, (((0,), (0,)), ((), ())), preferred_element_type=f32)


def iotas(shape):
    return lax.broadcasted_iota(jnp.int32, shape, 0), lax.broadcasted_iota(jnp.int32, shape, 1)


def column_of(row, lanes=128):
    return jnp.broadcast_to(row, (lanes, row.shape[1])).T


def scale_pass(source, gain_at, target):
    features, tokens = source.shape
    squares = jnp.zeros((8, tokens), f32)
    for start in range(0, features, 128):
        size = min(128, features - start)
        value = source[start : start + size, :].astype(f32)
        scale = column_of(gain_at(start, size))
        scale = jnp.concatenate([scale] * (tokens // 128), axis=1)
        target[:, start : start + size] = (value * scale).astype(bf16).T
        value = value * value
        for r in range(0, size, 8):
            squares = squares + value[r : r + 8]
    return squares


def inverse_of(squares, features):
    return lax.rsqrt(jnp.sum(squares, axis=0, keepdims=True) / features + epsilon)


def fill_columns(row, target):
    for start in range(0, row.shape[1], 128):
        target[start : start + 128, :] = column_of(row[:, start : start + 128])


def doubled(tile):
    return jnp.concatenate([tile, tile], axis=1)


def slots_of(meta, n):
    return [meta[CORE], 1 - meta[CORE]] if n == 2 else [0]


def load_pair(meta, pieces, whole, sem):
    part = pieces[0].shape[0]
    copies = [
        pltpu.make_async_copy(
            piece, whole.at[pl.ds(pl.multiple_of(slot * part, 16), part)], sem.at[p]
        )
        for p, (piece, slot) in enumerate(zip(pieces, slots_of(meta, len(pieces))))
    ]
    for copy in copies:
        copy.start()
    for copy in copies:
        copy.wait()


def held_rows(meta, at, weights, held, sem):
    span = held.shape[1]
    rows = pl.ds(pl.multiple_of(meta[at] * span, 16), span)
    copies = [
        pltpu.make_async_copy(ref.at[rows], held.at[i], sem.at[i]) for i, ref in enumerate(weights)
    ]
    for copy in copies:
        copy.start()
    return copies


def early_kernel(count_in, at, meta, *refs):
    first = at == CHIP
    pieces = refs[:count_in]
    gain, gates, w_key, w_value, w_query, w_down, w_out = refs[count_in : count_in + 7]
    refs = refs[count_in + 7 :]
    before, refs = (None, refs) if first else (refs[:5], refs[5:])
    acc_k, acc_v, acc_q, acc_g, squares = refs[:5]
    sent, (whole, scaled, held, held_sem, sem) = (refs[5:8], refs[8:]) if first else ((), refs[5:])
    rows_copies = held_rows(meta, at, (w_key, w_value, w_query), held, held_sem)
    copies = []
    if first:
        partner_w, their_rows, my_rows = sent
        ys = partner_w.shape[0]
        copies = [
            pltpu.make_async_copy(
                w_down.at[2 * y + 1 - meta[CORE]], partner_w.at[y], sem.at[count_in + y]
            )
            for y in range(ys)
        ]
        for i, (start, target) in enumerate(
            (
                ((1 - meta[CORE]) * 2 * my_rows.shape[0], their_rows),
                ((2 * meta[CORE] + meta[PARITY]) * my_rows.shape[0], my_rows),
            )
        ):
            rows = pl.ds(pl.multiple_of(start, 16), target.shape[0])
            copies.append(
                pltpu.make_async_copy(w_out.at[rows], target, sem.at[count_in + ys + i])
            )
    for copy in copies:
        copy.start()
    load_pair(meta, pieces, whole, sem)
    sums = scale_pass(whole, lambda at, size: gain[:, at : at + size], scaled)
    gate = dot_nt(gates[...], scaled[...])
    squares[...] = sums if first else before[4][...] + sums
    acc_g[...] = gate if first else before[3][...] + gate
    for i, out in enumerate((acc_k, acc_v, acc_q)):
        rows_copies[i].wait()
        product = dot(scaled[...], held[i])
        out[...] = product if first else before[i][...] + product
    for copy in copies:
        copy.wait()


def early_project(meta, at, pieces, gain, gates, w_key, w_value, w_query, w_down, w_out, before):
    first = before is None
    blocks, part, hidden = w_down.shape
    ys = blocks // 2
    span = gain.shape[1]
    count = pieces[0].shape[1]
    features, inner = w_key.shape
    return pl.pallas_call(
        functools.partial(early_kernel, len(pieces), at),
        out_shape=[shape_of((count, inner), f32)] * 3
        + [shape_of((16, count), f32), shape_of((8, count), f32)]
        + [
            shape_of((ys, part, hidden)),
            shape_of((features // 2, inner)),
            shape_of((features // 4, inner)),
        ]
        * first,
        in_specs=[SM] + [ANY] * len(pieces) + [VM] * 2 + [ANY] * 5 + [VM] * (0 if first else 5),
        out_specs=[VM] * (8 if first else 5),
        scratch_shapes=[
            pltpu.VMEM((span, count), bf16),
            pltpu.VMEM((count, span), bf16),
            pltpu.VMEM((3, span, inner), bf16),
            pltpu.SemaphoreType.DMA((3,)),
            pltpu.SemaphoreType.DMA((len(pieces) + ys + 2,)),
        ],
        compiler_params=params(48),
        cost_estimate=cost(3 * 10**9, 8 * 10**6),
        name="early_project",
    )(meta, *pieces, gain, gates, w_key, w_value, w_query, w_down, w_out, *(before or ()))


def maps_kernel(n, heads, at, meta, *refs):
    pieces = refs[:n]
    gain, rates, gates, w_key, w_value, acc_k, acc_v, acc_g, squares = refs[n : n + 9]
    scaled, scale_b, keys, erased, entry, own, sent, totals = refs[n + 9 : n + 17]
    whole, raw_k, raw_v, rows_at_head, total_b, beta_b, held, held_sem, acc, acc_sem, sem = refs[
        n + 17 :
    ]
    span, count = whole.shape
    blocks = count // BLOCK
    inner = heads * DK
    features = w_key.shape[0]
    parity = meta[PARITY]
    rows_copies = held_rows(meta, at, (w_key, w_value), held, held_sem)
    rows_copies += [
        pltpu.make_async_copy(ref, acc.at[i], acc_sem.at[i]) for i, ref in enumerate((acc_k, acc_v))
    ]
    for copy in rows_copies[2:]:
        copy.start()
    load_pair(meta, pieces, whole, sem)
    sums = scale_pass(whole, lambda at, size: gain[:, at : at + size], scaled)
    inverse = inverse_of(sums + squares[...], features)
    fill_columns(inverse, scale_b)

    pre = (acc_g[...] + dot_nt(gates[...], scaled[...])) * inverse
    soft = jnp.maximum(pre, 0.0) + jnp.log1p(jnp.exp(-jnp.abs(pre)))
    rate = jnp.concatenate([rates[...]] * (count // 128), axis=1)
    decay = -rate * soft
    beta = jax.nn.sigmoid(pre + rate)
    row_at, col_at = iotas((BLOCK, BLOCK))
    upper = (row_at <= col_at).astype(f32)
    rows_at_head[...] = jnp.zeros_like(rows_at_head)
    for c in range(blocks):
        tokens = slice(c * BLOCK, (c + 1) * BLOCK)
        total = jnp.dot(
            decay[:, tokens], upper, precision=lax.Precision.HIGHEST, preferred_element_type=f32
        )
        totals[c] = total
        rows_at_head[0:16, :] = total
        rows_at_head[16:32, :] = beta[:, tokens]
        columns = rows_at_head[...].T
        for h in range(heads):
            total_b[h, tokens, :] = jnp.broadcast_to(columns[:, h : h + 1], (BLOCK, DK))
            lane = 16 + heads + h
            beta_b[h, tokens, :] = jnp.broadcast_to(columns[:, lane : lane + 1], (BLOCK, DK))

    for copy in rows_copies:
        copy.wait()
    for start in range(0, inner, 256):
        cols = slice(start, start + 256)
        scale = doubled(scale_b[...])
        raw_k[:, cols] = ((acc[0, :, cols] + dot(scaled[...], held[0, :, cols])) * scale).astype(bf16)
        raw_v[:, cols] = ((acc[1, :, cols] + dot(scaled[...], held[1, :, cols])) * scale).astype(bf16)

    xor = jnp.where(row_at > col_at, row_at ^ col_at, 0)
    eye = jnp.where(row_at == col_at, 1.0, 0.0)
    group = 2 if heads % 2 == 0 else 1

    @pl.loop(0, heads // group)
    def _(batch):
        lows, solved = [], []
        chains = []
        for g in range(group):
            h = batch * group + g
            cols = pl.ds(pl.multiple_of(h * DK, DK), DK)
            wide = pl.ds(pl.multiple_of(h * 2 * DK, 2 * DK), 2 * DK)
            raw = raw_k[:, cols].astype(f32)
            unit = raw * lax.rsqrt(jnp.sum(raw * raw, axis=1, keepdims=True) + epsilon)
            keys[:, cols] = unit.astype(bf16)
            for c in range(blocks):
                chains.append((h, cols, wide, c, slice(c * BLOCK, (c + 1) * BLOCK)))
        for h, cols, wide, c, rows in chains:
            k = keys[rows, cols]
            fade = jnp.exp(jnp.minimum(total_b[h, rows, :] - totals[c, pl.ds(h, 1), :], 0.0))
            low = jnp.where(xor > 0, beta_b[h, rows, :] * fade * dot_nt(k, k), 0.0)
            lows.append(low)
            solved.append(eye - jnp.where(xor == 1, low, 0.0))
        size = 2
        while size < BLOCK:
            mask = (xor >= size) & (xor < 2 * size)
            first = []
            for i in range(len(chains)):
                link = jnp.where(mask, lows[i], 0.0).astype(bf16)
                first.append(dot(link, solved[i].astype(bf16)).astype(bf16))
            solved = [
                solved[i] - dot(solved[i].astype(bf16), first[i]) for i in range(len(chains))
            ]
            size *= 2
        grown = []
        for i, (h, cols, wide, c, rows) in enumerate(chains):
            k = keys[rows, cols].astype(f32)
            t_col = total_b[h, rows, :]
            b_col = beta_b[h, rows, :]
            right = jnp.concatenate(
                [
                    (b_col * jnp.exp(t_col) * k).astype(bf16),
                    (b_col * raw_v[rows, cols].astype(f32)).astype(bf16),
                ],
                axis=1,
            )
            both = dot(solved[i].astype(bf16), right).astype(bf16)
            erased[rows, wide] = both
            t_end = t_col[BLOCK - 1 : BLOCK, :]
            faded = (jnp.exp(t_end - t_col) * k).astype(bf16)
            grown.append((jnp.exp(t_end), dot_tn(faded, both)))
        states = [None] * group
        for c in range(blocks):
            for g in range(group):
                h, cols, wide = chains[g * blocks][:3]
                end, product = grown[g * blocks + c]
                erase, write = product[:, :DK], product[:, DK:]
                if c == 0:
                    state = jnp.concatenate([end * eye - erase, write], axis=1)
                else:
                    step = dot(erase.astype(bf16), states[g].astype(bf16))
                    state = (
                        jnp.concatenate([end, end], axis=1) * states[g]
                        - step
                        + jnp.concatenate([jnp.zeros_like(write), write], axis=1)
                    )
                if c < blocks - 1:
                    entry[c, :, wide] = state.astype(bf16)
                states[g] = state
        for g in range(group):
            h = batch * group + g
            half = heads // 2
            mine = (h >= half) == (parity == 1)
            slot = lax.rem(h, half)

            @pl.when(mine)
            def _():
                own[slot] = states[g].astype(bf16)

            @pl.when(jnp.logical_not(mine))
            def _():
                sent[slot] = states[g].astype(bf16)


def block_maps(meta, at, pieces, gain, rates, gates, w_key, w_value, early):
    n = len(pieces)
    acc_k, acc_v, acc_q, acc_g, squares = early
    count = pieces[0].shape[1]
    span = gain.shape[1]
    inner = w_key.shape[1]
    heads = inner // DK
    blocks = count // BLOCK
    return pl.pallas_call(
        functools.partial(maps_kernel, n, heads, at),
        out_shape=(
            shape_of((count, span)),
            shape_of((count, DK), f32),
            shape_of((count, inner)),
            shape_of((count, 2 * inner)),
            shape_of((blocks - 1, DK, 2 * inner)),
            shape_of((heads // 2, DK, 2 * DK)),
            shape_of((heads // 2, DK, 2 * DK)),
            shape_of((blocks, 16, 128), f32),
        ),
        in_specs=[SM] + [ANY] * n + [VM] * 3 + [ANY] * 4 + [VM] * 2,
        out_specs=[VM] * 8,
        scratch_shapes=[
            pltpu.VMEM((span, count), bf16),
            pltpu.VMEM((count, inner), bf16),
            pltpu.VMEM((count, inner), bf16),
            pltpu.VMEM((128, BLOCK), f32),
            pltpu.VMEM((heads, count, DK), f32),
            pltpu.VMEM((heads, count, DK), f32),
            pltpu.VMEM((2, span, inner), bf16),
            pltpu.SemaphoreType.DMA((2,)),
            pltpu.VMEM((2, count, inner), f32),
            pltpu.SemaphoreType.DMA((2,)),
            pltpu.SemaphoreType.DMA((n,)),
        ],
        compiler_params=params(16),
        cost_estimate=cost(10 * 10**9, 14 * 10**6),
        name="block_maps",
    )(meta, *pieces, gain, rates, gates, w_key, w_value, acc_k, acc_v, acc_g, squares)


def query_kernel(n, ys, meta, scaled, scale_b, weights, acc, *refs):
    pieces, (query, tokens_a, tokens_b, done, held, sem) = refs[: n * ys], refs[n * ys :]
    (copy,) = held_rows(meta, CHIP + ys - 1, (weights,), held, sem)
    span = scaled.shape[1]
    part, count = pieces[0].shape
    for d in range(ys):
        for p, slot in enumerate(slots_of(meta, n)):
            piece = pieces[d * n + p]
            base = meta[CHIP + d] * span + slot * part
            step = part // 7

            @pl.loop(0, 7)
            def _(r):
                rows = pl.ds(pl.multiple_of(r * step, 8), step)
                target = pl.ds(pl.multiple_of(base + r * step, 8), step)
                tokens_a[target, :BLOCK] = piece[rows, :BLOCK]
                tokens_a[target, BLOCK:] = piece[rows, count - BLOCK :]
                tokens_b[target, :] = piece[rows, BLOCK : count - BLOCK]

    done[...] = jnp.zeros_like(done)
    copy.wait()
    for start in range(0, query.shape[1], 256):
        cols = slice(start, start + 256)
        product = acc[:, cols] + dot(scaled[...], held[0, :, cols])
        query[:, cols] = (product * doubled(scale_b[...])).astype(bf16)


def queries(meta, ys, scaled, scale_b, weights, acc, pieces):
    n = len(pieces) // ys
    features = weights.shape[0]
    count = acc.shape[0]
    return pl.pallas_call(
        functools.partial(query_kernel, n, ys),
        out_shape=(
            shape_of(acc.shape),
            shape_of((features, 2 * BLOCK)),
            shape_of((features, count - 2 * BLOCK)),
            shape_of((8, 128), f32),
        ),
        in_specs=[SM] + [VM] * 2 + [ANY] + [VM] * (1 + len(pieces)),
        out_specs=[VM] * 4,
        scratch_shapes=[
            pltpu.VMEM((1, scaled.shape[1], acc.shape[1]), bf16),
            pltpu.SemaphoreType.DMA((1,)),
        ],
        compiler_params=params(12),
        cost_estimate=cost(10**9, 8 * 10**6),
        name="queries",
    )(meta, scaled, scale_b, weights, acc, *pieces)


def outputs_kernel(heads, query, keys, erased, entry, totals, after, shard_query, free, done, rows_at_head):
    count = query.shape[0]
    blocks = count // BLOCK
    row_at, col_at = iotas((BLOCK, BLOCK))
    done[...] = jnp.zeros_like(done)
    rows_at_head[...] = jnp.zeros_like(rows_at_head)
    for c in range(blocks):
        rows = slice(c * BLOCK, (c + 1) * BLOCK)
        rows_at_head[0:16, :] = totals[c]
        columns = rows_at_head[...].T
        for h in range(heads):
            cols = slice(h * DK, (h + 1) * DK)
            wide = slice(h * 2 * DK, (h + 1) * 2 * DK)
            t_col = jnp.broadcast_to(columns[:, h : h + 1], (BLOCK, BLOCK))
            t_row = totals[c, h : h + 1, :]
            fade = jnp.where(row_at >= col_at, jnp.exp(jnp.minimum(t_col - t_row, 0.0)), 0.0)
            q = query[rows, cols]
            scores = (fade * dot_nt(q, keys[rows, cols])).astype(bf16)
            both = dot(scores, erased[rows, wide])
            reach = jnp.exp(t_col) * q.astype(f32) - both[:, :DK]
            local = both[:, DK:]
            if c > 0:
                product = dot(reach.astype(bf16), entry[c - 1, :, wide])
                reach = product[:, :DK]
                local = local + product[:, DK:]
            shard_query[rows, cols] = reach.astype(bf16)
            free[rows, cols] = local


def block_outputs(query, keys, erased, entry, totals, after):
    heads = query.shape[1] // DK
    return pl.pallas_call(
        functools.partial(outputs_kernel, heads),
        out_shape=(shape_of(query.shape), shape_of(query.shape, f32), shape_of((8, 128), f32)),
        in_specs=[VM] * 5 + [ANY],
        out_specs=[VM] * 3,
        scratch_shapes=[pltpu.VMEM((128, BLOCK), f32)],
        compiler_params=params(8),
        cost_estimate=cost(3 * 10**9, 4 * 10**6),
        name="block_outputs",
    )(query, keys, erased, entry, totals, after)


def pair_kernel(meta, own, other, pair, first, done):
    even = meta[PARITY] == 0
    for h in range(own.shape[0]):
        mine, theirs = own[h], other[h]
        early = jnp.where(even, mine, theirs)
        late = jnp.where(even, theirs, mine)
        product = dot(late[:, :DK], early)
        shift = late[:, DK:].astype(f32)
        pair[h] = (product + jnp.concatenate([jnp.zeros_like(shift), shift], axis=1)).astype(bf16)
        first[h] = early
    done[...] = jnp.zeros_like(done)


def pair_maps(meta, own, other):
    return pl.pallas_call(
        pair_kernel,
        out_shape=(shape_of(own.shape), shape_of(own.shape), shape_of((8, 128), f32)),
        in_specs=[SM, VM, VM],
        out_specs=[VM] * 3,
        compiler_params=params(4),
        name="pair_maps",
    )(meta, own, other)


def apply_map(whole, state):
    high = state.astype(bf16)
    low = (state - high.astype(f32)).astype(bf16)
    product = dot(whole[:, :DK], jnp.concatenate([high, low], axis=1))
    return product[:, :DK] + product[:, DK:] + whole[:, DK:].astype(f32)


def start_kernel(steps, meta, first, *refs):
    pairs, (after, keep, give) = refs[:steps], refs[steps:]
    even = meta[PARITY] == 0
    for h in range(first.shape[0]):
        state = pairs[0][h][:, DK:].astype(f32)
        for pair in pairs[1:]:
            state = apply_map(pair[h], state)
        later = apply_map(first[h], state)
        keep[h] = jnp.where(even, state, later).astype(bf16)
        give[h] = jnp.where(even, later, state).astype(bf16)


def start_states(meta, first, pairs, after):
    heads = first.shape[0]
    shape = shape_of((heads, DK, DK))
    return pl.pallas_call(
        functools.partial(start_kernel, len(pairs)),
        out_shape=(shape, shape),
        in_specs=[SM] + [VM] * (1 + len(pairs)) + [ANY],
        out_specs=[VM] * 2,
        compiler_params=params(4),
        name="start_states",
    )(meta, first, *pairs, after)


def mixed_kernel(heads, meta, own, other, shard_query, free, gain, mixed_a, mixed_b):
    even = meta[PARITY] == 0
    half = heads // 2
    blocks = shard_query.shape[0] // BLOCK
    for h in range(heads):
        cols = slice(h * DK, (h + 1) * DK)
        if h < half:
            state = jnp.where(even, own[h], other[h])
        else:
            state = jnp.where(even, other[h - half], own[h - half])
        for unit in range(blocks):
            rows = slice(unit * BLOCK, (unit + 1) * BLOCK)
            out = dot(shard_query[rows, cols], state) + free[rows, cols]
            scale = lax.rsqrt(jnp.mean(out * out, axis=1, keepdims=True) + epsilon)
            value = (out * scale * gain[...].astype(f32)).astype(bf16)
            if unit == 0:
                mixed_a[:BLOCK, cols] = value
            elif unit == blocks - 1:
                mixed_a[BLOCK:, cols] = value
            else:
                mixed_b[(unit - 1) * BLOCK : unit * BLOCK, cols] = value


def mixed_heads(meta, own, other, shard_query, free, gain):
    count, inner = shard_query.shape
    return pl.pallas_call(
        functools.partial(mixed_kernel, inner // DK),
        out_shape=(shape_of((2 * BLOCK, inner)), shape_of((count - 2 * BLOCK, inner))),
        in_specs=[SM] + [VM] * 5,
        out_specs=[VM] * 2,
        compiler_params=params(6),
        cost_estimate=cost(10**9, 3 * 10**6),
        name="mixed_heads",
    )(meta, own, other, shard_query, free, gain)


def attend_kernel(ys, meta, tokens, own, partner, weights, partner_weights, *refs):
    far, middle = refs[:-1], refs[-1]
    half = middle.shape[0]
    size = half // 2
    for i in range(2):
        quarter = meta[PARITY] if i == 0 else 1 - meta[PARITY]
        base = meta[CORE] * half + quarter * size
        here = pl.ds(pl.multiple_of(base, 16), size)
        rows = pl.ds(pl.multiple_of(quarter * size, 16), size)
        total = tokens[here, :].astype(f32)
        total = total + dot_nt(weights[here, :], own[...])
        total = total + dot_nt(partner_weights[rows, :], partner[...])
        for d in range(ys - 1):
            same, diagonal, fetched, swapped, far_weights = far[5 * d : 5 * d + 5]
            total = total + dot_nt((fetched if i == 0 else swapped)[...], same[...])
            total = total + dot_nt(far_weights[rows, :], diagonal[...])
        middle[rows, :] = total.astype(bf16)


def attend(meta, ys, tokens, own, partner, weights, partner_weights, far):
    return pl.pallas_call(
        functools.partial(attend_kernel, ys),
        out_shape=shape_of((weights.shape[0] // 2, own.shape[0])),
        in_specs=[SM] + [VM] * (5 + len(far)),
        out_specs=VM,
        compiler_params=params(12),
        cost_estimate=cost(2 * 10**9, 7 * 10**6),
        name="attend",
    )(meta, tokens, own, partner, weights, partner_weights, *far)


def up_kernel(
    meta, own, other, gain, weights, lifted, middle_part, near_row, next_row, middle, hidden, scale_b
):
    features, count = middle.shape
    half = features // 2
    step = 160
    for side, source in ((meta[CORE], own), (1 - meta[CORE], other)):

        @pl.loop(0, half // step)
        def _(r):
            rows = pl.ds(pl.multiple_of(r * step, 32), step)
            target = pl.ds(pl.multiple_of(side * half + r * step, 32), step)
            middle[target, :] = source[rows, :].astype(f32)

    squares = scale_pass(middle, lambda at, size: gain[:, at : at + size], hidden)
    fill_columns(inverse_of(squares, features), scale_b)
    part = middle_part.shape[0]
    middle_part[...] = middle[pl.ds(pl.multiple_of(meta[ME] * part, 8), part), :]
    width = lifted.shape[1]
    for start in range(0, width, 256):
        size = min(256, width - start)
        cols = slice(start, start + size)
        scale = doubled(scale_b[...])[:, :size]
        lifted[:, cols] = (dot(hidden[...], weights[:, cols]) * scale).astype(bf16)
    even = meta[PARITY] == 0
    first, last = lifted[0:1, :], lifted[count - 1 : count, :]
    near_row[...] = jnp.where(even, last, first)
    next_row[...] = jnp.where(even, first, last)


def up_project(meta, own, other, gain, weights, part):
    features, hidden = weights.shape
    count = own.shape[1]
    return pl.pallas_call(
        up_kernel,
        out_shape=(
            shape_of((count, hidden)),
            shape_of((part, count), f32),
            shape_of((1, hidden)),
            shape_of((1, hidden)),
        ),
        in_specs=[SM] + [VM] * 4,
        out_specs=[VM] * 4,
        scratch_shapes=[
            pltpu.VMEM((features, count), f32),
            pltpu.VMEM((count, features), bf16),
            pltpu.VMEM((count, DK), f32),
        ],
        compiler_params=params(16),
        cost_estimate=cost(2 * 10**9, 8 * 10**6),
        name="up_project",
    )(meta, own, other, gain, weights)


def gelu_of(x):
    inner = 0.7978845608028654 * (x + 0.044715 * (x * x * x))
    return 0.5 * x * (1.0 + jnp.tanh(inner))


def act_kernel(late, meta, outer, inside, near_row, next_row, taps, act_t, padded, act):
    count = act.shape[0]
    even = meta[PARITY] == 0
    if late:
        padded[7:8, :] = inside[BLOCK - 1 : BLOCK, :].astype(f32)
        padded[8 : 8 + BLOCK, :] = inside[BLOCK:, :].astype(f32)
        padded[8 + BLOCK : 8 + count, :] = outer[BLOCK:, :].astype(f32)
        padded[8 + count : 9 + count, :] = jnp.where(even, near_row[...], next_row[...]).astype(f32)
    else:
        padded[7:8, :] = jnp.where(even, next_row[...], near_row[...]).astype(f32)
        padded[8 : 8 + BLOCK, :] = outer[:BLOCK, :].astype(f32)
        padded[8 + BLOCK : 8 + count, :] = inside[:BLOCK, :].astype(f32)
        padded[8 + count : 9 + count, :] = inside[BLOCK : BLOCK + 1, :].astype(f32)

    @pl.loop(0, count // 32)
    def _(r):
        base = pl.multiple_of(r * 32, 32)
        window = padded[pl.ds(base, 48), :]
        value = (
            taps[0:1, :] * window[7:39, :]
            + taps[1:2, :] * window[8:40, :]
            + taps[2:3, :] * window[9:41, :]
        )
        act[pl.ds(base, 32), :] = gelu_of(value).astype(bf16)

    act_t[...] = act[...].T


def activate(meta, outer, inside, near_row, next_row, taps, late):
    hidden = outer.shape[1]
    count = (outer.shape[0] + inside.shape[0]) // 2
    return pl.pallas_call(
        functools.partial(act_kernel, late),
        out_shape=shape_of((hidden, count)),
        in_specs=[SM] + [VM] * 5,
        out_specs=VM,
        scratch_shapes=[pltpu.VMEM((count + 16, hidden), f32), pltpu.VMEM((count, hidden), bf16)],
        compiler_params=params(8),
        cost_estimate=cost(10**9, 2 * 10**6),
        name="activate",
    )(meta, outer, inside, near_row, next_row, taps)


def far_kernel(ys, meta, own, other, weights, other_weights, *outs):
    for i, out in enumerate(outs):
        chip = meta[CHIP + ys + i]
        block = 2 * chip + meta[CORE]
        total = dot(weights[block], own[...]) + dot(other_weights[chip], other[...])
        out[...] = total.astype(bf16)


def far_project(meta, ys, own, other, weights, other_weights):
    part = weights.shape[1]
    return pl.pallas_call(
        functools.partial(far_kernel, ys),
        out_shape=[shape_of((part, own.shape[1]))] * (ys - 1),
        in_specs=[SM] + [VM] * 4,
        out_specs=[VM] * (ys - 1),
        compiler_params=params(8),
        cost_estimate=cost(10**9, 4 * 10**6),
        name="far_project",
    )(meta, own, other, weights, other_weights)


def near_kernel(meta, own_a, other_a, own_b, other_b, middle_a, middle_b, weights, other_weights, after, base):
    size = own_a.shape[1]
    middle = (
        jnp.concatenate([middle_a[:, :BLOCK], middle_b[:, :BLOCK]], axis=1),
        jnp.concatenate([middle_b[:, BLOCK:], middle_a[:, BLOCK:]], axis=1),
    )
    for i, (own, other) in enumerate(((own_a, other_a), (own_b, other_b))):
        total = dot(weights[meta[ME]], own[...])
        total = total + dot(other_weights[meta[CHIP]], other[...])
        base[:, i * size : (i + 1) * size] = total + middle[i]


def near_project(meta, own, other, middle_a, middle_b, weights, other_weights, after):
    part = weights.shape[1]
    return pl.pallas_call(
        near_kernel,
        out_shape=shape_of((part, 2 * own[0].shape[1]), f32),
        in_specs=[SM] + [VM] * 8 + [ANY],
        out_specs=VM,
        compiler_params=params(10),
        cost_estimate=cost(2 * 10**9, 6 * 10**6),
        name="near_project",
    )(meta, own[0], other[0], own[1], other[1], middle_a, middle_b, weights, other_weights, after)


def core_swap(value, n):
    return lax.ppermute(value, "head", [(i, i ^ 1) for i in range(n)])


def y_shift(value, n, step):
    return lax.ppermute(value, "head", [(i, (i + 2 * step) % n) for i in range(n)])


def pair_swap(value, n):
    return lax.ppermute(value, "seq", [(i, i ^ 1) for i in range(n)])


def later(value, n, step):
    return lax.ppermute(value, "seq", [(i, i + 2 * step) for i in range(n - 2 * step)])


def shards(
    tokens,
    norm_gain,
    w_query,
    w_key,
    w_value,
    w_decay,
    w_beta,
    head_rates,
    head_gain,
    w_out,
    ffn_gain,
    w_up,
    conv_taps,
    w_down,
):
    n = lax.axis_size("head")
    seqs = lax.axis_size("seq")
    me = lax.axis_index("head")
    at = lax.axis_index("seq")
    core = me % 2
    parity = at % 2
    ys = n // 2
    count, part = tokens.shape
    heads = w_query.shape[1] // DK
    hidden = w_up.shape[1]
    features = n * part

    mine = tokens.T
    shifted = [mine] + [y_shift(mine, n, d) for d in range(1, ys)]

    def group_of(piece):
        partner = core_swap(piece, n)
        if part % 16:
            first = jnp.where(core == 0, piece, partner)
            second = jnp.where(core == 0, partner, piece)
            return [jnp.concatenate([first, second], axis=0)]
        return [piece, partner]

    groups = [group_of(mine)]
    chip = me // 2
    here = [parity, core, me]
    sources = [(chip + ys - d) % ys for d in range(ys)]
    targets = [(chip + d) % ys for d in range(1, ys)]
    meta = jnp.stack(here + sources + targets).astype(jnp.int32)

    w_out_t = w_out.T
    w_parts = w_down.T.reshape(n, part, hidden)

    gates = jnp.concatenate([w_decay.T, w_beta.T], axis=0)
    gates = jnp.pad(gates, ((0, 16 - 2 * heads), (0, 0)))
    gates = gates.reshape(16, ys, 2 * part).transpose(1, 0, 2)
    rates = jnp.pad(head_rates.reshape(2 * heads, 1), ((0, 16 - 2 * heads), (0, 0)))
    rates = jnp.broadcast_to(rates, (16, 128))
    gain = norm_gain.astype(f32).reshape(ys, 1, 2 * part)

    def ours(rows, d):
        return lax.dynamic_index_in_dim(rows, sources[d], 0, False)

    ffn_scale = ffn_gain.astype(f32).reshape(1, features)
    taps = conv_taps.astype(f32)

    gains = [ours(gain, d) for d in range(ys)]
    gate_rows = [ours(gates, d) for d in range(ys)]
    gains, gate_rows, rates, taps, ffn_scale, head_scale, meta = lax.optimization_barrier(
        (gains, gate_rows, rates, taps, ffn_scale, head_gain.reshape(1, DK), meta)
    )

    early = None
    for d in range(ys - 1):
        early = early_project(
            meta, CHIP + d, groups[d], gains[d], gate_rows[d], w_key, w_value, w_query, w_parts, w_out_t, early
        )
        if d == 0:
            sent, early = early[5:], early[:5]
        piece, _ = lax.optimization_barrier((shifted[d + 1], early[4]))
        groups.append(group_of(piece))
    scaled, scale_b, keys, erased, entry, own_maps, sent_maps, totals = block_maps(
        meta, CHIP + ys - 1, groups[-1], gains[-1], rates, gate_rows[-1], w_key, w_value, early
    )

    sent, _ = lax.optimization_barrier((sent, groups[-1][-1]))
    sent_w_down, their_rows, my_rows = sent
    other_w_down = core_swap(sent_w_down, n)
    fetched = [y_shift(my_rows, n, d) for d in range(1, ys)]
    diagonal = [
        lax.ppermute(their_rows, "head", [(i, ((i + 2 * d) % n) ^ 1) for i in range(n)])
        for d in range(1, ys)
    ]
    partner_w_out = core_swap(their_rows, n)
    other_maps = pair_swap(sent_maps, seqs)
    pair, first, done = pair_maps(meta, own_maps, other_maps)
    fetched, _ = lax.optimization_barrier((fetched, done))
    swapped = [pair_swap(value, seqs) for value in fetched]
    pairs = [later(pair, seqs, d) for d in range(seqs // 2 - 1, 0, -1)]
    acc_query, partner_w_out, other_w_down, _ = lax.optimization_barrier(
        (early[2], partner_w_out, other_w_down, done)
    )
    query, tokens_a, tokens_b, _ = queries(
        meta, ys, scaled, scale_b, w_query, acc_query, sum(groups, [])
    )
    shard_query, free, out_done = block_outputs(query, keys, erased, entry, totals, done)
    kept_state, given_state = start_states(meta, first, pairs, out_done)
    other_state = pair_swap(given_state, seqs)

    mixed = mixed_heads(meta, kept_state, other_state, shard_query, free, head_scale)
    far_mixed = [[y_shift(value, n, d) for d in range(1, ys)] for value in mixed]


    def middle_of(i, far):
        heads_far = [[value, core_swap(value, n)] for value in far]
        operands = []
        for pair_of, *weights in zip(heads_far, fetched, swapped, diagonal):
            operands += pair_of + weights
        own_tokens = (tokens_a, tokens_b)[i]
        return attend(
            meta, ys, own_tokens, mixed[i], core_swap(mixed[i], n), w_out_t, partner_w_out, operands
        )

    middle = middle_of(0, far_mixed[0])
    outer, middle_a, near_row, next_row = up_project(
        meta, middle, core_swap(middle, n), ffn_scale, w_up, part
    )
    near_row = lax.ppermute(near_row, "seq", [(i, i ^ 1) for i in range(seqs)])
    next_row = lax.ppermute(
        next_row, "seq", [(i, ((i + 1) ^ 1) - 1) for i in range(1, seqs - 1)]
    )
    middle = middle_of(1, far_mixed[1])
    inside, middle_b, _, _ = up_project(
        meta, middle, core_swap(middle, n), ffn_scale, w_up, part
    )

    acts = [activate(meta, outer, inside, near_row, next_row, taps, late) for late in (False, True)]
    partner_acts = [core_swap(act, n) for act in acts]
    fars = [
        far_project(meta, ys, act, partner, w_parts, other_w_down)
        for act, partner in zip(acts, partner_acts)
    ]
    total = near_project(
        meta, acts, partner_acts, middle_a, middle_b, w_parts, other_w_down, fars[1][0]
    )
    for d in range(1, ys):
        halves = [y_shift(far[d - 1], n, d) for far in fars]
        total = total + jnp.concatenate(halves, axis=1).astype(f32)
    return total.astype(bf16).T


def solution(mesh):
    placed = (
        P("seq", "head"),
        P(),
        P(None, "head"),
        P(None, "head"),
        P(None, "head"),
        P(None, "head"),
        P(None, "head"),
        P(None, "head"),
        P(),
        P("head", None),
        P(),
        P(None, "head"),
        P(None, "head"),
        P("head", None),
    )
    return jax.shard_map(
        shards, mesh=mesh, in_specs=placed, out_specs=P("seq", "head"), check_vma=False
    )
```

```python
import functools

import jax
import jax.numpy as jnp
from jax import lax
from jax.experimental import pallas as pl
from jax.experimental.pallas import tpu as pltpu
from jax.sharding import PartitionSpec as P

DK = 128
BLOCK = 128
epsilon = 1e-06
f32 = jnp.float32
bf16 = jnp.bfloat16

PARITY, CORE, ME, CHIP = 0, 1, 2, 3

VM = pl.BlockSpec(memory_space=pltpu.VMEM)
SM = pl.BlockSpec(memory_space=pltpu.SMEM)
ANY = pl.BlockSpec(memory_space=pl.ANY)


def params(mebibytes):
    return pltpu.CompilerParams(vmem_limit_bytes=mebibytes * 1024 * 1024)


def cost(flops, moved):
    return pl.CostEstimate(flops=flops, bytes_accessed=moved, transcendentals=0)


def shape_of(shape, dtype=bf16):
    return jax.ShapeDtypeStruct(shape, dtype)


def dot(a, b):
    return jnp.dot(a, b, preferred_element_type=f32)


def dot_nt(a, b):
    return lax.dot_general(a, b, (((1,), (1,)), ((), ())), preferred_element_type=f32)


def dot_tn(a, b):
    return lax.dot_general(a, b, (((0,), (0,)), ((), ())), preferred_element_type=f32)


def iotas(shape):
    return lax.broadcasted_iota(jnp.int32, shape, 0), lax.broadcasted_iota(jnp.int32, shape, 1)


def column_of(row, lanes=128):
    return jnp.broadcast_to(row, (lanes, row.shape[1])).T


def scale_pass(source, gain_at, target):
    features, tokens = source.shape
    squares = jnp.zeros((8, tokens), f32)
    for start in range(0, features, 128):
        size = min(128, features - start)
        value = source[start : start + size, :].astype(f32)
        scale = column_of(gain_at(start, size))
        scale = jnp.concatenate([scale] * (tokens // 128), axis=1)
        target[:, start : start + size] = (value * scale).astype(bf16).T
        value = value * value
        for r in range(0, size, 8):
            squares = squares + value[r : r + 8]
    return squares


def inverse_of(squares, features):
    return lax.rsqrt(jnp.sum(squares, axis=0, keepdims=True) / features + epsilon)


def fill_columns(row, target):
    for start in range(0, row.shape[1], 128):
        target[start : start + 128, :] = column_of(row[:, start : start + 128])


def doubled(tile):
    return jnp.concatenate([tile, tile], axis=1)


def slots_of(meta, n):
    return [meta[CORE], 1 - meta[CORE]] if n == 2 else [0]


def load_pair(meta, pieces, whole, sem):
    part = pieces[0].shape[0]
    copies = [
        pltpu.make_async_copy(
            piece, whole.at[pl.ds(pl.multiple_of(slot * part, 16), part)], sem.at[p]
        )
        for p, (piece, slot) in enumerate(zip(pieces, slots_of(meta, len(pieces))))
    ]
    for copy in copies:
        copy.start()
    for copy in copies:
        copy.wait()


def held_rows(meta, at, weights, held, sem):
    span = held.shape[1]
    rows = pl.ds(pl.multiple_of(meta[at] * span, 16), span)
    copies = [
        pltpu.make_async_copy(ref.at[rows], held.at[i], sem.at[i]) for i, ref in enumerate(weights)
    ]
    for copy in copies:
        copy.start()
    return copies


def early_kernel(count_in, at, meta, *refs):
    first = at == CHIP
    pieces = refs[:count_in]
    gain, gates, w_key, w_value, w_query, w_down, w_out = refs[count_in : count_in + 7]
    refs = refs[count_in + 7 :]
    before, refs = (None, refs) if first else (refs[:5], refs[5:])
    acc_k, acc_v, acc_q, acc_g, squares = refs[:5]
    sent, (whole, scaled, held, held_sem, sem) = (refs[5:8], refs[8:]) if first else ((), refs[5:])
    rows_copies = held_rows(meta, at, (w_key, w_value, w_query), held, held_sem)
    copies = []
    if first:
        partner_w, their_rows, my_rows = sent
        ys = partner_w.shape[0]
        copies = [
            pltpu.make_async_copy(
                w_down.at[2 * y + 1 - meta[CORE]], partner_w.at[y], sem.at[count_in + y]
            )
            for y in range(ys)
        ]
        for i, (start, target) in enumerate(
            (
                ((1 - meta[CORE]) * 2 * my_rows.shape[0], their_rows),
                ((2 * meta[CORE] + meta[PARITY]) * my_rows.shape[0], my_rows),
            )
        ):
            rows = pl.ds(pl.multiple_of(start, 16), target.shape[0])
            copies.append(
                pltpu.make_async_copy(w_out.at[rows], target, sem.at[count_in + ys + i])
            )
    for copy in copies:
        copy.start()
    load_pair(meta, pieces, whole, sem)
    sums = scale_pass(whole, lambda at, size: gain[:, at : at + size], scaled)
    gate = dot_nt(gates[...], scaled[...])
    squares[...] = sums if first else before[4][...] + sums
    acc_g[...] = gate if first else before[3][...] + gate
    for i, out in enumerate((acc_k, acc_v, acc_q)):
        rows_copies[i].wait()
        product = dot(scaled[...], held[i])
        out[...] = product if first else before[i][...] + product
    for copy in copies:
        copy.wait()


def early_project(meta, at, pieces, gain, gates, w_key, w_value, w_query, w_down, w_out, before):
    first = before is None
    blocks, part, hidden = w_down.shape
    ys = blocks // 2
    span = gain.shape[1]
    count = pieces[0].shape[1]
    features, inner = w_key.shape
    return pl.pallas_call(
        functools.partial(early_kernel, len(pieces), at),
        out_shape=[shape_of((count, inner), f32)] * 3
        + [shape_of((16, count), f32), shape_of((8, count), f32)]
        + [
            shape_of((ys, part, hidden)),
            shape_of((features // 2, inner)),
            shape_of((features // 4, inner)),
        ]
        * first,
        in_specs=[SM] + [ANY] * len(pieces) + [VM] * 2 + [ANY] * 5 + [VM] * (0 if first else 5),
        out_specs=[VM] * (8 if first else 5),
        scratch_shapes=[
            pltpu.VMEM((span, count), bf16),
            pltpu.VMEM((count, span), bf16),
            pltpu.VMEM((3, span, inner), bf16),
            pltpu.SemaphoreType.DMA((3,)),
            pltpu.SemaphoreType.DMA((len(pieces) + ys + 2,)),
        ],
        compiler_params=params(48),
        cost_estimate=cost(3 * 10**9, 8 * 10**6),
        name="early_project",
    )(meta, *pieces, gain, gates, w_key, w_value, w_query, w_down, w_out, *(before or ()))


def maps_kernel(n, heads, at, meta, *refs):
    pieces = refs[:n]
    gain, rates, gates, w_key, w_value, acc_k, acc_v, acc_g, squares = refs[n : n + 9]
    scaled, scale_b, keys, erased, entry, own, sent, totals = refs[n + 9 : n + 17]
    whole, raw_k, raw_v, rows_at_head, total_b, beta_b, held, held_sem, acc, acc_sem, sem = refs[
        n + 17 :
    ]
    span, count = whole.shape
    blocks = count // BLOCK
    inner = heads * DK
    features = w_key.shape[0]
    parity = meta[PARITY]
    rows_copies = held_rows(meta, at, (w_key, w_value), held, held_sem)
    rows_copies += [
        pltpu.make_async_copy(ref, acc.at[i], acc_sem.at[i]) for i, ref in enumerate((acc_k, acc_v))
    ]
    for copy in rows_copies[2:]:
        copy.start()
    load_pair(meta, pieces, whole, sem)
    sums = scale_pass(whole, lambda at, size: gain[:, at : at + size], scaled)
    inverse = inverse_of(sums + squares[...], features)
    fill_columns(inverse, scale_b)

    pre = (acc_g[...] + dot_nt(gates[...], scaled[...])) * inverse
    soft = jnp.maximum(pre, 0.0) + jnp.log1p(jnp.exp(-jnp.abs(pre)))
    rate = jnp.concatenate([rates[...]] * (count // 128), axis=1)
    decay = -rate * soft
    beta = jax.nn.sigmoid(pre + rate)
    row_at, col_at = iotas((BLOCK, BLOCK))
    upper = (row_at <= col_at).astype(f32)
    rows_at_head[...] = jnp.zeros_like(rows_at_head)
    for c in range(blocks):
        tokens = slice(c * BLOCK, (c + 1) * BLOCK)
        total = jnp.dot(
            decay[:, tokens], upper, precision=lax.Precision.HIGHEST, preferred_element_type=f32
        )
        totals[c] = total
        rows_at_head[0:16, :] = total
        rows_at_head[16:32, :] = beta[:, tokens]
        columns = rows_at_head[...].T
        for h in range(heads):
            total_b[h, tokens, :] = jnp.broadcast_to(columns[:, h : h + 1], (BLOCK, DK))
            lane = 16 + heads + h
            beta_b[h, tokens, :] = jnp.broadcast_to(columns[:, lane : lane + 1], (BLOCK, DK))

    for copy in rows_copies:
        copy.wait()
    for start in range(0, inner, 256):
        cols = slice(start, start + 256)
        scale = doubled(scale_b[...])
        raw_k[:, cols] = ((acc[0, :, cols] + dot(scaled[...], held[0, :, cols])) * scale).astype(bf16)
        raw_v[:, cols] = ((acc[1, :, cols] + dot(scaled[...], held[1, :, cols])) * scale).astype(bf16)

    xor = jnp.where(row_at > col_at, row_at ^ col_at, 0)
    eye = jnp.where(row_at == col_at, 1.0, 0.0)
    group = 2 if heads % 2 == 0 else 1

    @pl.loop(0, heads // group)
    def _(batch):
        lows, solved = [], []
        chains = []
        for g in range(group):
            h = batch * group + g
            cols = pl.ds(pl.multiple_of(h * DK, DK), DK)
            wide = pl.ds(pl.multiple_of(h * 2 * DK, 2 * DK), 2 * DK)
            raw = raw_k[:, cols].astype(f32)
            unit = raw * lax.rsqrt(jnp.sum(raw * raw, axis=1, keepdims=True) + epsilon)
            keys[:, cols] = unit.astype(bf16)
            for c in range(blocks):
                chains.append((h, cols, wide, c, slice(c * BLOCK, (c + 1) * BLOCK)))
        for h, cols, wide, c, rows in chains:
            k = keys[rows, cols]
            fade = jnp.exp(jnp.minimum(total_b[h, rows, :] - totals[c, pl.ds(h, 1), :], 0.0))
            low = jnp.where(xor > 0, beta_b[h, rows, :] * fade * dot_nt(k, k), 0.0)
            lows.append(low)
            solved.append(eye - jnp.where(xor == 1, low, 0.0))
        size = 2
        while size < BLOCK:
            mask = (xor >= size) & (xor < 2 * size)
            first = []
            for i in range(len(chains)):
                link = jnp.where(mask, lows[i], 0.0).astype(bf16)
                first.append(dot(link, solved[i].astype(bf16)).astype(bf16))
            solved = [
                solved[i] - dot(solved[i].astype(bf16), first[i]) for i in range(len(chains))
            ]
            size *= 2
        grown = []
        for i, (h, cols, wide, c, rows) in enumerate(chains):
            k = keys[rows, cols].astype(f32)
            t_col = total_b[h, rows, :]
            b_col = beta_b[h, rows, :]
            right = jnp.concatenate(
                [
                    (b_col * jnp.exp(t_col) * k).astype(bf16),
                    (b_col * raw_v[rows, cols].astype(f32)).astype(bf16),
                ],
                axis=1,
            )
            both = dot(solved[i].astype(bf16), right).astype(bf16)
            erased[rows, wide] = both
            t_end = t_col[BLOCK - 1 : BLOCK, :]
            faded = (jnp.exp(t_end - t_col) * k).astype(bf16)
            grown.append((jnp.exp(t_end), dot_tn(faded, both)))
        states = [None] * group
        for c in range(blocks):
            for g in range(group):
                h, cols, wide = chains[g * blocks][:3]
                end, product = grown[g * blocks + c]
                erase, write = product[:, :DK], product[:, DK:]
                if c == 0:
                    state = jnp.concatenate([end * eye - erase, write], axis=1)
                else:
                    step = dot(erase.astype(bf16), states[g].astype(bf16))
                    state = (
                        jnp.concatenate([end, end], axis=1) * states[g]
                        - step
                        + jnp.concatenate([jnp.zeros_like(write), write], axis=1)
                    )
                if c < blocks - 1:
                    entry[c, :, wide] = state.astype(bf16)
                states[g] = state
        for g in range(group):
            h = batch * group + g
            half = heads // 2
            mine = (h >= half) == (parity == 1)
            slot = lax.rem(h, half)

            @pl.when(mine)
            def _():
                own[slot] = states[g].astype(bf16)

            @pl.when(jnp.logical_not(mine))
            def _():
                sent[slot] = states[g].astype(bf16)


def block_maps(meta, at, pieces, gain, rates, gates, w_key, w_value, early):
    n = len(pieces)
    acc_k, acc_v, acc_q, acc_g, squares = early
    count = pieces[0].shape[1]
    span = gain.shape[1]
    inner = w_key.shape[1]
    heads = inner // DK
    blocks = count // BLOCK
    return pl.pallas_call(
        functools.partial(maps_kernel, n, heads, at),
        out_shape=(
            shape_of((count, span)),
            shape_of((count, DK), f32),
            shape_of((count, inner)),
            shape_of((count, 2 * inner)),
            shape_of((blocks - 1, DK, 2 * inner)),
            shape_of((heads // 2, DK, 2 * DK)),
            shape_of((heads // 2, DK, 2 * DK)),
            shape_of((blocks, 16, 128), f32),
        ),
        in_specs=[SM] + [ANY] * n + [VM] * 3 + [ANY] * 4 + [VM] * 2,
        out_specs=[VM] * 8,
        scratch_shapes=[
            pltpu.VMEM((span, count), bf16),
            pltpu.VMEM((count, inner), bf16),
            pltpu.VMEM((count, inner), bf16),
            pltpu.VMEM((128, BLOCK), f32),
            pltpu.VMEM((heads, count, DK), f32),
            pltpu.VMEM((heads, count, DK), f32),
            pltpu.VMEM((2, span, inner), bf16),
            pltpu.SemaphoreType.DMA((2,)),
            pltpu.VMEM((2, count, inner), f32),
            pltpu.SemaphoreType.DMA((2,)),
            pltpu.SemaphoreType.DMA((n,)),
        ],
        compiler_params=params(16),
        cost_estimate=cost(10 * 10**9, 14 * 10**6),
        name="block_maps",
    )(meta, *pieces, gain, rates, gates, w_key, w_value, acc_k, acc_v, acc_g, squares)


def query_kernel(n, ys, meta, scaled, scale_b, weights, acc, *refs):
    pieces, (query, tokens_a, tokens_b, done, held, sem) = refs[: n * ys], refs[n * ys :]
    (copy,) = held_rows(meta, CHIP + ys - 1, (weights,), held, sem)
    span = scaled.shape[1]
    part, count = pieces[0].shape
    for d in range(ys):
        for p, slot in enumerate(slots_of(meta, n)):
            piece = pieces[d * n + p]
            base = meta[CHIP + d] * span + slot * part
            step = part // 7

            @pl.loop(0, 7)
            def _(r):
                rows = pl.ds(pl.multiple_of(r * step, 8), step)
                target = pl.ds(pl.multiple_of(base + r * step, 8), step)
                tokens_a[target, :BLOCK] = piece[rows, :BLOCK]
                tokens_a[target, BLOCK:] = piece[rows, count - BLOCK :]
                tokens_b[target, :] = piece[rows, BLOCK : count - BLOCK]

    done[...] = jnp.zeros_like(done)
    copy.wait()
    for start in range(0, query.shape[1], 256):
        cols = slice(start, start + 256)
        product = acc[:, cols] + dot(scaled[...], held[0, :, cols])
        query[:, cols] = (product * doubled(scale_b[...])).astype(bf16)


def queries(meta, ys, scaled, scale_b, weights, acc, pieces):
    n = len(pieces) // ys
    features = weights.shape[0]
    count = acc.shape[0]
    return pl.pallas_call(
        functools.partial(query_kernel, n, ys),
        out_shape=(
            shape_of(acc.shape),
            shape_of((features, 2 * BLOCK)),
            shape_of((features, count - 2 * BLOCK)),
            shape_of((8, 128), f32),
        ),
        in_specs=[SM] + [VM] * 2 + [ANY] + [VM] * (1 + len(pieces)),
        out_specs=[VM] * 4,
        scratch_shapes=[
            pltpu.VMEM((1, scaled.shape[1], acc.shape[1]), bf16),
            pltpu.SemaphoreType.DMA((1,)),
        ],
        compiler_params=params(12),
        cost_estimate=cost(10**9, 8 * 10**6),
        name="queries",
    )(meta, scaled, scale_b, weights, acc, *pieces)


def outputs_kernel(heads, query, keys, erased, entry, totals, after, shard_query, free, done, rows_at_head):
    count = query.shape[0]
    blocks = count // BLOCK
    row_at, col_at = iotas((BLOCK, BLOCK))
    done[...] = jnp.zeros_like(done)
    rows_at_head[...] = jnp.zeros_like(rows_at_head)
    for c in range(blocks):
        rows = slice(c * BLOCK, (c + 1) * BLOCK)
        rows_at_head[0:16, :] = totals[c]
        columns = rows_at_head[...].T
        for h in range(heads):
            cols = slice(h * DK, (h + 1) * DK)
            wide = slice(h * 2 * DK, (h + 1) * 2 * DK)
            t_col = jnp.broadcast_to(columns[:, h : h + 1], (BLOCK, BLOCK))
            t_row = totals[c, h : h + 1, :]
            fade = jnp.where(row_at >= col_at, jnp.exp(jnp.minimum(t_col - t_row, 0.0)), 0.0)
            q = query[rows, cols]
            scores = (fade * dot_nt(q, keys[rows, cols])).astype(bf16)
            both = dot(scores, erased[rows, wide])
            reach = jnp.exp(t_col) * q.astype(f32) - both[:, :DK]
            local = both[:, DK:]
            if c > 0:
                product = dot(reach.astype(bf16), entry[c - 1, :, wide])
                reach = product[:, :DK]
                local = local + product[:, DK:]
            shard_query[rows, cols] = reach.astype(bf16)
            free[rows, cols] = local


def block_outputs(query, keys, erased, entry, totals, after):
    heads = query.shape[1] // DK
    return pl.pallas_call(
        functools.partial(outputs_kernel, heads),
        out_shape=(shape_of(query.shape), shape_of(query.shape, f32), shape_of((8, 128), f32)),
        in_specs=[VM] * 5 + [ANY],
        out_specs=[VM] * 3,
        scratch_shapes=[pltpu.VMEM((128, BLOCK), f32)],
        compiler_params=params(8),
        cost_estimate=cost(3 * 10**9, 4 * 10**6),
        name="block_outputs",
    )(query, keys, erased, entry, totals, after)


def pair_kernel(meta, own, other, pair_map, pair_shift, first, done):
    even = meta[PARITY] == 0
    for h in range(own.shape[0]):
        mine, theirs = own[h], other[h]
        early = jnp.where(even, mine, theirs)
        late = jnp.where(even, theirs, mine)
        product = dot(late[:, :DK], early)
        shift = late[:, DK:].astype(f32)
        pair_map[h] = product[:, :DK].astype(bf16)
        pair_shift[h] = (product[:, DK:] + shift).astype(bf16)
        first[h] = early
    done[...] = jnp.zeros_like(done)


def pair_maps(meta, own, other):
    half = shape_of((own.shape[0], DK, DK))
    return pl.pallas_call(
        pair_kernel,
        out_shape=(half, half, shape_of(own.shape), shape_of((8, 128), f32)),
        in_specs=[SM, VM, VM],
        out_specs=[VM] * 4,
        compiler_params=params(4),
        name="pair_maps",
    )(meta, own, other)


def apply_map(matrix, shift, state):
    high = state.astype(bf16)
    low = (state - high.astype(f32)).astype(bf16)
    product = dot(matrix, jnp.concatenate([high, low], axis=1))
    return product[:, :DK] + product[:, DK:] + shift.astype(f32)


def start_kernel(steps, meta, first, *refs):
    maps, shifts, (after, keep, give) = refs[: steps - 1], refs[steps - 1 : -3], refs[-3:]
    even = meta[PARITY] == 0
    for h in range(first.shape[0]):
        state = shifts[0][h].astype(f32)
        for matrix, shift in zip(maps, shifts[1:]):
            state = apply_map(matrix[h], shift[h], state)
        later = apply_map(first[h][:, :DK], first[h][:, DK:], state)
        keep[h] = jnp.where(even, state, later).astype(bf16)
        give[h] = jnp.where(even, later, state).astype(bf16)


def start_states(meta, first, maps, shifts, after):
    heads = first.shape[0]
    shape = shape_of((heads, DK, DK))
    return pl.pallas_call(
        functools.partial(start_kernel, len(shifts)),
        out_shape=(shape, shape),
        in_specs=[SM] + [VM] * (1 + len(maps) + len(shifts)) + [ANY],
        out_specs=[VM] * 2,
        compiler_params=params(4),
        name="start_states",
    )(meta, first, *maps, *shifts, after)


def mixed_kernel(heads, meta, own, other, shard_query, free, gain, mixed_a, mixed_b):
    even = meta[PARITY] == 0
    half = heads // 2
    blocks = shard_query.shape[0] // BLOCK
    for h in range(heads):
        cols = slice(h * DK, (h + 1) * DK)
        if h < half:
            state = jnp.where(even, own[h], other[h])
        else:
            state = jnp.where(even, other[h - half], own[h - half])
        for unit in range(blocks):
            rows = slice(unit * BLOCK, (unit + 1) * BLOCK)
            out = dot(shard_query[rows, cols], state) + free[rows, cols]
            scale = lax.rsqrt(jnp.mean(out * out, axis=1, keepdims=True) + epsilon)
            value = (out * scale * gain[...].astype(f32)).astype(bf16)
            if unit == 0:
                mixed_a[:BLOCK, cols] = value
            elif unit == blocks - 1:
                mixed_a[BLOCK:, cols] = value
            else:
                mixed_b[(unit - 1) * BLOCK : unit * BLOCK, cols] = value


def mixed_heads(meta, own, other, shard_query, free, gain):
    count, inner = shard_query.shape
    return pl.pallas_call(
        functools.partial(mixed_kernel, inner // DK),
        out_shape=(shape_of((2 * BLOCK, inner)), shape_of((count - 2 * BLOCK, inner))),
        in_specs=[SM] + [VM] * 5,
        out_specs=[VM] * 2,
        compiler_params=params(6),
        cost_estimate=cost(10**9, 3 * 10**6),
        name="mixed_heads",
    )(meta, own, other, shard_query, free, gain)


def attend_kernel(ys, meta, tokens, own, partner, weights, partner_weights, *refs):
    far, middle = refs[:-1], refs[-1]
    half = middle.shape[0]
    size = half // 2
    for i in range(2):
        quarter = meta[PARITY] if i == 0 else 1 - meta[PARITY]
        base = meta[CORE] * half + quarter * size
        here = pl.ds(pl.multiple_of(base, 16), size)
        rows = pl.ds(pl.multiple_of(quarter * size, 16), size)
        total = tokens[here, :].astype(f32)
        total = total + dot_nt(weights[here, :], own[...])
        total = total + dot_nt(partner_weights[rows, :], partner[...])
        for d in range(ys - 1):
            same, diagonal, fetched, swapped, far_weights = far[5 * d : 5 * d + 5]
            total = total + dot_nt((fetched if i == 0 else swapped)[...], same[...])
            total = total + dot_nt(far_weights[rows, :], diagonal[...])
        middle[rows, :] = total.astype(bf16)


def attend(meta, ys, tokens, own, partner, weights, partner_weights, far):
    return pl.pallas_call(
        functools.partial(attend_kernel, ys),
        out_shape=shape_of((weights.shape[0] // 2, own.shape[0])),
        in_specs=[SM] + [VM] * (5 + len(far)),
        out_specs=VM,
        compiler_params=params(12),
        cost_estimate=cost(2 * 10**9, 7 * 10**6),
        name="attend",
    )(meta, tokens, own, partner, weights, partner_weights, *far)


def up_kernel(
    meta, own, other, gain, weights, lifted, middle_part, near_row, next_row, middle, hidden, scale_b
):
    features, count = middle.shape
    half = features // 2
    step = 160
    for side, source in ((meta[CORE], own), (1 - meta[CORE], other)):

        @pl.loop(0, half // step)
        def _(r):
            rows = pl.ds(pl.multiple_of(r * step, 32), step)
            target = pl.ds(pl.multiple_of(side * half + r * step, 32), step)
            middle[target, :] = source[rows, :].astype(f32)

    squares = scale_pass(middle, lambda at, size: gain[:, at : at + size], hidden)
    fill_columns(inverse_of(squares, features), scale_b)
    part = middle_part.shape[0]
    middle_part[...] = middle[pl.ds(pl.multiple_of(meta[ME] * part, 8), part), :]
    width = lifted.shape[1]
    for start in range(0, width, 256):
        size = min(256, width - start)
        cols = slice(start, start + size)
        scale = doubled(scale_b[...])[:, :size]
        lifted[:, cols] = (dot(hidden[...], weights[:, cols]) * scale).astype(bf16)
    even = meta[PARITY] == 0
    first, last = lifted[0:1, :], lifted[count - 1 : count, :]
    near_row[...] = jnp.where(even, last, first)
    next_row[...] = jnp.where(even, first, last)


def up_project(meta, own, other, gain, weights, part):
    features, hidden = weights.shape
    count = own.shape[1]
    return pl.pallas_call(
        up_kernel,
        out_shape=(
            shape_of((count, hidden)),
            shape_of((part, count), f32),
            shape_of((1, hidden)),
            shape_of((1, hidden)),
        ),
        in_specs=[SM] + [VM] * 4,
        out_specs=[VM] * 4,
        scratch_shapes=[
            pltpu.VMEM((features, count), f32),
            pltpu.VMEM((count, features), bf16),
            pltpu.VMEM((count, DK), f32),
        ],
        compiler_params=params(16),
        cost_estimate=cost(2 * 10**9, 8 * 10**6),
        name="up_project",
    )(meta, own, other, gain, weights)


def gelu_of(x):
    inner = 0.7978845608028654 * (x + 0.044715 * (x * x * x))
    return 0.5 * x * (1.0 + jnp.tanh(inner))


def act_kernel(late, meta, outer, inside, near_row, next_row, taps, act_t, padded, act):
    count = act.shape[0]
    even = meta[PARITY] == 0
    if late:
        padded[7:8, :] = inside[BLOCK - 1 : BLOCK, :].astype(f32)
        padded[8 : 8 + BLOCK, :] = inside[BLOCK:, :].astype(f32)
        padded[8 + BLOCK : 8 + count, :] = outer[BLOCK:, :].astype(f32)
        padded[8 + count : 9 + count, :] = jnp.where(even, near_row[...], next_row[...]).astype(f32)
    else:
        padded[7:8, :] = jnp.where(even, next_row[...], near_row[...]).astype(f32)
        padded[8 : 8 + BLOCK, :] = outer[:BLOCK, :].astype(f32)
        padded[8 + BLOCK : 8 + count, :] = inside[:BLOCK, :].astype(f32)
        padded[8 + count : 9 + count, :] = inside[BLOCK : BLOCK + 1, :].astype(f32)

    @pl.loop(0, count // 32)
    def _(r):
        base = pl.multiple_of(r * 32, 32)
        window = padded[pl.ds(base, 48), :]
        value = (
            taps[0:1, :] * window[7:39, :]
            + taps[1:2, :] * window[8:40, :]
            + taps[2:3, :] * window[9:41, :]
        )
        act[pl.ds(base, 32), :] = gelu_of(value).astype(bf16)

    act_t[...] = act[...].T


def activate(meta, outer, inside, near_row, next_row, taps, late):
    hidden = outer.shape[1]
    count = (outer.shape[0] + inside.shape[0]) // 2
    return pl.pallas_call(
        functools.partial(act_kernel, late),
        out_shape=shape_of((hidden, count)),
        in_specs=[SM] + [VM] * 5,
        out_specs=VM,
        scratch_shapes=[pltpu.VMEM((count + 16, hidden), f32), pltpu.VMEM((count, hidden), bf16)],
        compiler_params=params(8),
        cost_estimate=cost(10**9, 2 * 10**6),
        name="activate",
    )(meta, outer, inside, near_row, next_row, taps)


def far_kernel(ys, meta, own, other, weights, other_weights, *outs):
    for i, out in enumerate(outs):
        chip = meta[CHIP + ys + i]
        block = 2 * chip + meta[CORE]
        total = dot(weights[block], own[...]) + dot(other_weights[chip], other[...])
        out[...] = total.astype(bf16)


def far_project(meta, ys, own, other, weights, other_weights):
    part = weights.shape[1]
    return pl.pallas_call(
        functools.partial(far_kernel, ys),
        out_shape=[shape_of((part, own.shape[1]))] * (ys - 1),
        in_specs=[SM] + [VM] * 4,
        out_specs=[VM] * (ys - 1),
        compiler_params=params(8),
        cost_estimate=cost(10**9, 4 * 10**6),
        name="far_project",
    )(meta, own, other, weights, other_weights)


def near_kernel(meta, own_a, other_a, own_b, other_b, middle_a, middle_b, weights, other_weights, after, base):
    size = own_a.shape[1]
    middle = (
        jnp.concatenate([middle_a[:, :BLOCK], middle_b[:, :BLOCK]], axis=1),
        jnp.concatenate([middle_b[:, BLOCK:], middle_a[:, BLOCK:]], axis=1),
    )
    for i, (own, other) in enumerate(((own_a, other_a), (own_b, other_b))):
        total = dot(weights[meta[ME]], own[...])
        total = total + dot(other_weights[meta[CHIP]], other[...])
        base[:, i * size : (i + 1) * size] = total + middle[i]


def near_project(meta, own, other, middle_a, middle_b, weights, other_weights, after):
    part = weights.shape[1]
    return pl.pallas_call(
        near_kernel,
        out_shape=shape_of((part, 2 * own[0].shape[1]), f32),
        in_specs=[SM] + [VM] * 8 + [ANY],
        out_specs=VM,
        compiler_params=params(10),
        cost_estimate=cost(2 * 10**9, 6 * 10**6),
        name="near_project",
    )(meta, own[0], other[0], own[1], other[1], middle_a, middle_b, weights, other_weights, after)


def core_swap(value, n):
    return lax.ppermute(value, "head", [(i, i ^ 1) for i in range(n)])


def y_shift(value, n, step):
    return lax.ppermute(value, "head", [(i, (i + 2 * step) % n) for i in range(n)])


def pair_swap(value, n):
    return lax.ppermute(value, "seq", [(i, i ^ 1) for i in range(n)])


def later(value, n, step, start=0):
    return lax.ppermute(value, "seq", [(i, i + 2 * step) for i in range(start, n - 2 * step)])


def shards(
    tokens,
    norm_gain,
    w_query,
    w_key,
    w_value,
    w_decay,
    w_beta,
    head_rates,
    head_gain,
    w_out,
    ffn_gain,
    w_up,
    conv_taps,
    w_down,
):
    n = lax.axis_size("head")
    seqs = lax.axis_size("seq")
    me = lax.axis_index("head")
    at = lax.axis_index("seq")
    core = me % 2
    parity = at % 2
    ys = n // 2
    count, part = tokens.shape
    heads = w_query.shape[1] // DK
    hidden = w_up.shape[1]
    features = n * part

    mine = tokens.T
    shifted = [mine] + [y_shift(mine, n, d) for d in range(1, ys)]

    def group_of(piece):
        partner = core_swap(piece, n)
        if part % 16:
            first = jnp.where(core == 0, piece, partner)
            second = jnp.where(core == 0, partner, piece)
            return [jnp.concatenate([first, second], axis=0)]
        return [piece, partner]

    groups = [group_of(mine)]
    chip = me // 2
    here = [parity, core, me]
    sources = [(chip + ys - d) % ys for d in range(ys)]
    targets = [(chip + d) % ys for d in range(1, ys)]
    meta = jnp.stack(here + sources + targets).astype(jnp.int32)

    w_out_t = w_out.T
    w_parts = w_down.T.reshape(n, part, hidden)

    gates = jnp.concatenate([w_decay.T, w_beta.T], axis=0)
    gates = jnp.pad(gates, ((0, 16 - 2 * heads), (0, 0)))
    gates = gates.reshape(16, ys, 2 * part).transpose(1, 0, 2)
    rates = jnp.pad(head_rates.reshape(2 * heads, 1), ((0, 16 - 2 * heads), (0, 0)))
    rates = jnp.broadcast_to(rates, (16, 128))
    gain = norm_gain.astype(f32).reshape(ys, 1, 2 * part)

    def ours(rows, d):
        return lax.dynamic_index_in_dim(rows, sources[d], 0, False)

    ffn_scale = ffn_gain.astype(f32).reshape(1, features)
    taps = conv_taps.astype(f32)

    gains = [ours(gain, d) for d in range(ys)]
    gate_rows = [ours(gates, d) for d in range(ys)]
    gains, gate_rows, rates, taps, ffn_scale, head_scale, meta = lax.optimization_barrier(
        (gains, gate_rows, rates, taps, ffn_scale, head_gain.reshape(1, DK), meta)
    )

    early = None
    for d in range(ys - 1):
        early = early_project(
            meta, CHIP + d, groups[d], gains[d], gate_rows[d], w_key, w_value, w_query, w_parts, w_out_t, early
        )
        if d == 0:
            sent, early = early[5:], early[:5]
        piece, _ = lax.optimization_barrier((shifted[d + 1], early[4]))
        groups.append(group_of(piece))
    scaled, scale_b, keys, erased, entry, own_maps, sent_maps, totals = block_maps(
        meta, CHIP + ys - 1, groups[-1], gains[-1], rates, gate_rows[-1], w_key, w_value, early
    )

    sent, _ = lax.optimization_barrier((sent, groups[-1][-1]))
    sent_w_down, their_rows, my_rows = sent
    other_w_down = core_swap(sent_w_down, n)
    fetched = [y_shift(my_rows, n, d) for d in range(1, ys)]
    diagonal = [
        lax.ppermute(their_rows, "head", [(i, ((i + 2 * d) % n) ^ 1) for i in range(n)])
        for d in range(1, ys)
    ]
    partner_w_out = core_swap(their_rows, n)
    other_maps = pair_swap(sent_maps, seqs)
    pair_map, pair_shift, first, done = pair_maps(meta, own_maps, other_maps)
    fetched, _ = lax.optimization_barrier((fetched, done))
    swapped = [pair_swap(value, seqs) for value in fetched]
    shifts = [later(pair_shift, seqs, d) for d in range(seqs // 2 - 1, 0, -1)]
    maps = [later(pair_map, seqs, d, 2) for d in range(seqs // 2 - 2, 0, -1)]
    acc_query, partner_w_out, other_w_down, _ = lax.optimization_barrier(
        (early[2], partner_w_out, other_w_down, done)
    )
    query, tokens_a, tokens_b, _ = queries(
        meta, ys, scaled, scale_b, w_query, acc_query, sum(groups, [])
    )
    shard_query, free, out_done = block_outputs(query, keys, erased, entry, totals, done)
    kept_state, given_state = start_states(meta, first, maps, shifts, out_done)
    other_state = pair_swap(given_state, seqs)

    mixed = mixed_heads(meta, kept_state, other_state, shard_query, free, head_scale)
    far_mixed = [[y_shift(value, n, d) for d in range(1, ys)] for value in mixed]


    def middle_of(i, far):
        heads_far = [[value, core_swap(value, n)] for value in far]
        operands = []
        for pair_of, *weights in zip(heads_far, fetched, swapped, diagonal):
            operands += pair_of + weights
        own_tokens = (tokens_a, tokens_b)[i]
        return attend(
            meta, ys, own_tokens, mixed[i], core_swap(mixed[i], n), w_out_t, partner_w_out, operands
        )

    middle = middle_of(0, far_mixed[0])
    outer, middle_a, near_row, next_row = up_project(
        meta, middle, core_swap(middle, n), ffn_scale, w_up, part
    )
    near_row = lax.ppermute(near_row, "seq", [(i, i ^ 1) for i in range(seqs)])
    next_row = lax.ppermute(
        next_row, "seq", [(i, ((i + 1) ^ 1) - 1) for i in range(1, seqs - 1)]
    )
    middle = middle_of(1, far_mixed[1])
    inside, middle_b, _, _ = up_project(
        meta, middle, core_swap(middle, n), ffn_scale, w_up, part
    )

    acts = [activate(meta, outer, inside, near_row, next_row, taps, late) for late in (False, True)]
    partner_acts = [core_swap(act, n) for act in acts]
    fars = [
        far_project(meta, ys, act, partner, w_parts, other_w_down)
        for act, partner in zip(acts, partner_acts)
    ]
    total = near_project(
        meta, acts, partner_acts, middle_a, middle_b, w_parts, other_w_down, fars[1][0]
    )
    for d in range(1, ys):
        halves = [y_shift(far[d - 1], n, d) for far in fars]
        total = total + jnp.concatenate(halves, axis=1).astype(f32)
    return total.astype(bf16).T


def solution(mesh):
    placed = (
        P("seq", "head"),
        P(),
        P(None, "head"),
        P(None, "head"),
        P(None, "head"),
        P(None, "head"),
        P(None, "head"),
        P(None, "head"),
        P(),
        P("head", None),
        P(),
        P(None, "head"),
        P(None, "head"),
        P("head", None),
    )
    return jax.shard_map(
        shards, mesh=mesh, in_specs=placed, out_specs=P("seq", "head"), check_vma=False
    )
```

```python
import functools

import jax
import jax.numpy as jnp
from jax import lax
from jax.experimental import pallas as pl
from jax.experimental.pallas import tpu as pltpu
from jax.sharding import PartitionSpec as P

DK = 128
BLOCK = 128
epsilon = 1e-06
f32 = jnp.float32
bf16 = jnp.bfloat16

PARITY, CORE, ME, CHIP = 0, 1, 2, 3

VM = pl.BlockSpec(memory_space=pltpu.VMEM)
SM = pl.BlockSpec(memory_space=pltpu.SMEM)
ANY = pl.BlockSpec(memory_space=pl.ANY)


def params(mebibytes):
    return pltpu.CompilerParams(vmem_limit_bytes=mebibytes * 1024 * 1024)


def cost(flops, moved):
    return pl.CostEstimate(flops=flops, bytes_accessed=moved, transcendentals=0)


def shape_of(shape, dtype=bf16):
    return jax.ShapeDtypeStruct(shape, dtype)


def dot(a, b):
    return jnp.dot(a, b, preferred_element_type=f32)


def dot_nt(a, b):
    return lax.dot_general(a, b, (((1,), (1,)), ((), ())), preferred_element_type=f32)


def dot_tn(a, b):
    return lax.dot_general(a, b, (((0,), (0,)), ((), ())), preferred_element_type=f32)


def iotas(shape):
    return lax.broadcasted_iota(jnp.int32, shape, 0), lax.broadcasted_iota(jnp.int32, shape, 1)


def column_of(row, lanes=128):
    return jnp.broadcast_to(row, (lanes, row.shape[1])).T


def scale_pass(source, gain_at, target):
    features, tokens = source.shape
    squares = jnp.zeros((8, tokens), f32)
    for start in range(0, features, 128):
        size = min(128, features - start)
        value = source[start : start + size, :].astype(f32)
        scale = column_of(gain_at(start, size))
        scale = jnp.concatenate([scale] * (tokens // 128), axis=1)
        target[:, start : start + size] = (value * scale).astype(bf16).T
        value = value * value
        for r in range(0, size, 8):
            squares = squares + value[r : r + 8]
    return squares


def inverse_of(squares, features):
    return lax.rsqrt(jnp.sum(squares, axis=0, keepdims=True) / features + epsilon)


def fill_columns(row, target):
    for start in range(0, row.shape[1], 128):
        target[start : start + 128, :] = column_of(row[:, start : start + 128])


def later_rows(tile, size):
    return jnp.concatenate(
        [tile[at + size : at + 2 * size] for at in range(0, tile.shape[0], 2 * size)], axis=0
    )


def spread_rows(tile, size):
    empty = jnp.zeros((size, tile.shape[1]), tile.dtype)
    parts = []
    for at in range(0, tile.shape[0], size):
        parts += [empty, tile[at : at + size]]
    return jnp.concatenate(parts, axis=0)


def doubled(tile):
    return jnp.concatenate([tile, tile], axis=1)


def slots_of(meta, n):
    return [meta[CORE], 1 - meta[CORE]] if n == 2 else [0]


def load_pair(meta, pieces, whole, sem):
    part = pieces[0].shape[0]
    copies = [
        pltpu.make_async_copy(
            piece, whole.at[pl.ds(pl.multiple_of(slot * part, 16), part)], sem.at[p]
        )
        for p, (piece, slot) in enumerate(zip(pieces, slots_of(meta, len(pieces))))
    ]
    for copy in copies:
        copy.start()
    for copy in copies:
        copy.wait()


def held_rows(meta, at, weights, held, sem):
    span = held.shape[1]
    rows = pl.ds(pl.multiple_of(meta[at] * span, 16), span)
    copies = [
        pltpu.make_async_copy(ref.at[rows], held.at[i], sem.at[i]) for i, ref in enumerate(weights)
    ]
    for copy in copies:
        copy.start()
    return copies


def early_kernel(count_in, at, meta, *refs):
    first = at == CHIP
    pieces = refs[:count_in]
    gain, gates, w_key, w_value, w_query, w_down, w_out = refs[count_in : count_in + 7]
    refs = refs[count_in + 7 :]
    before, refs = (None, refs) if first else (refs[:5], refs[5:])
    acc_k, acc_v, acc_q, acc_g, squares = refs[:5]
    sent, (whole, scaled, held, held_sem, sem) = (refs[5:8], refs[8:]) if first else ((), refs[5:])
    rows_copies = held_rows(meta, at, (w_key, w_value, w_query), held, held_sem)
    copies = []
    if first:
        partner_w, their_rows, my_rows = sent
        ys = partner_w.shape[0]
        copies = [
            pltpu.make_async_copy(
                w_down.at[2 * y + 1 - meta[CORE]], partner_w.at[y], sem.at[count_in + y]
            )
            for y in range(ys)
        ]
        for i, (start, target) in enumerate(
            (
                ((1 - meta[CORE]) * 2 * my_rows.shape[0], their_rows),
                ((2 * meta[CORE] + meta[PARITY]) * my_rows.shape[0], my_rows),
            )
        ):
            rows = pl.ds(pl.multiple_of(start, 16), target.shape[0])
            copies.append(
                pltpu.make_async_copy(w_out.at[rows], target, sem.at[count_in + ys + i])
            )
    for copy in copies:
        copy.start()
    load_pair(meta, pieces, whole, sem)
    sums = scale_pass(whole, lambda at, size: gain[:, at : at + size], scaled)
    gate = dot_nt(gates[...], scaled[...])
    squares[...] = sums if first else before[4][...] + sums
    acc_g[...] = gate if first else before[3][...] + gate
    for i, out in enumerate((acc_k, acc_v, acc_q)):
        rows_copies[i].wait()
        product = dot(scaled[...], held[i])
        out[...] = product if first else before[i][...] + product
    for copy in copies:
        copy.wait()


def early_project(meta, at, pieces, gain, gates, w_key, w_value, w_query, w_down, w_out, before):
    first = before is None
    blocks, part, hidden = w_down.shape
    ys = blocks // 2
    span = gain.shape[1]
    count = pieces[0].shape[1]
    features, inner = w_key.shape
    return pl.pallas_call(
        functools.partial(early_kernel, len(pieces), at),
        out_shape=[shape_of((count, inner), f32)] * 3
        + [shape_of((16, count), f32), shape_of((8, count), f32)]
        + [
            shape_of((ys, part, hidden)),
            shape_of((features // 2, inner)),
            shape_of((features // 4, inner)),
        ]
        * first,
        in_specs=[SM] + [ANY] * len(pieces) + [VM] * 2 + [ANY] * 5 + [VM] * (0 if first else 5),
        out_specs=[VM] * (8 if first else 5),
        scratch_shapes=[
            pltpu.VMEM((span, count), bf16),
            pltpu.VMEM((count, span), bf16),
            pltpu.VMEM((3, span, inner), bf16),
            pltpu.SemaphoreType.DMA((3,)),
            pltpu.SemaphoreType.DMA((len(pieces) + ys + 2,)),
        ],
        compiler_params=params(48),
        cost_estimate=cost(3 * 10**9, 8 * 10**6),
        name="early_project",
    )(meta, *pieces, gain, gates, w_key, w_value, w_query, w_down, w_out, *(before or ()))


def maps_kernel(n, heads, at, meta, *refs):
    pieces = refs[:n]
    gain, rates, gates, w_key, w_value, acc_k, acc_v, acc_g, squares = refs[n : n + 9]
    scaled, scale_b, keys, erased, entry, own, sent, totals = refs[n + 9 : n + 17]
    whole, raw_k, raw_v, rows_at_head, total_b, beta_b, held, held_sem, acc, acc_sem, sem = refs[
        n + 17 :
    ]
    span, count = whole.shape
    blocks = count // BLOCK
    inner = heads * DK
    features = w_key.shape[0]
    parity = meta[PARITY]
    rows_copies = held_rows(meta, at, (w_key, w_value), held, held_sem)
    rows_copies += [
        pltpu.make_async_copy(ref, acc.at[i], acc_sem.at[i]) for i, ref in enumerate((acc_k, acc_v))
    ]
    for copy in rows_copies[2:]:
        copy.start()
    load_pair(meta, pieces, whole, sem)
    sums = scale_pass(whole, lambda at, size: gain[:, at : at + size], scaled)
    inverse = inverse_of(sums + squares[...], features)
    fill_columns(inverse, scale_b)

    pre = (acc_g[...] + dot_nt(gates[...], scaled[...])) * inverse
    soft = jnp.maximum(pre, 0.0) + jnp.log1p(jnp.exp(-jnp.abs(pre)))
    rate = jnp.concatenate([rates[...]] * (count // 128), axis=1)
    decay = -rate * soft
    beta = jax.nn.sigmoid(pre + rate)
    row_at, col_at = iotas((BLOCK, BLOCK))
    upper = (row_at <= col_at).astype(f32)
    rows_at_head[...] = jnp.zeros_like(rows_at_head)
    for c in range(blocks):
        tokens = slice(c * BLOCK, (c + 1) * BLOCK)
        total = jnp.dot(
            decay[:, tokens], upper, precision=lax.Precision.HIGHEST, preferred_element_type=f32
        )
        totals[c] = total
        rows_at_head[0:16, :] = total
        rows_at_head[16:32, :] = beta[:, tokens]
        columns = rows_at_head[...].T
        for h in range(heads):
            total_b[h, tokens, :] = jnp.broadcast_to(columns[:, h : h + 1], (BLOCK, DK))
            lane = 16 + heads + h
            beta_b[h, tokens, :] = jnp.broadcast_to(columns[:, lane : lane + 1], (BLOCK, DK))

    for copy in rows_copies:
        copy.wait()
    for start in range(0, inner, 256):
        cols = slice(start, start + 256)
        scale = doubled(scale_b[...])
        raw_k[:, cols] = ((acc[0, :, cols] + dot(scaled[...], held[0, :, cols])) * scale).astype(bf16)
        raw_v[:, cols] = ((acc[1, :, cols] + dot(scaled[...], held[1, :, cols])) * scale).astype(bf16)

    xor = jnp.where(row_at > col_at, row_at ^ col_at, 0)
    eye = jnp.where(row_at == col_at, 1.0, 0.0)
    group = 2 if heads % 2 == 0 else 1

    @pl.loop(0, heads // group)
    def _(batch):
        lows, solved = [], []
        chains = []
        for g in range(group):
            h = batch * group + g
            cols = pl.ds(pl.multiple_of(h * DK, DK), DK)
            wide = pl.ds(pl.multiple_of(h * 2 * DK, 2 * DK), 2 * DK)
            raw = raw_k[:, cols].astype(f32)
            unit = raw * lax.rsqrt(jnp.sum(raw * raw, axis=1, keepdims=True) + epsilon)
            keys[:, cols] = unit.astype(bf16)
            for c in range(blocks):
                chains.append((h, cols, wide, c, slice(c * BLOCK, (c + 1) * BLOCK)))
        for h, cols, wide, c, rows in chains:
            k = keys[rows, cols]
            fade = jnp.exp(jnp.minimum(total_b[h, rows, :] - totals[c, pl.ds(h, 1), :], 0.0))
            low = jnp.where(xor > 0, beta_b[h, rows, :] * fade * dot_nt(k, k), 0.0)
            lows.append(low)
            solved.append(eye - jnp.where(xor == 1, low, 0.0))
        size = 2
        steps = [None] * len(chains)
        while size < BLOCK:
            if size >= 16:
                mask = later_rows(xor, size) >= size
                for i in range(len(chains)):
                    link = jnp.where(mask & (later_rows(xor, size) < 2 * size), later_rows(lows[i], size), 0.0)
                    whole_b = solved[i].astype(bf16)
                    moved = dot(link.astype(bf16), whole_b).astype(bf16)
                    steps[i] = dot(later_rows(whole_b, size), spread_rows(moved, size))
                solved = [solved[i] - spread_rows(steps[i], size) for i in range(len(chains))]
                size *= 2
                continue
            mask = (xor >= size) & (xor < 2 * size)
            first = []
            for i in range(len(chains)):
                link = jnp.where(mask, lows[i], 0.0).astype(bf16)
                first.append(dot(link, solved[i].astype(bf16)).astype(bf16))
            solved = [
                solved[i] - dot(solved[i].astype(bf16), first[i]) for i in range(len(chains))
            ]
            size *= 2
        grown = []
        for i, (h, cols, wide, c, rows) in enumerate(chains):
            k = keys[rows, cols].astype(f32)
            t_col = total_b[h, rows, :]
            b_col = beta_b[h, rows, :]
            right = jnp.concatenate(
                [
                    (b_col * jnp.exp(t_col) * k).astype(bf16),
                    (b_col * raw_v[rows, cols].astype(f32)).astype(bf16),
                ],
                axis=1,
            )
            both = dot(solved[i].astype(bf16), right).astype(bf16)
            erased[rows, wide] = both
            t_end = t_col[BLOCK - 1 : BLOCK, :]
            faded = (jnp.exp(t_end - t_col) * k).astype(bf16)
            grown.append((jnp.exp(t_end), dot_tn(faded, both)))
        states = [None] * group
        for c in range(blocks):
            for g in range(group):
                h, cols, wide = chains[g * blocks][:3]
                end, product = grown[g * blocks + c]
                erase, write = product[:, :DK], product[:, DK:]
                if c == 0:
                    state = jnp.concatenate([end * eye - erase, write], axis=1)
                else:
                    step = dot(erase.astype(bf16), states[g].astype(bf16))
                    state = (
                        jnp.concatenate([end, end], axis=1) * states[g]
                        - step
                        + jnp.concatenate([jnp.zeros_like(write), write], axis=1)
                    )
                if c < blocks - 1:
                    entry[c, :, wide] = state.astype(bf16)
                states[g] = state
        for g in range(group):
            h = batch * group + g
            half = heads // 2
            mine = (h >= half) == (parity == 1)
            slot = lax.rem(h, half)

            @pl.when(mine)
            def _():
                own[slot] = states[g].astype(bf16)

            @pl.when(jnp.logical_not(mine))
            def _():
                sent[slot] = states[g].astype(bf16)


def block_maps(meta, at, pieces, gain, rates, gates, w_key, w_value, early):
    n = len(pieces)
    acc_k, acc_v, acc_q, acc_g, squares = early
    count = pieces[0].shape[1]
    span = gain.shape[1]
    inner = w_key.shape[1]
    heads = inner // DK
    blocks = count // BLOCK
    return pl.pallas_call(
        functools.partial(maps_kernel, n, heads, at),
        out_shape=(
            shape_of((count, span)),
            shape_of((count, DK), f32),
            shape_of((count, inner)),
            shape_of((count, 2 * inner)),
            shape_of((blocks - 1, DK, 2 * inner)),
            shape_of((heads // 2, DK, 2 * DK)),
            shape_of((heads // 2, DK, 2 * DK)),
            shape_of((blocks, 16, 128), f32),
        ),
        in_specs=[SM] + [ANY] * n + [VM] * 3 + [ANY] * 4 + [VM] * 2,
        out_specs=[VM] * 8,
        scratch_shapes=[
            pltpu.VMEM((span, count), bf16),
            pltpu.VMEM((count, inner), bf16),
            pltpu.VMEM((count, inner), bf16),
            pltpu.VMEM((128, BLOCK), f32),
            pltpu.VMEM((heads, count, DK), f32),
            pltpu.VMEM((heads, count, DK), f32),
            pltpu.VMEM((2, span, inner), bf16),
            pltpu.SemaphoreType.DMA((2,)),
            pltpu.VMEM((2, count, inner), f32),
            pltpu.SemaphoreType.DMA((2,)),
            pltpu.SemaphoreType.DMA((n,)),
        ],
        compiler_params=params(16),
        cost_estimate=cost(10 * 10**9, 14 * 10**6),
        name="block_maps",
    )(meta, *pieces, gain, rates, gates, w_key, w_value, acc_k, acc_v, acc_g, squares)


def query_kernel(n, ys, meta, scaled, scale_b, weights, acc, *refs):
    pieces, (query, tokens_a, tokens_b, done, held, sem) = refs[: n * ys], refs[n * ys :]
    (copy,) = held_rows(meta, CHIP + ys - 1, (weights,), held, sem)
    span = scaled.shape[1]
    part, count = pieces[0].shape
    for d in range(ys):
        for p, slot in enumerate(slots_of(meta, n)):
            piece = pieces[d * n + p]
            base = meta[CHIP + d] * span + slot * part
            step = part // 7

            @pl.loop(0, 7)
            def _(r):
                rows = pl.ds(pl.multiple_of(r * step, 8), step)
                target = pl.ds(pl.multiple_of(base + r * step, 8), step)
                tokens_a[target, :BLOCK] = piece[rows, :BLOCK]
                tokens_a[target, BLOCK:] = piece[rows, count - BLOCK :]
                tokens_b[target, :] = piece[rows, BLOCK : count - BLOCK]

    done[...] = jnp.zeros_like(done)
    copy.wait()
    for start in range(0, query.shape[1], 256):
        cols = slice(start, start + 256)
        product = acc[:, cols] + dot(scaled[...], held[0, :, cols])
        query[:, cols] = (product * doubled(scale_b[...])).astype(bf16)


def queries(meta, ys, scaled, scale_b, weights, acc, pieces):
    n = len(pieces) // ys
    features = weights.shape[0]
    count = acc.shape[0]
    return pl.pallas_call(
        functools.partial(query_kernel, n, ys),
        out_shape=(
            shape_of(acc.shape),
            shape_of((features, 2 * BLOCK)),
            shape_of((features, count - 2 * BLOCK)),
            shape_of((8, 128), f32),
        ),
        in_specs=[SM] + [VM] * 2 + [ANY] + [VM] * (1 + len(pieces)),
        out_specs=[VM] * 4,
        scratch_shapes=[
            pltpu.VMEM((1, scaled.shape[1], acc.shape[1]), bf16),
            pltpu.SemaphoreType.DMA((1,)),
        ],
        compiler_params=params(12),
        cost_estimate=cost(10**9, 8 * 10**6),
        name="queries",
    )(meta, scaled, scale_b, weights, acc, *pieces)


def outputs_kernel(heads, query, keys, erased, entry, totals, after, shard_query, free, done, rows_at_head):
    count = query.shape[0]
    blocks = count // BLOCK
    row_at, col_at = iotas((BLOCK, BLOCK))
    done[...] = jnp.zeros_like(done)
    rows_at_head[...] = jnp.zeros_like(rows_at_head)
    for c in range(blocks):
        rows = slice(c * BLOCK, (c + 1) * BLOCK)
        rows_at_head[0:16, :] = totals[c]
        columns = rows_at_head[...].T
        for h in range(heads):
            cols = slice(h * DK, (h + 1) * DK)
            wide = slice(h * 2 * DK, (h + 1) * 2 * DK)
            t_col = jnp.broadcast_to(columns[:, h : h + 1], (BLOCK, BLOCK))
            t_row = totals[c, h : h + 1, :]
            fade = jnp.where(row_at >= col_at, jnp.exp(jnp.minimum(t_col - t_row, 0.0)), 0.0)
            q = query[rows, cols]
            scores = (fade * dot_nt(q, keys[rows, cols])).astype(bf16)
            both = dot(scores, erased[rows, wide])
            reach = jnp.exp(t_col) * q.astype(f32) - both[:, :DK]
            local = both[:, DK:]
            if c > 0:
                product = dot(reach.astype(bf16), entry[c - 1, :, wide])
                reach = product[:, :DK]
                local = local + product[:, DK:]
            shard_query[rows, cols] = reach.astype(bf16)
            free[rows, cols] = local


def block_outputs(query, keys, erased, entry, totals, after):
    heads = query.shape[1] // DK
    return pl.pallas_call(
        functools.partial(outputs_kernel, heads),
        out_shape=(shape_of(query.shape), shape_of(query.shape, f32), shape_of((8, 128), f32)),
        in_specs=[VM] * 5 + [ANY],
        out_specs=[VM] * 3,
        scratch_shapes=[pltpu.VMEM((128, BLOCK), f32)],
        compiler_params=params(8),
        cost_estimate=cost(3 * 10**9, 4 * 10**6),
        name="block_outputs",
    )(query, keys, erased, entry, totals, after)


def pair_kernel(meta, own, other, pair_map, pair_shift, first, done):
    even = meta[PARITY] == 0
    for h in range(own.shape[0]):
        mine, theirs = own[h], other[h]
        early = jnp.where(even, mine, theirs)
        late = jnp.where(even, theirs, mine)
        product = dot(late[:, :DK], early)
        shift = late[:, DK:].astype(f32)
        pair_map[h] = product[:, :DK].astype(bf16)
        pair_shift[h] = (product[:, DK:] + shift).astype(bf16)
        first[h] = early
    done[...] = jnp.zeros_like(done)


def pair_maps(meta, own, other):
    half = shape_of((own.shape[0], DK, DK))
    return pl.pallas_call(
        pair_kernel,
        out_shape=(half, half, shape_of(own.shape), shape_of((8, 128), f32)),
        in_specs=[SM, VM, VM],
        out_specs=[VM] * 4,
        compiler_params=params(4),
        name="pair_maps",
    )(meta, own, other)


def apply_map(matrix, shift, state):
    high = state.astype(bf16)
    low = (state - high.astype(f32)).astype(bf16)
    product = dot(matrix, jnp.concatenate([high, low], axis=1))
    return product[:, :DK] + product[:, DK:] + shift.astype(f32)


def start_kernel(steps, meta, first, *refs):
    maps, shifts, (after, keep, give) = refs[: steps - 1], refs[steps - 1 : -3], refs[-3:]
    even = meta[PARITY] == 0
    for h in range(first.shape[0]):
        state = shifts[0][h].astype(f32)
        for matrix, shift in zip(maps, shifts[1:]):
            state = apply_map(matrix[h], shift[h], state)
        later = apply_map(first[h][:, :DK], first[h][:, DK:], state)
        keep[h] = jnp.where(even, state, later).astype(bf16)
        give[h] = jnp.where(even, later, state).astype(bf16)


def start_states(meta, first, maps, shifts, after):
    heads = first.shape[0]
    shape = shape_of((heads, DK, DK))
    return pl.pallas_call(
        functools.partial(start_kernel, len(shifts)),
        out_shape=(shape, shape),
        in_specs=[SM] + [VM] * (1 + len(maps) + len(shifts)) + [ANY],
        out_specs=[VM] * 2,
        compiler_params=params(4),
        name="start_states",
    )(meta, first, *maps, *shifts, after)


def mixed_kernel(heads, meta, own, other, shard_query, free, gain, mixed_a, mixed_b):
    even = meta[PARITY] == 0
    half = heads // 2
    blocks = shard_query.shape[0] // BLOCK
    for h in range(heads):
        cols = slice(h * DK, (h + 1) * DK)
        if h < half:
            state = jnp.where(even, own[h], other[h])
        else:
            state = jnp.where(even, other[h - half], own[h - half])
        for unit in range(blocks):
            rows = slice(unit * BLOCK, (unit + 1) * BLOCK)
            out = dot(shard_query[rows, cols], state) + free[rows, cols]
            scale = lax.rsqrt(jnp.mean(out * out, axis=1, keepdims=True) + epsilon)
            value = (out * scale * gain[...].astype(f32)).astype(bf16)
            if unit == 0:
                mixed_a[:BLOCK, cols] = value
            elif unit == blocks - 1:
                mixed_a[BLOCK:, cols] = value
            else:
                mixed_b[(unit - 1) * BLOCK : unit * BLOCK, cols] = value


def mixed_heads(meta, own, other, shard_query, free, gain):
    count, inner = shard_query.shape
    return pl.pallas_call(
        functools.partial(mixed_kernel, inner // DK),
        out_shape=(shape_of((2 * BLOCK, inner)), shape_of((count - 2 * BLOCK, inner))),
        in_specs=[SM] + [VM] * 5,
        out_specs=[VM] * 2,
        compiler_params=params(6),
        cost_estimate=cost(10**9, 3 * 10**6),
        name="mixed_heads",
    )(meta, own, other, shard_query, free, gain)


def attend_kernel(ys, meta, tokens, own, partner, weights, partner_weights, *refs):
    far, middle = refs[:-1], refs[-1]
    half = middle.shape[0]
    size = half // 2
    for i in range(2):
        quarter = meta[PARITY] if i == 0 else 1 - meta[PARITY]
        base = meta[CORE] * half + quarter * size
        here = pl.ds(pl.multiple_of(base, 16), size)
        rows = pl.ds(pl.multiple_of(quarter * size, 16), size)
        total = tokens[here, :].astype(f32)
        total = total + dot_nt(weights[here, :], own[...])
        total = total + dot_nt(partner_weights[rows, :], partner[...])
        for d in range(ys - 1):
            same, diagonal, fetched, swapped, far_weights = far[5 * d : 5 * d + 5]
            total = total + dot_nt((fetched if i == 0 else swapped)[...], same[...])
            total = total + dot_nt(far_weights[rows, :], diagonal[...])
        middle[rows, :] = total.astype(bf16)


def attend(meta, ys, tokens, own, partner, weights, partner_weights, far):
    return pl.pallas_call(
        functools.partial(attend_kernel, ys),
        out_shape=shape_of((weights.shape[0] // 2, own.shape[0])),
        in_specs=[SM] + [VM] * (5 + len(far)),
        out_specs=VM,
        compiler_params=params(12),
        cost_estimate=cost(2 * 10**9, 7 * 10**6),
        name="attend",
    )(meta, tokens, own, partner, weights, partner_weights, *far)


def up_kernel(
    meta, own, other, gain, weights, lifted, middle_part, near_row, next_row, middle, hidden, scale_b
):
    features, count = middle.shape
    half = features // 2
    step = 160
    for side, source in ((meta[CORE], own), (1 - meta[CORE], other)):

        @pl.loop(0, half // step)
        def _(r):
            rows = pl.ds(pl.multiple_of(r * step, 32), step)
            target = pl.ds(pl.multiple_of(side * half + r * step, 32), step)
            middle[target, :] = source[rows, :].astype(f32)

    squares = scale_pass(middle, lambda at, size: gain[:, at : at + size], hidden)
    fill_columns(inverse_of(squares, features), scale_b)
    part = middle_part.shape[0]
    middle_part[...] = middle[pl.ds(pl.multiple_of(meta[ME] * part, 8), part), :]
    width = lifted.shape[1]
    for start in range(0, width, 256):
        size = min(256, width - start)
        cols = slice(start, start + size)
        scale = doubled(scale_b[...])[:, :size]
        lifted[:, cols] = (dot(hidden[...], weights[:, cols]) * scale).astype(bf16)
    even = meta[PARITY] == 0
    first, last = lifted[0:1, :], lifted[count - 1 : count, :]
    near_row[...] = jnp.where(even, last, first)
    next_row[...] = jnp.where(even, first, last)


def up_project(meta, own, other, gain, weights, part):
    features, hidden = weights.shape
    count = own.shape[1]
    return pl.pallas_call(
        up_kernel,
        out_shape=(
            shape_of((count, hidden)),
            shape_of((part, count), f32),
            shape_of((1, hidden)),
            shape_of((1, hidden)),
        ),
        in_specs=[SM] + [VM] * 4,
        out_specs=[VM] * 4,
        scratch_shapes=[
            pltpu.VMEM((features, count), f32),
            pltpu.VMEM((count, features), bf16),
            pltpu.VMEM((count, DK), f32),
        ],
        compiler_params=params(16),
        cost_estimate=cost(2 * 10**9, 8 * 10**6),
        name="up_project",
    )(meta, own, other, gain, weights)


def gelu_of(x):
    half = 0.5 * x
    return half + half * jnp.tanh(x * (0.7978845608028654 + 0.035677408136300125 * (x * x)))


def act_kernel(late, meta, outer, inside, near_row, next_row, taps, act_t, padded, act):
    count = act.shape[0]
    even = meta[PARITY] == 0
    if late:
        padded[7:8, :] = inside[BLOCK - 1 : BLOCK, :].astype(f32)
        padded[8 : 8 + BLOCK, :] = inside[BLOCK:, :].astype(f32)
        padded[8 + BLOCK : 8 + count, :] = outer[BLOCK:, :].astype(f32)
        padded[8 + count : 9 + count, :] = jnp.where(even, near_row[...], next_row[...]).astype(f32)
    else:
        padded[7:8, :] = jnp.where(even, next_row[...], near_row[...]).astype(f32)
        padded[8 : 8 + BLOCK, :] = outer[:BLOCK, :].astype(f32)
        padded[8 + BLOCK : 8 + count, :] = inside[:BLOCK, :].astype(f32)
        padded[8 + count : 9 + count, :] = inside[BLOCK : BLOCK + 1, :].astype(f32)

    @pl.loop(0, count // 32)
    def _(r):
        base = pl.multiple_of(r * 32, 32)
        window = padded[pl.ds(base, 48), :]
        value = (
            taps[0:1, :] * window[7:39, :]
            + taps[1:2, :] * window[8:40, :]
            + taps[2:3, :] * window[9:41, :]
        )
        act[pl.ds(base, 32), :] = gelu_of(value).astype(bf16)

    act_t[...] = act[...].T


def activate(meta, outer, inside, near_row, next_row, taps, late):
    hidden = outer.shape[1]
    count = (outer.shape[0] + inside.shape[0]) // 2
    return pl.pallas_call(
        functools.partial(act_kernel, late),
        out_shape=shape_of((hidden, count)),
        in_specs=[SM] + [VM] * 5,
        out_specs=VM,
        scratch_shapes=[pltpu.VMEM((count + 16, hidden), f32), pltpu.VMEM((count, hidden), bf16)],
        compiler_params=params(8),
        cost_estimate=cost(10**9, 2 * 10**6),
        name="activate",
    )(meta, outer, inside, near_row, next_row, taps)


def far_kernel(ys, meta, own, other, weights, other_weights, *outs):
    for i, out in enumerate(outs):
        chip = meta[CHIP + ys + i]
        block = 2 * chip + meta[CORE]
        total = dot(weights[block], own[...]) + dot(other_weights[chip], other[...])
        out[...] = total.astype(bf16)


def far_project(meta, ys, own, other, weights, other_weights):
    part = weights.shape[1]
    return pl.pallas_call(
        functools.partial(far_kernel, ys),
        out_shape=[shape_of((part, own.shape[1]))] * (ys - 1),
        in_specs=[SM] + [VM] * 4,
        out_specs=[VM] * (ys - 1),
        compiler_params=params(8),
        cost_estimate=cost(10**9, 4 * 10**6),
        name="far_project",
    )(meta, own, other, weights, other_weights)


def near_kernel(meta, own_a, other_a, own_b, other_b, middle_a, middle_b, weights, other_weights, after, base):
    size = own_a.shape[1]
    middle = (
        jnp.concatenate([middle_a[:, :BLOCK], middle_b[:, :BLOCK]], axis=1),
        jnp.concatenate([middle_b[:, BLOCK:], middle_a[:, BLOCK:]], axis=1),
    )
    for i, (own, other) in enumerate(((own_a, other_a), (own_b, other_b))):
        total = dot(weights[meta[ME]], own[...])
        total = total + dot(other_weights[meta[CHIP]], other[...])
        base[:, i * size : (i + 1) * size] = total + middle[i]


def near_project(meta, own, other, middle_a, middle_b, weights, other_weights, after):
    part = weights.shape[1]
    return pl.pallas_call(
        near_kernel,
        out_shape=shape_of((part, 2 * own[0].shape[1]), f32),
        in_specs=[SM] + [VM] * 8 + [ANY],
        out_specs=VM,
        compiler_params=params(10),
        cost_estimate=cost(2 * 10**9, 6 * 10**6),
        name="near_project",
    )(meta, own[0], other[0], own[1], other[1], middle_a, middle_b, weights, other_weights, after)


def core_swap(value, n):
    return lax.ppermute(value, "head", [(i, i ^ 1) for i in range(n)])


def y_shift(value, n, step):
    return lax.ppermute(value, "head", [(i, (i + 2 * step) % n) for i in range(n)])


def pair_swap(value, n):
    return lax.ppermute(value, "seq", [(i, i ^ 1) for i in range(n)])


def later(value, n, step, start=0):
    return lax.ppermute(value, "seq", [(i, i + 2 * step) for i in range(start, n - 2 * step)])


def shards(
    tokens,
    norm_gain,
    w_query,
    w_key,
    w_value,
    w_decay,
    w_beta,
    head_rates,
    head_gain,
    w_out,
    ffn_gain,
    w_up,
    conv_taps,
    w_down,
):
    n = lax.axis_size("head")
    seqs = lax.axis_size("seq")
    me = lax.axis_index("head")
    at = lax.axis_index("seq")
    core = me % 2
    parity = at % 2
    ys = n // 2
    count, part = tokens.shape
    heads = w_query.shape[1] // DK
    hidden = w_up.shape[1]
    features = n * part

    mine = tokens.T
    shifted = [mine] + [y_shift(mine, n, d) for d in range(1, ys)]

    def group_of(piece):
        partner = core_swap(piece, n)
        if part % 16:
            first = jnp.where(core == 0, piece, partner)
            second = jnp.where(core == 0, partner, piece)
            return [jnp.concatenate([first, second], axis=0)]
        return [piece, partner]

    groups = [group_of(mine)]
    chip = me // 2
    here = [parity, core, me]
    sources = [(chip + ys - d) % ys for d in range(ys)]
    targets = [(chip + d) % ys for d in range(1, ys)]
    meta = jnp.stack(here + sources + targets).astype(jnp.int32)

    w_out_t = w_out.T
    w_parts = w_down.T.reshape(n, part, hidden)

    gates = jnp.concatenate([w_decay.T, w_beta.T], axis=0)
    gates = jnp.pad(gates, ((0, 16 - 2 * heads), (0, 0)))
    gates = gates.reshape(16, ys, 2 * part).transpose(1, 0, 2)
    rates = jnp.pad(head_rates.reshape(2 * heads, 1), ((0, 16 - 2 * heads), (0, 0)))
    rates = jnp.broadcast_to(rates, (16, 128))
    gain = norm_gain.astype(f32).reshape(ys, 1, 2 * part)

    def ours(rows, d):
        return lax.dynamic_index_in_dim(rows, sources[d], 0, False)

    ffn_scale = ffn_gain.astype(f32).reshape(1, features)
    taps = conv_taps.astype(f32)

    gains = [ours(gain, d) for d in range(ys)]
    gate_rows = [ours(gates, d) for d in range(ys)]
    gains, gate_rows, rates, taps, ffn_scale, head_scale, meta = lax.optimization_barrier(
        (gains, gate_rows, rates, taps, ffn_scale, head_gain.reshape(1, DK), meta)
    )

    early = None
    for d in range(ys - 1):
        early = early_project(
            meta, CHIP + d, groups[d], gains[d], gate_rows[d], w_key, w_value, w_query, w_parts, w_out_t, early
        )
        if d == 0:
            sent, early = early[5:], early[:5]
        piece, _ = lax.optimization_barrier((shifted[d + 1], early[4]))
        groups.append(group_of(piece))
    scaled, scale_b, keys, erased, entry, own_maps, sent_maps, totals = block_maps(
        meta, CHIP + ys - 1, groups[-1], gains[-1], rates, gate_rows[-1], w_key, w_value, early
    )

    sent, _ = lax.optimization_barrier((sent, groups[-1][-1]))
    sent_w_down, their_rows, my_rows = sent
    other_w_down = core_swap(sent_w_down, n)
    fetched = [y_shift(my_rows, n, d) for d in range(1, ys)]
    diagonal = [
        lax.ppermute(their_rows, "head", [(i, ((i + 2 * d) % n) ^ 1) for i in range(n)])
        for d in range(1, ys)
    ]
    partner_w_out = core_swap(their_rows, n)
    other_maps = pair_swap(sent_maps, seqs)
    pair_map, pair_shift, first, done = pair_maps(meta, own_maps, other_maps)
    fetched, _ = lax.optimization_barrier((fetched, done))
    swapped = [pair_swap(value, seqs) for value in fetched]
    shifts = [later(pair_shift, seqs, d) for d in range(seqs // 2 - 1, 0, -1)]
    maps = [later(pair_map, seqs, d, 2) for d in range(seqs // 2 - 2, 0, -1)]
    acc_query, partner_w_out, other_w_down, _ = lax.optimization_barrier(
        (early[2], partner_w_out, other_w_down, done)
    )
    query, tokens_a, tokens_b, _ = queries(
        meta, ys, scaled, scale_b, w_query, acc_query, sum(groups, [])
    )
    shard_query, free, out_done = block_outputs(query, keys, erased, entry, totals, done)
    kept_state, given_state = start_states(meta, first, maps, shifts, out_done)
    other_state = pair_swap(given_state, seqs)

    mixed = mixed_heads(meta, kept_state, other_state, shard_query, free, head_scale)
    far_mixed = [[y_shift(value, n, d) for d in range(1, ys)] for value in mixed]


    def middle_of(i, far):
        heads_far = [[value, core_swap(value, n)] for value in far]
        operands = []
        for pair_of, *weights in zip(heads_far, fetched, swapped, diagonal):
            operands += pair_of + weights
        own_tokens = (tokens_a, tokens_b)[i]
        return attend(
            meta, ys, own_tokens, mixed[i], core_swap(mixed[i], n), w_out_t, partner_w_out, operands
        )

    middle = middle_of(0, far_mixed[0])
    outer, middle_a, near_row, next_row = up_project(
        meta, middle, core_swap(middle, n), ffn_scale, w_up, part
    )
    near_row = lax.ppermute(near_row, "seq", [(i, i ^ 1) for i in range(seqs)])
    next_row = lax.ppermute(
        next_row, "seq", [(i, ((i + 1) ^ 1) - 1) for i in range(1, seqs - 1)]
    )
    middle = middle_of(1, far_mixed[1])
    inside, middle_b, _, _ = up_project(
        meta, middle, core_swap(middle, n), ffn_scale, w_up, part
    )

    acts = [activate(meta, outer, inside, near_row, next_row, taps, late) for late in (False, True)]
    partner_acts = [core_swap(act, n) for act in acts]
    fars = [
        far_project(meta, ys, act, partner, w_parts, other_w_down)
        for act, partner in zip(acts, partner_acts)
    ]
    total = near_project(
        meta, acts, partner_acts, middle_a, middle_b, w_parts, other_w_down, fars[1][0]
    )
    for d in range(1, ys):
        halves = [y_shift(far[d - 1], n, d) for far in fars]
        total = total + jnp.concatenate(halves, axis=1).astype(f32)
    return total.astype(bf16).T


def solution(mesh):
    placed = (
        P("seq", "head"),
        P(),
        P(None, "head"),
        P(None, "head"),
        P(None, "head"),
        P(None, "head"),
        P(None, "head"),
        P(None, "head"),
        P(),
        P("head", None),
        P(),
        P(None, "head"),
        P(None, "head"),
        P("head", None),
    )
    return jax.shard_map(
        shards, mesh=mesh, in_specs=placed, out_specs=P("seq", "head"), check_vma=False
    )
```
